32 devices in a mesh: groups: 2 (over x), modes: 16 (over z, y, core).
Axes of the slice: x: 2, y: 2, z: 4, core: 2. Of those that a mesh axis runs over, the one named last changes fastest.
Arguments:
- rhs: float32 [64, 8, 8192], P(('groups', 'modes')), parts along dimension 0, may hold values from -6 to 6
- diffusivity: float32 [8], replicated, may hold values from 0.05 to 0.5
- jac_coef: float32 [9, 8, 8, 8192], P(None, None, None, 'modes'), may hold values from -0.3 to 0.3
- coef_index: int32 [512], replicated, may hold values from 0 to 8
- row_mode: int32 [512], replicated, may hold values from 0 to 31
- col_mode: int32 [512], replicated, may hold values from 0 to 31
- multiplicity: int32 [512], replicated, may hold values from 1 to 4
Outputs:
- update: float32 [64, 8, 8192], P(('groups', 'modes')), parts along dimension 0
- basis_next: float32 [64, 8, 8192], P(('groups', 'modes')), parts along dimension 0
The draws below stay inside these ranges and needn't reach their ends.
There are 2 independent parts, one for each index of `groups`. The reference program is written for one: setup_inputs(seed, part) draws one part's arguments, and reference() takes and returns one part's arrays. A program takes and returns all parts, laid end to end along the dimension named above; an argument that names none is the same for every part. Nothing has to cross between parts.
All inputs are finite; a program needn't handle non-finite values.
Results may differ from the reference program's by a relative error of at most 0.00029.
Values sent between devices are 32-bit elements; how exact they have to be, the bound alone decides.
No kernel may reach another device: no remote copies, remote signals or barrier semaphores. Data moves between devices by JAX's collectives and lax.ppermute only.
A program may use at most 128 MiB of HBM per device.

```python
import math
import jax
import jax.numpy as jnp
from jax import lax

S = 8
NCOEF = 9
GX = 256
GY = 32
MODES = 32
CELLS = 8192
TRIPLES = 512


def place_ends(values, stream_key, smallest, high):
    extent = values.shape
    index_at = [jax.random.randint(jax.random.fold_in(stream_key, axis), (), 0, extent[axis]) for axis in range(len(extent))]
    values = values.at[tuple(index_at)].set(smallest)
    longest = extent.index(max(extent))
    index_at[longest] = (index_at[longest] + 1) % extent[longest]
    return values.at[tuple(index_at)].set(high)


def block_scale(rng, dims, split, smallest, high):
    factor_of, own = 1.0, jax.random.fold_in(rng, 6)
    for position, shards_of in split:
        heights = jnp.exp(jax.random.uniform(jax.random.fold_in(own, position), (shards_of,), jnp.float32, smallest / len(split), high / len(split)))
        factor_of = factor_of * jnp.repeat(heights, dims[position] // shards_of).reshape([-1 if axis == position else 1 for axis in range(len(dims))])
    return factor_of


def centred(rng, extent, scale, bound, split=(), kind=jnp.bfloat16):
    array = jax.random.normal(rng, extent, jnp.float32) * scale
    if len(split) > 0:
        array = block_scale(rng, extent, split, -0.22, 0.18) * array
    return jnp.clip(array, min=-bound, max=bound).astype(kind)


def setup_inputs(seed: int = 0, part: int = 0) -> dict:
    key_list = jax.random.split(jax.random.key(seed), 8)
    own_keys = jax.random.split(jax.random.fold_in(key_list[7], part), 8)
    return {
        "rhs": centred(own_keys[0], (MODES, S, CELLS), 1.0, 6.0, ((0, 16),), jnp.float32),
        "diffusivity": jnp.clip(jnp.exp(jax.random.uniform(key_list[1], (S,), jnp.float32, math.log(0.05), math.log(0.5))), 0.05, 0.5),
        "jac_coef": centred(key_list[2], (NCOEF, S, S, CELLS), 0.05, 0.3, ((3, 16),), jnp.float32),
        "coef_index": place_ends(jax.random.randint(key_list[3], (TRIPLES,), 0, NCOEF), jax.random.fold_in(key_list[3], 1), 0, NCOEF - 1).astype(jnp.int32),
        "row_mode": place_ends(jax.random.randint(key_list[4], (TRIPLES,), 0, MODES), jax.random.fold_in(key_list[4], 1), 0, MODES - 1).astype(jnp.int32),
        "col_mode": place_ends(jax.random.randint(key_list[5], (TRIPLES,), 0, MODES), jax.random.fold_in(key_list[5], 1), 0, MODES - 1).astype(jnp.int32),
        "multiplicity": place_ends(jax.random.randint(key_list[6], (TRIPLES,), 1, 5), jax.random.fold_in(key_list[6], 1), 1, 4).astype(jnp.int32),
    }


def build_coupling(coef_index, row_mode, col_mode, multiplicity):
    flat = (coef_index * MODES + row_mode) * MODES + col_mode
    weights = 0.25 * multiplicity.astype(jnp.float32)
    dense = jax.ops.segment_sum(weights, flat, num_segments=NCOEF * MODES * MODES)
    dense = dense.reshape(NCOEF, MODES, MODES)
    return dense.at[0].add(jnp.eye(MODES, dtype=jnp.float32))

def diffuse(field, diffusivity):
    grid = field.reshape(field.shape[0], S, GX, GY)
    beside = jnp.roll(grid, 1, 2) + jnp.roll(grid, -1, 2) + jnp.roll(grid, 1, 3) + jnp.roll(grid, -1, 3)
    out = grid + diffusivity[None, :, None, None] * (4.0 * grid - beside)
    return out.reshape(field.shape)

def react(field, coupling, jac_coef):
    mixed = jnp.einsum('ikj,jsc->iksc', coupling, field, precision=lax.Precision.HIGHEST)
    return jnp.einsum('istc,iktc->ksc', jac_coef, mixed, precision=lax.Precision.HIGHEST)

def reference(rhs, diffusivity, jac_coef, coef_index, row_mode, col_mode, multiplicity):
    coupling = build_coupling(coef_index, row_mode, col_mode, multiplicity)

    def apply(field):
        return diffuse(field, diffusivity) - react(field, coupling, jac_coef)
    beta = jnp.sqrt(jnp.sum(rhs * rhs))
    first = rhs / beta
    work = apply(first)
    h11 = jnp.sum(first * work)
    work = work - h11 * first
    h21 = jnp.sqrt(jnp.sum(work * work))
    second = work / h21
    image = apply(second)
    h12 = jnp.sum(first * image)
    h22 = jnp.sum(second * image)
    third = image - h12 * first - h22 * second
    h32 = jnp.sqrt(jnp.sum(third * third))
    basis_next = third / h32
    m11 = h11 * h11 + h21 * h21
    m12 = h11 * h12 + h21 * h22
    m22 = h12 * h12 + h22 * h22 + h32 * h32
    g1 = beta * h11
    g2 = beta * h12
    determ = m11 * m22 - m12 * m12
    coef_one = (m22 * g1 - m12 * g2) / determ
    coef_two = (m11 * g2 - m12 * g1) / determ
    update = coef_one * first + coef_two * second
    return (update, basis_next)
```

```python
import functools

import jax
import jax.numpy as jnp
from jax import lax
from jax.experimental import pallas as pl
from jax.experimental.pallas import tpu as pltpu
from jax.sharding import PartitionSpec as P

NCOEF = 9
GY = 32
S = 8
LANES = 128
F32 = jnp.float32
BF16 = jnp.bfloat16
VMEM = pl.BlockSpec(memory_space=pltpu.VMEM)
PARAMS = pltpu.CompilerParams(vmem_limit_bytes=40 * 1024 * 1024)


def lane_iota():
    return lax.broadcasted_iota(jnp.int32, (S, LANES), 1)


def arrange_kernel(parts, rhs_ref, out_ref):
    own, _, total = rhs_ref.shape
    cells = total // parts
    tiles = cells // LANES
    low = lane_iota() < LANES // 2
    for d in range(parts):
        after = ((d + 1) * cells) % total
        before = (d * cells - LANES) % total
        for m in range(own):
            for ct in range(tiles):
                at = d * cells + ct * LANES
                out_ref[d * own + m, ct] = rhs_ref[m, :, at : at + LANES]
            out_ref[d * own + m, tiles] = jnp.where(
                low, rhs_ref[m, :, after : after + LANES], rhs_ref[m, :, before : before + LANES]
            )


def pack_kernel(first_ref, last_ref, head_ref, tail_ref):
    piece = lane_iota() // GY
    for i in range(NCOEF):
        for q in range(S // 4):
            head = first_ref[i, q * 4]
            tail = pltpu.roll(last_ref[i, q * 4], GY, 1)
            for p in range(1, 4):
                head = jnp.where(piece == p, pltpu.roll(first_ref[i, q * 4 + p], GY * p, 1), head)
                moved = last_ref[i, q * 4 + p]
                if p < 3:
                    moved = pltpu.roll(moved, GY * (p + 1), 1)
                tail = jnp.where(piece == p, moved, tail)
            head_ref[i, q] = head
            tail_ref[i, q] = tail


def coupling_kernel(modes, coef_ref, row_ref, col_ref, mult_ref, out_ref):
    rows, cols = out_ref.shape
    triples = coef_ref.shape[1]
    key = coef_ref[...] * modes + row_ref[...]
    weight = 0.25 * mult_ref[...].astype(F32)
    row = lax.broadcasted_iota(jnp.int32, (rows, triples), 0)
    left = jnp.where(row == key, weight, 0.0).astype(BF16)
    col = lax.rem(lax.broadcasted_iota(jnp.int32, (cols, triples), 0), modes)
    right = jnp.where(col == col_ref[...], 1.0, 0.0).astype(BF16)
    dense = lax.dot_general(left, right, (((1,), (1,)), ((), ())), preferred_element_type=F32)
    r = lax.broadcasted_iota(jnp.int32, (rows, cols), 0)
    c = lax.broadcasted_iota(jnp.int32, (rows, cols), 1)
    dense = dense + jnp.where(r == lax.rem(c, modes), 1.0, 0.0)
    high = dense.astype(BF16)
    low = (dense - high.astype(F32)).astype(BF16)
    out_ref[...] = jnp.where(c < 2 * modes, high.astype(F32), low.astype(F32)).astype(BF16)


def main_kernel(
    n, tiles, dif_ref, r_ref, jac_ref, next_ref, prev_ref, coup_ref, out_ref, v_ref, w_ref, z_ref, jh_ref, vs_ref, mx_ref
):
    lane = lane_iota()
    col = lane % GY
    every = tiles + 1

    for ct in range(every):
        for s in range(S):
            v_ref[ct, s] = r_ref[pl.ds(ct * S + s, n, stride=every * S), :]

    def unpack(i, _):
        for q in range(S // 4):
            after, before = next_ref[i, q], prev_ref[i, q]
            for p in range(4):
                a = after if p == 0 else pltpu.roll(after, LANES - GY * p, 1)
                b = before if p == 3 else pltpu.roll(before, LANES - GY - GY * p, 1)
                jh_ref[i * S + q * 4 + p] = jnp.where(lane < LANES // 2, a, b)
        return 0

    lax.fori_loop(0, NCOEF, unpack, 0)

    def apply_tile(src, dst, jac, ct):
        for t in range(S):
            x = src[ct, t]
            high = x.astype(BF16)
            low = (x - high.astype(F32)).astype(BF16)
            at = slice(t * LANES, (t + 1) * LANES)
            vs_ref[0:n, at] = high
            vs_ref[n : 2 * n, at] = low
            vs_ref[2 * n : 3 * n, at] = high
        mx_ref[...] = jnp.dot(coup_ref[...], vs_ref[...], preferred_element_type=F32)
        before, after = lax.rem(ct + every - 1, every), lax.rem(ct + 1, every)
        for kb in range(0, n, 32):

            def body(i, acc):
                acc = list(acc)
                for t in range(S):
                    m = [
                        mx_ref[pl.ds(pl.multiple_of(i * n + kb + kt * 8, 8), 8), t * LANES : (t + 1) * LANES]
                        for kt in range(4)
                    ]
                    for s in range(S):
                        j = jnp.broadcast_to(jac(i * S + s, t), (8, LANES))
                        for kt in range(4):
                            acc[s * 4 + kt] = acc[s * 4 + kt] + j * m[kt]
                return tuple(acc)

            acc = lax.fori_loop(0, NCOEF, body, tuple(jnp.zeros((8, LANES), F32) for _ in range(32)))
            for s in range(S):
                for kt in range(4):
                    at = slice(kb + kt * 8, kb + kt * 8 + 8)
                    x = src[ct, s, at]
                    up, down = pltpu.roll(x, GY, 1), pltpu.roll(x, LANES - GY, 1)
                    beside = pltpu.roll(jnp.where(col == GY - 1, down, x), 1, 1)
                    beside += pltpu.roll(jnp.where(col == 0, up, x), LANES - 1, 1)
                    beside += jnp.where(lane < GY, pltpu.roll(src[before, s, at], GY, 1), up)
                    beside += jnp.where(lane >= LANES - GY, pltpu.roll(src[after, s, at], LANES - GY, 1), down)
                    dst[ct, s, at] = dif_ref[s] * (4.0 * x - beside) - acc[s * 4 + kt]

    def own_jac(ct):
        start = pl.multiple_of(ct * LANES, LANES)
        return lambda row, t: jac_ref[row, t : t + 1, pl.ds(start, LANES)]

    def first(ct, _):
        apply_tile(v_ref, w_ref, own_jac(ct), ct)
        return 0

    lax.fori_loop(0, tiles, first, 0)
    apply_tile(v_ref, w_ref, lambda row, t: jh_ref[row, t : t + 1, :], jnp.int32(tiles))

    def second(ct, _):
        apply_tile(w_ref, z_ref, own_jac(ct), ct)
        return 0

    lax.fori_loop(0, tiles, second, 0)

    def total(x):
        return jnp.sum(x)

    rr = rw = rz = jnp.zeros((n, LANES), F32)
    for ct in range(tiles):
        for s in range(S):
            v, w, z = v_ref[ct, s], w_ref[ct, s], z_ref[ct, s]
            rr, rw, rz = rr + v * v, rw + v * w, rz + v * z

    def ratio(a, b):
        return jnp.where(b > 0.0, a / jnp.where(b > 0.0, b, 1.0), 0.0)

    def full(x):
        return jnp.full((8, LANES), x, F32)

    rr, rw, rz = full(total(rr)), full(total(rw)), full(total(rz))
    c1, c2 = ratio(rw, rr), ratio(rz, rr)
    c1n, c2n = c1[:1], c2[:1]
    uu = ut = jnp.zeros((n, LANES), F32)
    per = 2 * tiles + 1
    for ct in range(tiles):
        for s in range(S):
            v, w, z = v_ref[ct, s], w_ref[ct, s], z_ref[ct, s]
            out_ref[pl.ds(ct * S + s, n, stride=per * S), :] = w
            out_ref[pl.ds((tiles + ct) * S + s, n, stride=per * S), :] = z
            u, t = w - c1n * v, z - c2n * v
            uu, ut = uu + u * u, ut + u * t
    uu, ut = full(total(uu)), full(total(ut))
    c3 = ratio(ut, uu)
    c3n = c3[:1]
    xx = jnp.zeros((n, LANES), F32)
    for ct in range(tiles):
        for s in range(S):
            v, w, z = v_ref[ct, s], w_ref[ct, s], z_ref[ct, s]
            x = (z - c2n * v) - c3n * (w - c1n * v)
            xx = xx + x * x
    xx = full(total(xx))
    stat = lax.broadcasted_iota(jnp.int32, (8, LANES), 0)
    tile = jnp.zeros((8, LANES), F32)
    for q, value in enumerate((rr, c1, uu, c2, c3, xx)):
        tile = jnp.where(stat == q, value, tile)
    for k in range(n):
        out_ref[(k * per + 2 * tiles) * S : (k * per + per) * S, :] = tile


def combine_kernel(parts, tiles, rhs_ref, got_ref, update_ref, basis_ref):
    own = rhs_ref.shape[0]
    per = 2 * tiles + 1

    def stat(q):
        return got_ref[pl.ds(2 * tiles * S + q, parts, stride=own * per * S), :]

    def add(x):
        return jnp.sum(x, axis=0, keepdims=True)

    rr, c1, uu, c2, c3, xx = (stat(q) for q in range(6))
    all_rr = add(rr)
    g1 = add(rr * c1) / all_rr
    g2 = add(rr * c2) / all_rr
    e1, e2 = c1 - g1, c2 - g2
    all_uu = add(uu + e1 * e1 * rr)
    g3 = add(c3 * uu + e1 * e2 * rr) / all_uu
    e3 = c3 - g3
    f = e2 - g3 * e1
    all_xx = add(xx + e3 * e3 * uu + f * f * rr)
    beta, nu, nx = jnp.sqrt(all_rr), jnp.sqrt(all_uu), jnp.sqrt(all_xx)
    h11 = 1.0 + g1
    h21 = nu / beta
    h12 = (g2 - g1 * g1) * beta / nu
    h22 = 1.0 + (g3 - g1)
    h32 = nx / nu
    m11 = h11 * h11 + h21 * h21
    m12 = h11 * h12 + h21 * h22
    m22 = h12 * h12 + h22 * h22 + h32 * h32
    b1, b2 = beta * h11, beta * h12
    determ = m11 * m22 - m12 * m12
    y1 = (m22 * b1 - m12 * b2) / determ
    y2 = (m11 * b2 - m12 * b1) / determ
    uw = y2 / nu
    ur = y1 / beta - uw * g1
    bz = 1.0 / nx
    bw = -g3 * bz
    br = (g3 * g1 - g2) * bz
    ur, uw, br, bw, bz = (jnp.broadcast_to(x, (S, LANES)) for x in (ur, uw, br, bw, bz))
    for d in range(parts):
        for m in range(own):
            for ct in range(tiles):
                at = slice((d * tiles + ct) * LANES, (d * tiles + ct + 1) * LANES)
                base = ((d * own + m) * per + ct) * S
                r = rhs_ref[m, :, at]
                w = got_ref[base : base + S, :]
                z = got_ref[base + tiles * S : base + tiles * S + S, :]
                update_ref[m, :, at] = ur * r + uw * w
                basis_ref[m, :, at] = br * r + bw * w + bz * z


def local(rhs, diffusivity, jac_coef, coef_index, row_mode, col_mode, multiplicity):
    parts = lax.axis_size("modes")
    own, _, total = rhs.shape
    n = own * parts
    cells = total // parts
    tiles = cells // LANES
    sds = jax.ShapeDtypeStruct

    send = pl.pallas_call(
        functools.partial(arrange_kernel, parts),
        out_shape=sds((n, tiles + 1, S, LANES), F32),
        in_specs=[VMEM],
        out_specs=VMEM,
        compiler_params=PARAMS,
        name="arrange",
    )(rhs)
    vector = lax.all_to_all(send, "modes", split_axis=0, concat_axis=0, tiled=True)

    edge = (NCOEF, S, S, LANES)
    head, tail = pl.pallas_call(
        pack_kernel,
        grid=(1,),
        out_shape=[sds((NCOEF, S // 4, S, LANES), F32)] * 2,
        in_specs=[
            pl.BlockSpec(edge, lambda g: (0, 0, 0, 0)),
            pl.BlockSpec(edge, lambda g: (0, 0, 0, tiles - 1)),
        ],
        compiler_params=PARAMS,
        name="pack",
    )(jac_coef, jac_coef)
    up = [(i, (i + 1) % parts) for i in range(parts)]
    down = [(j, i) for i, j in up]
    after = lax.ppermute(head, "modes", down)
    before = lax.ppermute(tail, "modes", up)

    coupling = pl.pallas_call(
        functools.partial(coupling_kernel, n),
        out_shape=sds((NCOEF * n, 3 * n), BF16),
        in_specs=[VMEM] * 4,
        out_specs=VMEM,
        compiler_params=PARAMS,
        name="coupling",
    )(*(x.reshape(1, -1) for x in (coef_index, row_mode, col_mode, multiplicity)))

    per = 2 * tiles + 1
    field = pltpu.VMEM((tiles + 1, S, n, LANES), F32)
    out = pl.pallas_call(
        functools.partial(main_kernel, n, tiles),
        out_shape=sds((n * per * S, LANES), F32),
        in_specs=[pl.BlockSpec(memory_space=pltpu.SMEM)] + [VMEM] * 5,
        out_specs=VMEM,
        scratch_shapes=[
            field,
            field,
            field,
            pltpu.VMEM((NCOEF * S, S, LANES), F32),
            pltpu.VMEM((3 * n, S * LANES), BF16),
            pltpu.VMEM((NCOEF * n, S * LANES), F32),
        ],
        compiler_params=PARAMS,
        name="krylov",
    )(
        diffusivity,
        vector.reshape(n * (tiles + 1) * S, LANES),
        jac_coef.reshape(NCOEF * S, S, cells),
        after,
        before,
        coupling,
    )
    got = lax.all_to_all(out.reshape(n, per, S, LANES), "modes", split_axis=0, concat_axis=0, tiled=True)
    update, basis_next = pl.pallas_call(
        functools.partial(combine_kernel, parts, tiles),
        out_shape=[sds(rhs.shape, F32)] * 2,
        in_specs=[VMEM] * 2,
        out_specs=[VMEM] * 2,
        compiler_params=PARAMS,
        name="combine",
    )(rhs, got.reshape(n * per * S, LANES))
    return (update, basis_next)


def solution(mesh):
    return jax.shard_map(
        local,
        mesh=mesh,
        in_specs=(
            P(("groups", "modes"), None, None),
            P(),
            P(None, None, None, "modes"),
            P(),
            P(),
            P(),
            P(),
        ),
        out_specs=(P(("groups", "modes"), None, None), P(("groups", "modes"), None, None)),
        check_vma=False,
    )
```

```python
import functools

import jax
import jax.numpy as jnp
from jax import lax
from jax.experimental import pallas as pl
from jax.experimental.pallas import tpu as pltpu
from jax.sharding import PartitionSpec as P

NCOEF = 9
GY = 32
S = 8
LANES = 128
F32 = jnp.float32
BF16 = jnp.bfloat16
VMEM = pl.BlockSpec(memory_space=pltpu.VMEM)
PARAMS = pltpu.CompilerParams(vmem_limit_bytes=40 * 1024 * 1024)


def lane_iota():
    return lax.broadcasted_iota(jnp.int32, (S, LANES), 1)


def arrange_kernel(parts, rhs_ref, out_ref):
    own, _, total = rhs_ref.shape
    cells = total // parts
    tiles = cells // LANES
    low = lane_iota() < LANES // 2
    for d in range(parts):
        after = ((d + 1) * cells) % total
        before = (d * cells - LANES) % total
        for m in range(own):
            for ct in range(tiles):
                at = d * cells + ct * LANES
                out_ref[d * own + m, ct] = rhs_ref[m, :, at : at + LANES]
            out_ref[d * own + m, tiles] = jnp.where(
                low, rhs_ref[m, :, after : after + LANES], rhs_ref[m, :, before : before + LANES]
            )


def pack_kernel(first_ref, last_ref, head_ref, tail_ref):
    piece = lane_iota() // GY
    for i in range(NCOEF):
        for q in range(S // 4):
            head = first_ref[i, q * 4]
            tail = pltpu.roll(last_ref[i, q * 4], GY, 1)
            for p in range(1, 4):
                head = jnp.where(piece == p, pltpu.roll(first_ref[i, q * 4 + p], GY * p, 1), head)
                moved = last_ref[i, q * 4 + p]
                if p < 3:
                    moved = pltpu.roll(moved, GY * (p + 1), 1)
                tail = jnp.where(piece == p, moved, tail)
            head_ref[i, q] = head
            tail_ref[i, q] = tail


def coupling_kernel(modes, coef_ref, row_ref, col_ref, mult_ref, out_ref, stencil_ref):
    rows, cols = out_ref.shape
    triples = coef_ref.shape[1]
    key = coef_ref[...] * modes + row_ref[...]
    weight = 0.25 * mult_ref[...].astype(F32)
    row = lax.broadcasted_iota(jnp.int32, (rows, triples), 0)
    left = jnp.where(row == key, weight, 0.0).astype(BF16)
    col = lax.rem(lax.broadcasted_iota(jnp.int32, (cols, triples), 0), modes)
    right = jnp.where(col == col_ref[...], 1.0, 0.0).astype(BF16)
    dense = lax.dot_general(left, right, (((1,), (1,)), ((), ())), preferred_element_type=F32)
    r = lax.broadcasted_iota(jnp.int32, (rows, cols), 0)
    c = lax.broadcasted_iota(jnp.int32, (rows, cols), 1)
    dense = dense + jnp.where(r == lax.rem(c, modes), 1.0, 0.0)
    high = dense.astype(BF16)
    low = (dense - high.astype(F32)).astype(BF16)
    out_ref[...] = jnp.where(c < 2 * modes, high.astype(F32), low.astype(F32)).astype(BF16)

    a = lax.broadcasted_iota(jnp.int32, (LANES, LANES), 0)
    b = lax.broadcasted_iota(jnp.int32, (LANES, LANES), 1)
    step = jnp.bitwise_and(a - b, GY - 1)
    same = (a // GY == b // GY) & ((step == 1) | (step == GY - 1))
    apart = jnp.abs(a - b)
    inner = jnp.where(apart == 0, 4.0, jnp.where(same | (apart == GY), -1.0, 0.0)).astype(BF16)
    outer = jnp.where(apart == LANES - GY, -1.0, 0.0).astype(BF16)
    stencil_ref[0:LANES] = inner
    stencil_ref[LANES : 2 * LANES] = inner
    stencil_ref[2 * LANES : 3 * LANES] = outer
    stencil_ref[3 * LANES :] = outer


def split(x):
    high = x.astype(BF16)
    return high, (x - high.astype(F32)).astype(BF16)


def ratio(a, b):
    return jnp.where(b > 0.0, a / jnp.where(b > 0.0, b, 1.0), 0.0)


def main_kernel(
    n,
    tiles,
    dif_ref,
    r_ref,
    jac_ref,
    next_ref,
    prev_ref,
    coup_ref,
    stencil_ref,
    out_ref,
    v_ref,
    w_ref,
    z_ref,
    jh_ref,
    vs_ref,
    xs_ref,
    mx_ref,
    bs_ref,
):
    lane = lane_iota()
    every = tiles + 1
    per = 2 * tiles + 1

    for ct in range(every):
        for s in range(S):
            v_ref[ct, s] = r_ref[pl.ds(ct * S + s, n, stride=every * S), :]

    def unpack(i, _):
        for q in range(S // 4):
            after, before = next_ref[i, q], prev_ref[i, q]
            for p in range(4):
                a = after if p == 0 else pltpu.roll(after, LANES - GY * p, 1)
                b = before if p == 3 else pltpu.roll(before, LANES - GY - GY * p, 1)
                jh_ref[i * S + q * 4 + p] = jnp.where(lane < LANES // 2, a, b)
        return 0

    lax.fori_loop(0, NCOEF, unpack, 0)

    def mix(src, ct, slot):
        wide = lax.broadcasted_iota(jnp.int32, (n, LANES), 1) < LANES // 2
        before, after = (ct - 1) % every, (ct + 1) % every
        for t in range(S):
            at = slice(t * LANES, (t + 1) * LANES)
            to = slice(t * n, (t + 1) * n)
            high, low = split(src[ct, t])
            vs_ref[slot, 0:n, at] = high
            vs_ref[slot, n : 2 * n, at] = low
            vs_ref[slot, 2 * n : 3 * n, at] = high
            xs_ref[slot, to, 0:LANES] = high
            xs_ref[slot, to, LANES : 2 * LANES] = low
            high, low = split(jnp.where(wide, src[after, t], src[before, t]))
            xs_ref[slot, to, 2 * LANES : 3 * LANES] = high
            xs_ref[slot, to, 3 * LANES :] = low
        mx_ref[slot] = jnp.dot(coup_ref[...], vs_ref[slot], preferred_element_type=F32)
        bs_ref[slot] = jnp.dot(xs_ref[slot], stencil_ref[...], preferred_element_type=F32)

    def react(ct, slot, finish):
        for kb in range(0, n, 32):
            acc = [None] * 32
            for i in range(NCOEF):
                for t in range(S):
                    m = [
                        mx_ref[slot, i * n + kb + kt * 8 : i * n + kb + kt * 8 + 8, t * LANES : (t + 1) * LANES]
                        for kt in range(4)
                    ]
                    for s in range(S):
                        if ct < tiles:
                            j = jac_ref[i * S + s, t : t + 1, ct * LANES : (ct + 1) * LANES]
                        else:
                            j = jh_ref[i * S + s, t : t + 1, :]
                        j = jnp.broadcast_to(j, (8, LANES))
                        for kt in range(4):
                            term = j * m[kt]
                            at = s * 4 + kt
                            acc[at] = term if acc[at] is None else acc[at] + term
            for s in range(S):
                for kt in range(4):
                    k = kb + kt * 8
                    b = bs_ref[slot, s * n + k : s * n + k + 8]
                    finish(s, k, dif_ref[s] * b - acc[s * 4 + kt])

    def total(x):
        return jnp.broadcast_to(jnp.sum(x, axis=(0, 1), keepdims=True), (8, LANES))

    sums = {}

    def gather(name, at, term):
        key = (name, at % 4)
        sums[key] = sums[key] + term if key in sums else term

    def collect(name):
        parts = [value for (key, _), value in sums.items() if key == name]
        return total(functools.reduce(lambda a, b: a + b, parts))

    def finish_first(ct):
        def finish(s, k, w):
            w_ref[ct, s, k : k + 8] = w
            if ct < tiles:
                v = v_ref[ct, s, k : k + 8]
                out_ref[pl.ds(k * per * S + ct * S + s, 8, stride=per * S), :] = w
                gather("rr", k // 8, v * v)
                gather("rw", k // 8, v * w)

        return finish

    def finish_second(ct, c1):
        def finish(s, k, z):
            v, w = v_ref[ct, s, k : k + 8], w_ref[ct, s, k : k + 8]
            z_ref[ct, s, k : k + 8] = z
            out_ref[pl.ds(k * per * S + (tiles + ct) * S + s, 8, stride=per * S), :] = z
            u = w - c1 * v
            gather("uu", k // 8, u * u)
            gather("ur", k // 8, u * v)
            gather("uz", k // 8, u * z)
            gather("rz", k // 8, v * z)

        return finish

    order = [tiles] + list(range(tiles))
    mix(v_ref, order[0], 0)
    for at, ct in enumerate(order):
        if at + 1 < every:
            mix(v_ref, order[at + 1], (at + 1) % 2)
        elif tiles > 1:
            mix(w_ref, 0, every % 2)
        react(ct, at % 2, finish_first(ct))
    if tiles == 1:
        mix(w_ref, 0, every % 2)
    rr, rw = collect("rr"), collect("rw")
    c1 = ratio(rw, rr)
    for ct in range(tiles):
        if ct + 1 < tiles:
            mix(w_ref, ct + 1, (every + ct + 1) % 2)
        react(ct, (every + ct) % 2, finish_second(ct, c1))
    uu, ur, uz, rz = (collect(name) for name in ("uu", "ur", "uz", "rz"))
    c2 = ratio(rz, rr)
    c3 = ratio(uz - c2 * ur, uu)
    for ct in range(tiles):
        for s in range(S):
            for k in range(0, n, 8):
                v, w, z = (ref[ct, s, k : k + 8] for ref in (v_ref, w_ref, z_ref))
                x = (z - c2 * v) - c3 * (w - c1 * v)
                gather("xx", k // 8, x * x)
    xx = collect("xx")
    stat = lax.broadcasted_iota(jnp.int32, (8, LANES), 0)
    tile = jnp.zeros((8, LANES), F32)
    for q, value in enumerate((rr, c1, uu, c2, c3, xx)):
        tile = jnp.where(stat == q, value, tile)
    for k in range(n):
        out_ref[(k * per + 2 * tiles) * S : (k * per + per) * S, :] = tile


def combine_kernel(parts, tiles, rhs_ref, got_ref, update_ref, basis_ref):
    own = rhs_ref.shape[0]
    per = 2 * tiles + 1

    def stat(q):
        return got_ref[pl.ds(2 * tiles * S + q, parts, stride=own * per * S), :]

    def add(x):
        return jnp.sum(x, axis=0, keepdims=True)

    rr, c1, uu, c2, c3, xx = (stat(q) for q in range(6))
    all_rr = add(rr)
    g1 = add(rr * c1) / all_rr
    g2 = add(rr * c2) / all_rr
    e1, e2 = c1 - g1, c2 - g2
    all_uu = add(uu + e1 * e1 * rr)
    g3 = add(c3 * uu + e1 * e2 * rr) / all_uu
    e3 = c3 - g3
    f = e2 - g3 * e1
    all_xx = add(xx + e3 * e3 * uu + f * f * rr)
    beta, nu, nx = jnp.sqrt(all_rr), jnp.sqrt(all_uu), jnp.sqrt(all_xx)
    h11 = 1.0 + g1
    h21 = nu / beta
    h12 = (g2 - g1 * g1) * beta / nu
    h22 = 1.0 + (g3 - g1)
    h32 = nx / nu
    m11 = h11 * h11 + h21 * h21
    m12 = h11 * h12 + h21 * h22
    m22 = h12 * h12 + h22 * h22 + h32 * h32
    b1, b2 = beta * h11, beta * h12
    determ = m11 * m22 - m12 * m12
    y1 = (m22 * b1 - m12 * b2) / determ
    y2 = (m11 * b2 - m12 * b1) / determ
    uw = y2 / nu
    ur = y1 / beta - uw * g1
    bz = 1.0 / nx
    bw = -g3 * bz
    br = (g3 * g1 - g2) * bz
    ur, uw, br, bw, bz = (jnp.broadcast_to(x, (S, LANES)) for x in (ur, uw, br, bw, bz))
    for d in range(parts):
        for m in range(own):
            for ct in range(tiles):
                at = slice((d * tiles + ct) * LANES, (d * tiles + ct + 1) * LANES)
                base = ((d * own + m) * per + ct) * S
                r = rhs_ref[m, :, at]
                w = got_ref[base : base + S, :]
                z = got_ref[base + tiles * S : base + tiles * S + S, :]
                update_ref[m, :, at] = ur * r + uw * w
                basis_ref[m, :, at] = br * r + bw * w + bz * z


def local(rhs, diffusivity, jac_coef, coef_index, row_mode, col_mode, multiplicity):
    parts = lax.axis_size("modes")
    own, _, total = rhs.shape
    n = own * parts
    cells = total // parts
    tiles = cells // LANES
    sds = jax.ShapeDtypeStruct

    send = pl.pallas_call(
        functools.partial(arrange_kernel, parts),
        out_shape=sds((n, tiles + 1, S, LANES), F32),
        in_specs=[VMEM],
        out_specs=VMEM,
        compiler_params=PARAMS,
        name="arrange",
    )(rhs)
    vector = lax.all_to_all(send, "modes", split_axis=0, concat_axis=0, tiled=True)

    edge = (NCOEF, S, S, LANES)
    head, tail = pl.pallas_call(
        pack_kernel,
        grid=(1,),
        out_shape=[sds((NCOEF, S // 4, S, LANES), F32)] * 2,
        in_specs=[
            pl.BlockSpec(edge, lambda g: (0, 0, 0, 0)),
            pl.BlockSpec(edge, lambda g: (0, 0, 0, tiles - 1)),
        ],
        compiler_params=PARAMS,
        name="pack",
    )(jac_coef, jac_coef)
    up = [(i, (i + 1) % parts) for i in range(parts)]
    down = [(j, i) for i, j in up]
    after = lax.ppermute(head, "modes", down)
    before = lax.ppermute(tail, "modes", up)

    coupling, stencil = pl.pallas_call(
        functools.partial(coupling_kernel, n),
        out_shape=[sds((NCOEF * n, 3 * n), BF16), sds((4 * LANES, LANES), BF16)],
        in_specs=[VMEM] * 4,
        out_specs=[VMEM] * 2,
        compiler_params=PARAMS,
        name="coupling",
    )(*(x.reshape(1, -1) for x in (coef_index, row_mode, col_mode, multiplicity)))

    per = 2 * tiles + 1
    field = pltpu.VMEM((tiles + 1, S, n, LANES), F32)
    out = pl.pallas_call(
        functools.partial(main_kernel, n, tiles),
        out_shape=sds((n * per * S, LANES), F32),
        in_specs=[pl.BlockSpec(memory_space=pltpu.SMEM)] + [VMEM] * 6,
        out_specs=VMEM,
        scratch_shapes=[
            field,
            field,
            field,
            pltpu.VMEM((NCOEF * S, S, LANES), F32),
            pltpu.VMEM((2, 3 * n, S * LANES), BF16),
            pltpu.VMEM((2, S * n, 4 * LANES), BF16),
            pltpu.VMEM((2, NCOEF * n, S * LANES), F32),
            pltpu.VMEM((2, S * n, LANES), F32),
        ],
        compiler_params=PARAMS,
        name="krylov",
    )(
        diffusivity,
        vector.reshape(n * (tiles + 1) * S, LANES),
        jac_coef.reshape(NCOEF * S, S, cells),
        after,
        before,
        coupling,
        stencil,
    )
    got = lax.all_to_all(out.reshape(n, per, S, LANES), "modes", split_axis=0, concat_axis=0, tiled=True)
    update, basis_next = pl.pallas_call(
        functools.partial(combine_kernel, parts, tiles),
        out_shape=[sds(rhs.shape, F32)] * 2,
        in_specs=[VMEM] * 2,
        out_specs=[VMEM] * 2,
        compiler_params=PARAMS,
        name="combine",
    )(rhs, got.reshape(n * per * S, LANES))
    return (update, basis_next)


def solution(mesh):
    return jax.shard_map(
        local,
        mesh=mesh,
        in_specs=(
            P(("groups", "modes"), None, None),
            P(),
            P(None, None, None, "modes"),
            P(),
            P(),
            P(),
            P(),
        ),
        out_specs=(P(("groups", "modes"), None, None), P(("groups", "modes"), None, None)),
        check_vma=False,
    )
```

```python
import functools

import jax
import jax.numpy as jnp
from jax import lax
from jax.experimental import pallas as pl
from jax.experimental.pallas import tpu as pltpu
from jax.sharding import PartitionSpec as P

NCOEF = 9
GY = 32
S = 8
LANES = 128
F32 = jnp.float32
BF16 = jnp.bfloat16
VMEM = pl.BlockSpec(memory_space=pltpu.VMEM)
PARAMS = pltpu.CompilerParams(vmem_limit_bytes=40 * 1024 * 1024)


def lane_iota():
    return lax.broadcasted_iota(jnp.int32, (S, LANES), 1)


def arrange_kernel(parts, rhs_ref, out_ref):
    own, _, total = rhs_ref.shape
    cells = total // parts
    tiles = cells // LANES
    low = lane_iota() < LANES // 2
    for d in range(parts):
        after = ((d + 1) * cells) % total
        before = (d * cells - LANES) % total
        for m in range(own):
            for ct in range(tiles):
                at = d * cells + ct * LANES
                out_ref[d * own + m, ct] = rhs_ref[m, :, at : at + LANES]
            out_ref[d * own + m, tiles] = jnp.where(
                low, rhs_ref[m, :, after : after + LANES], rhs_ref[m, :, before : before + LANES]
            )


def pack_kernel(first_ref, last_ref, head_ref, tail_ref):
    piece = lane_iota() // GY
    for i in range(NCOEF):
        for q in range(S // 4):
            head = first_ref[i, q * 4]
            tail = pltpu.roll(last_ref[i, q * 4], GY, 1)
            for p in range(1, 4):
                head = jnp.where(piece == p, pltpu.roll(first_ref[i, q * 4 + p], GY * p, 1), head)
                moved = last_ref[i, q * 4 + p]
                if p < 3:
                    moved = pltpu.roll(moved, GY * (p + 1), 1)
                tail = jnp.where(piece == p, moved, tail)
            head_ref[i, q] = head
            tail_ref[i, q] = tail


def coupling_kernel(modes, coef_ref, row_ref, col_ref, mult_ref, out_ref, stencil_ref):
    rows, cols = out_ref.shape
    triples = coef_ref.shape[1]
    key = coef_ref[...] * modes + row_ref[...]
    weight = 0.25 * mult_ref[...].astype(F32)
    row = lax.broadcasted_iota(jnp.int32, (rows, triples), 0)
    left = jnp.where(row == key, weight, 0.0).astype(BF16)
    col = lax.rem(lax.broadcasted_iota(jnp.int32, (cols, triples), 0), modes)
    right = jnp.where(col == col_ref[...], 1.0, 0.0).astype(BF16)
    dense = lax.dot_general(left, right, (((1,), (1,)), ((), ())), preferred_element_type=F32)
    r = lax.broadcasted_iota(jnp.int32, (rows, cols), 0)
    c = lax.broadcasted_iota(jnp.int32, (rows, cols), 1)
    dense = dense + jnp.where(r == lax.rem(c, modes), 1.0, 0.0)
    high = dense.astype(BF16)
    low = (dense - high.astype(F32)).astype(BF16)
    out_ref[...] = jnp.where(c < 2 * modes, high.astype(F32), low.astype(F32)).astype(BF16)

    a = lax.broadcasted_iota(jnp.int32, (LANES, LANES), 0)
    b = lax.broadcasted_iota(jnp.int32, (LANES, LANES), 1)
    step = jnp.bitwise_and(a - b, GY - 1)
    same = (a // GY == b // GY) & ((step == 1) | (step == GY - 1))
    apart = jnp.abs(a - b)
    inner = jnp.where(apart == 0, 4.0, jnp.where(same | (apart == GY), -1.0, 0.0)).astype(BF16)
    outer = jnp.where(apart == LANES - GY, -1.0, 0.0).astype(BF16)
    stencil_ref[0:LANES] = inner
    stencil_ref[LANES : 2 * LANES] = inner
    stencil_ref[2 * LANES : 3 * LANES] = outer
    stencil_ref[3 * LANES :] = outer


def split(x):
    high = x.astype(BF16)
    return high, (x - high.astype(F32)).astype(BF16)


def ratio(a, b):
    return jnp.where(b > 0.0, a / jnp.where(b > 0.0, b, 1.0), 0.0)


def transpose_in(r_ref, v_ref, n, every):
    for ct in range(every):
        for s in range(S):
            v_ref[ct, s] = r_ref[pl.ds(ct * S + s, n, stride=every * S), :]


def unpack_edges(next_ref, prev_ref, jh_ref):
    lane = lane_iota()

    def unpack(i, _):
        for q in range(S // 4):
            after, before = next_ref[i, q], prev_ref[i, q]
            for p in range(4):
                a = after if p == 0 else pltpu.roll(after, LANES - GY * p, 1)
                b = before if p == 3 else pltpu.roll(before, LANES - GY - GY * p, 1)
                jh_ref[i * S + q * 4 + p] = jnp.where(lane < LANES // 2, a, b)
        return 0

    lax.fori_loop(0, NCOEF, unpack, 0)


def mix(src, ct, slot, every, coup_ref, stencil_ref, vs_ref, xs_ref, mx_ref, bs_ref):
    n = src.shape[2]
    wide = lax.broadcasted_iota(jnp.int32, (n, LANES), 1) < LANES // 2
    before, after = (ct - 1) % every, (ct + 1) % every
    for t in range(S):
        at = slice(t * LANES, (t + 1) * LANES)
        to = slice(t * n, (t + 1) * n)
        high, low = split(src[ct, t])
        vs_ref[slot, 0:n, at] = high
        vs_ref[slot, n : 2 * n, at] = low
        vs_ref[slot, 2 * n : 3 * n, at] = high
        xs_ref[slot, to, 0:LANES] = high
        xs_ref[slot, to, LANES : 2 * LANES] = low
        high, low = split(jnp.where(wide, src[after, t], src[before, t]))
        xs_ref[slot, to, 2 * LANES : 3 * LANES] = high
        xs_ref[slot, to, 3 * LANES :] = low
    mx_ref[slot] = jnp.dot(coup_ref[...], vs_ref[slot], preferred_element_type=F32)
    bs_ref[slot] = jnp.dot(xs_ref[slot], stencil_ref[...], preferred_element_type=F32)


def react(n, jac, slot, dif_ref, mx_ref, bs_ref, finish):
    for kb in range(0, n, 32):
        acc = [None] * 32
        for i in range(NCOEF):
            for t in range(S):
                m = [
                    mx_ref[slot, i * n + kb + kt * 8 : i * n + kb + kt * 8 + 8, t * LANES : (t + 1) * LANES]
                    for kt in range(4)
                ]
                for s in range(S):
                    j = jnp.broadcast_to(jac(i * S + s, t), (8, LANES))
                    for kt in range(4):
                        term = j * m[kt]
                        at = s * 4 + kt
                        acc[at] = term if acc[at] is None else acc[at] + term
        for s in range(S):
            for kt in range(4):
                k = kb + kt * 8
                b = bs_ref[slot, s * n + k : s * n + k + 8]
                finish(s, k, dif_ref[s] * b - acc[s * 4 + kt])


def tile_of(jac_ref, ct):
    return lambda row, t: jac_ref[row, t : t + 1, ct * LANES : (ct + 1) * LANES]


class Sums:
    def __init__(self):
        self.parts = {}

    def add(self, name, at, term):
        mine = self.parts.setdefault(name, {})
        mine[at % 4] = mine[at % 4] + term if at % 4 in mine else term

    def total(self, name):
        x = functools.reduce(lambda a, b: a + b, self.parts[name].values())
        return jnp.broadcast_to(jnp.sum(x, axis=(0, 1), keepdims=True), (8, LANES))


def first_kernel(
    n,
    tiles,
    place_ref,
    dif_ref,
    r_ref,
    jac_ref,
    next_ref,
    prev_ref,
    coup_ref,
    stencil_ref,
    v_ref,
    w_ref,
    sum_ref,
    *refs,
):
    every = tiles + 1
    send_refs, (jh_ref, vs_ref, xs_ref, mx_ref, bs_ref) = refs[: n // 8], refs[n // 8 :]
    work = (coup_ref, stencil_ref, vs_ref, xs_ref, mx_ref, bs_ref)
    transpose_in(r_ref, v_ref, n, every)
    unpack_edges(next_ref, prev_ref, jh_ref)
    sums = Sums()

    def finisher(ct):
        def finish(s, k, w):
            w_ref[ct, s, k : k + 8] = w
            if ct < tiles:
                v = v_ref[ct, s, k : k + 8]
                sums.add("rr", k // 8, v * v)
                sums.add("rw", k // 8, v * w)

        return finish

    order = list(range(tiles)) + [tiles]
    mix(v_ref, order[0], 0, every, *work)
    for at, ct in enumerate(order):
        if at + 1 < every:
            mix(v_ref, order[at + 1], (at + 1) % 2, every, *work)
        jac = tile_of(jac_ref, ct) if ct < tiles else tile_of(jh_ref, 0)
        react(n, jac, at % 2, dif_ref, mx_ref, bs_ref, finisher(ct))
    for q in range(n // 8):
        at = pl.multiple_of(jnp.bitwise_xor(place_ref[0], q) * 8, 8)
        for ct in range(tiles):
            for s in range(S):
                send_refs[q][pl.ds(ct * S + s, 8, stride=tiles * S), :] = w_ref[ct, s, pl.ds(at, 8)]
    sum_ref[0:8] = sums.total("rr")
    sum_ref[8:16] = sums.total("rw")


def second_kernel(
    n,
    tiles,
    dif_ref,
    v_ref,
    w_ref,
    sum_ref,
    jac_ref,
    coup_ref,
    stencil_ref,
    out_ref,
    z_ref,
    vs_ref,
    xs_ref,
    mx_ref,
    bs_ref,
):
    every = tiles + 1
    per = tiles * S + 1
    work = (coup_ref, stencil_ref, vs_ref, xs_ref, mx_ref, bs_ref)
    rr, rw = sum_ref[0:8], sum_ref[8:16]
    c1 = ratio(rw, rr)
    sums = Sums()

    def finisher(ct):
        def finish(s, k, z):
            v, w = v_ref[ct, s, k : k + 8], w_ref[ct, s, k : k + 8]
            z_ref[ct, s, k : k + 8] = z
            out_ref[pl.ds(k * per + ct * S + s, 8, stride=per), :] = z
            u = w - c1 * v
            sums.add("uu", k // 8, u * u)
            sums.add("ur", k // 8, u * v)
            sums.add("uz", k // 8, u * z)
            sums.add("rz", k // 8, v * z)

        return finish

    mix(w_ref, 0, 0, every, *work)
    for ct in range(tiles):
        if ct + 1 < tiles:
            mix(w_ref, ct + 1, (ct + 1) % 2, every, *work)
        react(n, tile_of(jac_ref, ct), ct % 2, dif_ref, mx_ref, bs_ref, finisher(ct))
    uu, ur, uz, rz = (sums.total(name) for name in ("uu", "ur", "uz", "rz"))
    c2 = ratio(rz, rr)
    c3 = ratio(uz - c2 * ur, uu)
    for ct in range(tiles):
        for s in range(S):
            for k in range(0, n, 8):
                v, w, z = (ref[ct, s, k : k + 8] for ref in (v_ref, w_ref, z_ref))
                x = (z - c2 * v) - c3 * (w - c1 * v)
                sums.add("xx", k // 8, x * x)
    xx = sums.total("xx")
    lane = lane_iota()
    tile = jnp.zeros((8, LANES), F32)
    for q, value in enumerate((rr, c1, uu, c2, c3, xx)):
        tile = jnp.where(lane == q, value, tile)
    for k in range(0, n, 8):
        out_ref[pl.ds(k * per + tiles * S, 8, stride=per), :] = tile


def relay_kernel(own, place_ref, *refs):
    parts = 8 // own
    count = len(refs) - parts
    for k in range(parts):
        at = jnp.bitwise_xor(place_ref[1], k)
        for q in range(count):
            refs[count + k][q] = refs[q][at]


def combine_kernel(parts, tiles, place_ref, rhs_ref, got_ref, *refs):
    own = rhs_ref.shape[0]
    plane = 8 // own
    w_refs, (update_ref, basis_ref) = refs[:plane], refs[plane:]
    per = tiles * S + 1
    stats = got_ref[pl.ds(tiles * S, parts, stride=own * per), :]

    def stat(q):
        return jnp.broadcast_to(stats[:, q : q + 1], (parts, LANES))

    def add(x):
        return jnp.sum(x, axis=0, keepdims=True)

    rr, c1, uu, c2, c3, xx = (stat(q) for q in range(6))
    all_rr = add(rr)
    g1 = add(rr * c1) / all_rr
    g2 = add(rr * c2) / all_rr
    e1, e2 = c1 - g1, c2 - g2
    all_uu = add(uu + e1 * e1 * rr)
    g3 = add(c3 * uu + e1 * e2 * rr) / all_uu
    e3 = c3 - g3
    f = e2 - g3 * e1
    all_xx = add(xx + e3 * e3 * uu + f * f * rr)
    beta, nu, nx = jnp.sqrt(all_rr), jnp.sqrt(all_uu), jnp.sqrt(all_xx)
    h11 = 1.0 + g1
    h21 = nu / beta
    h12 = (g2 - g1 * g1) * beta / nu
    h22 = 1.0 + (g3 - g1)
    h32 = nx / nu
    m11 = h11 * h11 + h21 * h21
    m12 = h11 * h12 + h21 * h22
    m22 = h12 * h12 + h22 * h22 + h32 * h32
    b1, b2 = beta * h11, beta * h12
    determ = m11 * m22 - m12 * m12
    y1 = (m22 * b1 - m12 * b2) / determ
    y2 = (m11 * b2 - m12 * b1) / determ
    uw = y2 / nu
    ur = y1 / beta - uw * g1
    bz = 1.0 / nx
    bw = -g3 * bz
    br = (g3 * g1 - g2) * bz
    ur, uw, br, bw, bz = (jnp.broadcast_to(x, (S, LANES)) for x in (ur, uw, br, bw, bz))
    for d in range(parts):
        for m in range(own):
            for ct in range(tiles):
                at = slice((d * tiles + ct) * LANES, (d * tiles + ct + 1) * LANES)
                base = (d * own + m) * per + ct * S
                basis_ref[m, :, at] = br * rhs_ref[m, :, at] + bz * got_ref[base : base + S, :]
    for k in range(plane):
        for q in range(parts // plane):
            d = jnp.bitwise_xor(place_ref[0], q) * plane + jnp.bitwise_xor(place_ref[1], k)
            for m in range(own):
                for ct in range(tiles):
                    at = pl.ds(pl.multiple_of(d * (tiles * LANES) + ct * LANES, LANES), LANES)
                    w = w_refs[k][q, m, ct * S : (ct + 1) * S, :]
                    update_ref[m, :, at] = ur * rhs_ref[m, :, at] + uw * w
                    basis_ref[m, :, at] += bw * w


def local(rhs, diffusivity, jac_coef, coef_index, row_mode, col_mode, multiplicity):
    parts = lax.axis_size("modes")
    own, _, total = rhs.shape
    n = own * parts
    cells = total // parts
    tiles = cells // LANES
    plane = 8 // own
    sds = jax.ShapeDtypeStruct
    smem = pl.BlockSpec(memory_space=pltpu.SMEM)
    index = lax.axis_index("modes")
    place = jnp.stack([index // plane, index % plane]).astype(jnp.int32)

    send = pl.pallas_call(
        functools.partial(arrange_kernel, parts),
        out_shape=sds((n, tiles + 1, S, LANES), F32),
        in_specs=[VMEM],
        out_specs=VMEM,
        compiler_params=PARAMS,
        name="arrange",
    )(rhs)
    vector = lax.all_to_all(send, "modes", split_axis=0, concat_axis=0, tiled=True)

    edge = (NCOEF, S, S, LANES)
    head, tail = pl.pallas_call(
        pack_kernel,
        grid=(1,),
        out_shape=[sds((NCOEF, S // 4, S, LANES), F32)] * 2,
        in_specs=[
            pl.BlockSpec(edge, lambda g: (0, 0, 0, 0)),
            pl.BlockSpec(edge, lambda g: (0, 0, 0, tiles - 1)),
        ],
        compiler_params=PARAMS,
        name="pack",
    )(jac_coef, jac_coef)
    up = [(i, (i + 1) % parts) for i in range(parts)]
    down = [(j, i) for i, j in up]
    after = lax.ppermute(head, "modes", down)
    before = lax.ppermute(tail, "modes", up)

    coupling, stencil = pl.pallas_call(
        functools.partial(coupling_kernel, n),
        out_shape=[sds((NCOEF * n, 3 * n), BF16), sds((4 * LANES, LANES), BF16)],
        in_specs=[VMEM] * 4,
        out_specs=[VMEM] * 2,
        compiler_params=PARAMS,
        name="coupling",
    )(*(x.reshape(1, -1) for x in (coef_index, row_mode, col_mode, multiplicity)))

    jac = jac_coef.reshape(NCOEF * S, S, cells)
    field = (tiles + 1, S, n, LANES)
    work = [
        pltpu.VMEM((2, 3 * n, S * LANES), BF16),
        pltpu.VMEM((2, S * n, 4 * LANES), BF16),
        pltpu.VMEM((2, NCOEF * n, S * LANES), F32),
        pltpu.VMEM((2, S * n, LANES), F32),
    ]
    v, w, sums, *w_send = pl.pallas_call(
        functools.partial(first_kernel, n, tiles),
        out_shape=[sds(field, F32)] * 2 + [sds((16, LANES), F32)] + [sds((8 * tiles * S, LANES), F32)] * (n // 8),
        in_specs=[smem] * 2 + [VMEM] * 6,
        out_specs=[VMEM] * (3 + n // 8),
        scratch_shapes=[pltpu.VMEM((NCOEF * S, S, LANES), F32)] + work,
        compiler_params=PARAMS,
        name="first",
    )(place, diffusivity, vector.reshape(n * (tiles + 1) * S, LANES), jac, after, before, coupling, stencil)

    moved = w_send[:1]
    for q in range(1, n // 8):
        moved.append(lax.ppermute(w_send[q], "modes", [(i, i ^ (q * plane)) for i in range(parts)]))

    z_send = pl.pallas_call(
        functools.partial(second_kernel, n, tiles),
        out_shape=sds((n * (tiles * S + 1), LANES), F32),
        in_specs=[smem] + [VMEM] * 6,
        out_specs=VMEM,
        scratch_shapes=[pltpu.VMEM(field, F32)] + work,
        compiler_params=PARAMS,
        cost_estimate=pl.CostEstimate(flops=2 * NCOEF * S * n * n * cells, bytes_accessed=16 << 20, transcendentals=0),
        name="second",
    )(diffusivity, v, w, sums, jac, coupling, stencil)
    line = (tiles * S + 1) * LANES
    got = lax.all_to_all(z_send.reshape(n, 1, line), "modes", split_axis=0, concat_axis=0, tiled=True)

    relayed = pl.pallas_call(
        functools.partial(relay_kernel, own),
        out_shape=[sds((n // 8, own, tiles * S, LANES), F32)] * plane,
        in_specs=[smem] + [VMEM] * (n // 8),
        out_specs=[VMEM] * plane,
        compiler_params=PARAMS,
        cost_estimate=pl.CostEstimate(flops=10**11, bytes_accessed=1 << 20, transcendentals=0),
        name="relay",
    )(place, *(x.reshape(plane, own, tiles * S, LANES) for x in moved))
    w_own = [relayed[0]]
    for k in range(1, plane):
        w_own.append(lax.ppermute(relayed[k], "modes", [(i, i ^ k) for i in range(parts)]))

    update, basis_next = pl.pallas_call(
        functools.partial(combine_kernel, parts, tiles),
        out_shape=[sds(rhs.shape, F32)] * 2,
        in_specs=[smem] + [VMEM] * (2 + plane),
        out_specs=[VMEM] * 2,
        compiler_params=PARAMS,
        name="combine",
    )(place, rhs, got.reshape(n * (tiles * S + 1), LANES), *w_own)
    return (update, basis_next)


def solution(mesh):
    return jax.shard_map(
        local,
        mesh=mesh,
        in_specs=(
            P(("groups", "modes"), None, None),
            P(),
            P(None, None, None, "modes"),
            P(),
            P(),
            P(),
            P(),
        ),
        out_specs=(P(("groups", "modes"), None, None), P(("groups", "modes"), None, None)),
        check_vma=False,
    )
```

```python
import functools

import jax
import jax.numpy as jnp
from jax import lax
from jax.experimental import pallas as pl
from jax.experimental.pallas import tpu as pltpu
from jax.sharding import PartitionSpec as P

NCOEF = 9
GY = 32
S = 8
LANES = 128
F32 = jnp.float32
BF16 = jnp.bfloat16
VMEM = pl.BlockSpec(memory_space=pltpu.VMEM)
PARAMS = pltpu.CompilerParams(vmem_limit_bytes=40 * 1024 * 1024)


def lane_iota():
    return lax.broadcasted_iota(jnp.int32, (S, LANES), 1)


def arrange_kernel(parts, early, place_ref, rhs_ref, out_ref, *refs):
    own, _, total = rhs_ref.shape
    cells = total // parts
    tiles = cells // LANES
    plane = 8 // own
    low = lane_iota() < LANES // 2
    for q in range(parts // plane):
        base = jnp.bitwise_xor(place_ref[0], q) * plane
        for k in range(plane):
            for m in range(own):
                for ct in range(early):
                    at = pl.multiple_of((base + k) * cells + ct * LANES, LANES)
                    refs[q][k, m, ct * S : (ct + 1) * S, :] = rhs_ref[m, :, pl.ds(at, LANES)]
    for d in range(parts):
        after = ((d + 1) * cells) % total
        before = (d * cells - LANES) % total
        for m in range(own):
            for ct in range(early, tiles):
                at = d * cells + ct * LANES
                out_ref[d * own + m, ct - early] = rhs_ref[m, :, at : at + LANES]
            out_ref[d * own + m, tiles - early] = jnp.where(
                low, rhs_ref[m, :, after : after + LANES], rhs_ref[m, :, before : before + LANES]
            )


def pack_kernel(first_ref, last_ref, head_ref, tail_ref):
    piece = lane_iota() // GY
    for i in range(NCOEF):
        for q in range(S // 4):
            head = first_ref[i, q * 4]
            tail = pltpu.roll(last_ref[i, q * 4], GY, 1)
            for p in range(1, 4):
                head = jnp.where(piece == p, pltpu.roll(first_ref[i, q * 4 + p], GY * p, 1), head)
                moved = last_ref[i, q * 4 + p]
                if p < 3:
                    moved = pltpu.roll(moved, GY * (p + 1), 1)
                tail = jnp.where(piece == p, moved, tail)
            head_ref[i, q] = head
            tail_ref[i, q] = tail


def coupling_kernel(modes, coef_ref, row_ref, col_ref, mult_ref, out_ref, stencil_ref):
    rows, cols = out_ref.shape
    triples = coef_ref.shape[1]
    key = coef_ref[...] * modes + row_ref[...]
    weight = 0.25 * mult_ref[...].astype(F32)
    row = lax.broadcasted_iota(jnp.int32, (rows, triples), 0)
    left = jnp.where(row == key, weight, 0.0).astype(BF16)
    col = lax.rem(lax.broadcasted_iota(jnp.int32, (cols, triples), 0), modes)
    right = jnp.where(col == col_ref[...], 1.0, 0.0).astype(BF16)
    dense = lax.dot_general(left, right, (((1,), (1,)), ((), ())), preferred_element_type=F32)
    r = lax.broadcasted_iota(jnp.int32, (rows, cols), 0)
    c = lax.broadcasted_iota(jnp.int32, (rows, cols), 1)
    dense = dense + jnp.where(r == lax.rem(c, modes), 1.0, 0.0)
    high = dense.astype(BF16)
    low = (dense - high.astype(F32)).astype(BF16)
    out_ref[...] = jnp.where(c < 2 * modes, high.astype(F32), low.astype(F32)).astype(BF16)

    a = lax.broadcasted_iota(jnp.int32, (LANES, LANES), 0)
    b = lax.broadcasted_iota(jnp.int32, (LANES, LANES), 1)
    step = jnp.bitwise_and(a - b, GY - 1)
    same = (a // GY == b // GY) & ((step == 1) | (step == GY - 1))
    apart = jnp.abs(a - b)
    inner = jnp.where(apart == 0, 4.0, jnp.where(same | (apart == GY), -1.0, 0.0)).astype(BF16)
    outer = jnp.where(apart == LANES - GY, -1.0, 0.0).astype(BF16)
    stencil_ref[0:LANES] = inner
    stencil_ref[LANES : 2 * LANES] = inner
    stencil_ref[2 * LANES : 3 * LANES] = outer
    stencil_ref[3 * LANES :] = outer


def split(x):
    high = x.astype(BF16)
    return high, (x - high.astype(F32)).astype(BF16)


def ratio(a, b):
    return jnp.where(b > 0.0, a / jnp.where(b > 0.0, b, 1.0), 0.0)


def transpose_in(place_ref, near_refs, gather_ref, r_ref, v_ref, early):
    every, _, n, _ = v_ref.shape
    plane = len(near_refs)
    for k in range(plane):
        for q in range(near_refs[k].shape[0]):
            d = jnp.bitwise_xor(place_ref[0], q) * plane + jnp.bitwise_xor(place_ref[1], k)
            gather_ref[d] = near_refs[k][q]
    flat = gather_ref.reshape(n * early * S, LANES)
    for ct in range(early):
        for s in range(S):
            v_ref[ct, s] = flat[pl.ds(ct * S + s, n, stride=early * S), :]
    for ct in range(early, every):
        for s in range(S):
            v_ref[ct, s] = r_ref[pl.ds((ct - early) * S + s, n, stride=(every - early) * S), :]


def unpack_edges(next_ref, prev_ref, jh_ref):
    lane = lane_iota()

    def unpack(i, _):
        for q in range(S // 4):
            after, before = next_ref[i, q], prev_ref[i, q]
            for p in range(4):
                a = after if p == 0 else pltpu.roll(after, LANES - GY * p, 1)
                b = before if p == 3 else pltpu.roll(before, LANES - GY - GY * p, 1)
                jh_ref[i * S + q * 4 + p] = jnp.where(lane < LANES // 2, a, b)
        return 0

    lax.fori_loop(0, NCOEF, unpack, 0)


def mix(src, ct, slot, every, coup_ref, stencil_ref, vs_ref, xs_ref, mx_ref, bs_ref):
    n = src.shape[2]
    wide = lax.broadcasted_iota(jnp.int32, (n, LANES), 1) < LANES // 2
    before, after = (ct - 1) % every, (ct + 1) % every
    for t in range(S):
        at = slice(t * LANES, (t + 1) * LANES)
        to = slice(t * n, (t + 1) * n)
        high, low = split(src[ct, t])
        vs_ref[slot, 0:n, at] = high
        vs_ref[slot, n : 2 * n, at] = low
        vs_ref[slot, 2 * n : 3 * n, at] = high
        xs_ref[slot, to, 0:LANES] = high
        xs_ref[slot, to, LANES : 2 * LANES] = low
        high, low = split(jnp.where(wide, src[after, t], src[before, t]))
        xs_ref[slot, to, 2 * LANES : 3 * LANES] = high
        xs_ref[slot, to, 3 * LANES :] = low
    mx_ref[slot] = jnp.dot(coup_ref[...], vs_ref[slot], preferred_element_type=F32)
    bs_ref[slot] = jnp.dot(xs_ref[slot], stencil_ref[...], preferred_element_type=F32)


def react(n, jac, slot, dif_ref, mx_ref, bs_ref, finish):
    for kb in range(0, n, 32):
        acc = [None] * 32
        for i in range(NCOEF):
            for t in range(S):
                m = [
                    mx_ref[slot, i * n + kb + kt * 8 : i * n + kb + kt * 8 + 8, t * LANES : (t + 1) * LANES]
                    for kt in range(4)
                ]
                for s in range(S):
                    j = jnp.broadcast_to(jac(i * S + s, t), (8, LANES))
                    for kt in range(4):
                        term = j * m[kt]
                        at = s * 4 + kt
                        acc[at] = term if acc[at] is None else acc[at] + term
        for s in range(S):
            for kt in range(4):
                k = kb + kt * 8
                b = bs_ref[slot, s * n + k : s * n + k + 8]
                finish(s, k, dif_ref[s] * b - acc[s * 4 + kt])


def tile_of(jac_ref, ct):
    return lambda row, t: jac_ref[row, t : t + 1, ct * LANES : (ct + 1) * LANES]


class Sums:
    def __init__(self):
        self.parts = {}

    def add(self, name, at, term):
        mine = self.parts.setdefault(name, {})
        mine[at % 4] = mine[at % 4] + term if at % 4 in mine else term

    def total(self, name):
        x = functools.reduce(lambda a, b: a + b, self.parts[name].values())
        return jnp.broadcast_to(jnp.sum(x, axis=(0, 1), keepdims=True), (8, LANES))


def first_kernel(
    n,
    tiles,
    early,
    plane,
    place_ref,
    dif_ref,
    r_ref,
    jac_ref,
    next_ref,
    prev_ref,
    coup_ref,
    stencil_ref,
    *refs,
):
    every = tiles + 1
    near_refs, (v_ref, w_ref, sum_ref), refs = refs[:plane], refs[plane : plane + 3], refs[plane + 3 :]
    send_refs, (gather_ref, jh_ref, vs_ref, xs_ref, mx_ref, bs_ref) = refs[: n // 8], refs[n // 8 :]
    work = (coup_ref, stencil_ref, vs_ref, xs_ref, mx_ref, bs_ref)
    transpose_in(place_ref, near_refs, gather_ref, r_ref, v_ref, early)
    unpack_edges(next_ref, prev_ref, jh_ref)
    sums = Sums()

    def finisher(ct):
        def finish(s, k, w):
            w_ref[ct, s, k : k + 8] = w
            if ct < tiles:
                v = v_ref[ct, s, k : k + 8]
                sums.add("rr", k // 8, v * v)
                sums.add("rw", k // 8, v * w)

        return finish

    order = list(range(tiles)) + [tiles]
    mix(v_ref, order[0], 0, every, *work)
    for at, ct in enumerate(order):
        if at + 1 < every:
            mix(v_ref, order[at + 1], (at + 1) % 2, every, *work)
        jac = tile_of(jac_ref, ct) if ct < tiles else tile_of(jh_ref, 0)
        react(n, jac, at % 2, dif_ref, mx_ref, bs_ref, finisher(ct))
    for q in range(n // 8):
        at = pl.multiple_of(jnp.bitwise_xor(place_ref[0], q) * 8, 8)
        flat = send_refs[q].reshape(8 * tiles * S, LANES)
        for ct in range(tiles):
            for s in range(S):
                flat[pl.ds(ct * S + s, 8, stride=tiles * S), :] = w_ref[ct, s, pl.ds(at, 8)]
    sum_ref[0:8] = sums.total("rr")
    sum_ref[8:16] = sums.total("rw")


def second_kernel(
    n,
    tiles,
    dif_ref,
    v_ref,
    w_ref,
    sum_ref,
    jac_ref,
    coup_ref,
    stencil_ref,
    out_ref,
    z_ref,
    vs_ref,
    xs_ref,
    mx_ref,
    bs_ref,
):
    every = tiles + 1
    per = tiles * S + 1
    work = (coup_ref, stencil_ref, vs_ref, xs_ref, mx_ref, bs_ref)
    rr, rw = sum_ref[0:8], sum_ref[8:16]
    c1 = ratio(rw, rr)
    sums = Sums()

    def finisher(ct):
        def finish(s, k, z):
            v, w = v_ref[ct, s, k : k + 8], w_ref[ct, s, k : k + 8]
            z_ref[ct, s, k : k + 8] = z
            out_ref[pl.ds(k * per + ct * S + s, 8, stride=per), :] = z
            u = w - c1 * v
            sums.add("uu", k // 8, u * u)
            sums.add("ur", k // 8, u * v)
            sums.add("uz", k // 8, u * z)
            sums.add("rz", k // 8, v * z)

        return finish

    mix(w_ref, 0, 0, every, *work)
    for ct in range(tiles):
        if ct + 1 < tiles:
            mix(w_ref, ct + 1, (ct + 1) % 2, every, *work)
        react(n, tile_of(jac_ref, ct), ct % 2, dif_ref, mx_ref, bs_ref, finisher(ct))
    uu, ur, uz, rz = (sums.total(name) for name in ("uu", "ur", "uz", "rz"))
    c2 = ratio(rz, rr)
    c3 = ratio(uz - c2 * ur, uu)
    for ct in range(tiles):
        for s in range(S):
            for k in range(0, n, 8):
                v, w, z = (ref[ct, s, k : k + 8] for ref in (v_ref, w_ref, z_ref))
                x = (z - c2 * v) - c3 * (w - c1 * v)
                sums.add("xx", k // 8, x * x)
    xx = sums.total("xx")
    lane = lane_iota()
    tile = jnp.zeros((8, LANES), F32)
    for q, value in enumerate((rr, c1, uu, c2, c3, xx)):
        tile = jnp.where(lane == q, value, tile)
    for k in range(0, n, 8):
        out_ref[pl.ds(k * per + tiles * S, 8, stride=per), :] = tile


def relay_kernel(own, place_ref, *refs):
    parts = 8 // own
    count = len(refs) - parts
    for k in range(parts):
        at = jnp.bitwise_xor(place_ref[1], k)
        for q in range(count):
            refs[count + k][q] = refs[q][at]


def combine_kernel(parts, tiles, place_ref, rhs_ref, got_ref, *refs):
    own = rhs_ref.shape[0]
    plane = 8 // own
    w_refs, (update_ref, basis_ref) = refs[:plane], refs[plane:]
    per = tiles * S + 1
    stats = got_ref[pl.ds(tiles * S, parts, stride=own * per), :]

    def stat(q):
        return jnp.broadcast_to(stats[:, q : q + 1], (parts, LANES))

    def add(x):
        return jnp.sum(x, axis=0, keepdims=True)

    rr, c1, uu, c2, c3, xx = (stat(q) for q in range(6))
    all_rr = add(rr)
    g1 = add(rr * c1) / all_rr
    g2 = add(rr * c2) / all_rr
    e1, e2 = c1 - g1, c2 - g2
    all_uu = add(uu + e1 * e1 * rr)
    g3 = add(c3 * uu + e1 * e2 * rr) / all_uu
    e3 = c3 - g3
    f = e2 - g3 * e1
    all_xx = add(xx + e3 * e3 * uu + f * f * rr)
    beta, nu, nx = jnp.sqrt(all_rr), jnp.sqrt(all_uu), jnp.sqrt(all_xx)
    h11 = 1.0 + g1
    h21 = nu / beta
    h12 = (g2 - g1 * g1) * beta / nu
    h22 = 1.0 + (g3 - g1)
    h32 = nx / nu
    m11 = h11 * h11 + h21 * h21
    m12 = h11 * h12 + h21 * h22
    m22 = h12 * h12 + h22 * h22 + h32 * h32
    b1, b2 = beta * h11, beta * h12
    determ = m11 * m22 - m12 * m12
    y1 = (m22 * b1 - m12 * b2) / determ
    y2 = (m11 * b2 - m12 * b1) / determ
    uw = y2 / nu
    ur = y1 / beta - uw * g1
    bz = 1.0 / nx
    bw = -g3 * bz
    br = (g3 * g1 - g2) * bz
    ur, uw, br, bw, bz = (jnp.broadcast_to(x, (S, LANES)) for x in (ur, uw, br, bw, bz))
    for d in range(parts):
        for m in range(own):
            for ct in range(tiles):
                at = slice((d * tiles + ct) * LANES, (d * tiles + ct + 1) * LANES)
                base = (d * own + m) * per + ct * S
                basis_ref[m, :, at] = br * rhs_ref[m, :, at] + bz * got_ref[base : base + S, :]
    for k in range(plane):
        for q in range(parts // plane):
            d = jnp.bitwise_xor(place_ref[0], q) * plane + jnp.bitwise_xor(place_ref[1], k)
            for m in range(own):
                for ct in range(tiles):
                    at = pl.ds(pl.multiple_of(d * (tiles * LANES) + ct * LANES, LANES), LANES)
                    w = w_refs[k][q, m, ct * S : (ct + 1) * S, :]
                    update_ref[m, :, at] = ur * rhs_ref[m, :, at] + uw * w
                    basis_ref[m, :, at] += bw * w


def local(rhs, diffusivity, jac_coef, coef_index, row_mode, col_mode, multiplicity):
    parts = lax.axis_size("modes")
    own, _, total = rhs.shape
    n = own * parts
    cells = total // parts
    tiles = cells // LANES
    plane = 8 // own
    sds = jax.ShapeDtypeStruct
    smem = pl.BlockSpec(memory_space=pltpu.SMEM)
    index = lax.axis_index("modes")
    place = jnp.stack([index // plane, index % plane]).astype(jnp.int32)

    early = (tiles + 1) // 2
    block = (plane, own, early * S, LANES)

    def across(arrays):
        lead, rows = len(arrays), arrays[0].shape[2]
        come = [arrays[0]]
        for q in range(1, lead):
            come.append(lax.ppermute(arrays[q], "modes", [(i, i ^ (q * plane)) for i in range(parts)]))
        relayed = pl.pallas_call(
            functools.partial(relay_kernel, own),
            out_shape=[sds((lead, own, rows, LANES), F32)] * plane,
            in_specs=[smem] + [VMEM] * lead,
            out_specs=[VMEM] * plane,
            compiler_params=PARAMS,
            cost_estimate=pl.CostEstimate(flops=10**11, bytes_accessed=1 << 20, transcendentals=0),
            name="relay",
        )(place, *come)
        out = [relayed[0]]
        for k in range(1, plane):
            out.append(lax.ppermute(relayed[k], "modes", [(i, i ^ k) for i in range(parts)]))
        return out

    late_send, *early_send = pl.pallas_call(
        functools.partial(arrange_kernel, parts, early),
        out_shape=[sds((n, tiles + 1 - early, S, LANES), F32)] + [sds(block, F32)] * (parts // plane),
        in_specs=[smem, VMEM],
        out_specs=[VMEM] * (1 + parts // plane),
        compiler_params=PARAMS,
        name="arrange",
    )(place, rhs)
    near = across(early_send)
    vector = lax.all_to_all(late_send, "modes", split_axis=0, concat_axis=0, tiled=True)

    edge = (NCOEF, S, S, LANES)
    head, tail = pl.pallas_call(
        pack_kernel,
        grid=(1,),
        out_shape=[sds((NCOEF, S // 4, S, LANES), F32)] * 2,
        in_specs=[
            pl.BlockSpec(edge, lambda g: (0, 0, 0, 0)),
            pl.BlockSpec(edge, lambda g: (0, 0, 0, tiles - 1)),
        ],
        compiler_params=PARAMS,
        name="pack",
    )(jac_coef, jac_coef)
    up = [(i, (i + 1) % parts) for i in range(parts)]
    down = [(j, i) for i, j in up]
    after = lax.ppermute(head, "modes", down)
    before = lax.ppermute(tail, "modes", up)

    coupling, stencil = pl.pallas_call(
        functools.partial(coupling_kernel, n),
        out_shape=[sds((NCOEF * n, 3 * n), BF16), sds((4 * LANES, LANES), BF16)],
        in_specs=[VMEM] * 4,
        out_specs=[VMEM] * 2,
        compiler_params=PARAMS,
        name="coupling",
    )(*(x.reshape(1, -1) for x in (coef_index, row_mode, col_mode, multiplicity)))

    jac = jac_coef.reshape(NCOEF * S, S, cells)
    field = (tiles + 1, S, n, LANES)
    work = [
        pltpu.VMEM((2, 3 * n, S * LANES), BF16),
        pltpu.VMEM((2, S * n, 4 * LANES), BF16),
        pltpu.VMEM((2, NCOEF * n, S * LANES), F32),
        pltpu.VMEM((2, S * n, LANES), F32),
    ]
    v, w, sums, *w_send = pl.pallas_call(
        functools.partial(first_kernel, n, tiles, early, plane),
        out_shape=[sds(field, F32)] * 2 + [sds((16, LANES), F32)] + [sds((plane, own, tiles * S, LANES), F32)] * (n // 8),
        in_specs=[smem] * 2 + [VMEM] * (6 + plane),
        out_specs=[VMEM] * (3 + n // 8),
        scratch_shapes=[
            pltpu.VMEM((parts, own, early * S, LANES), F32),
            pltpu.VMEM((NCOEF * S, S, LANES), F32),
        ]
        + work,
        compiler_params=PARAMS,
        name="first",
    )(
        place,
        diffusivity,
        vector.reshape(n * (tiles + 1 - early) * S, LANES),
        jac,
        after,
        before,
        coupling,
        stencil,
        *near,
    )

    w_own = across(w_send)

    z_send = pl.pallas_call(
        functools.partial(second_kernel, n, tiles),
        out_shape=sds((n * (tiles * S + 1), LANES), F32),
        in_specs=[smem] + [VMEM] * 6,
        out_specs=VMEM,
        scratch_shapes=[pltpu.VMEM(field, F32)] + work,
        compiler_params=PARAMS,
        cost_estimate=pl.CostEstimate(flops=2 * NCOEF * S * n * n * cells, bytes_accessed=16 << 20, transcendentals=0),
        name="second",
    )(diffusivity, v, w, sums, jac, coupling, stencil)
    line = (tiles * S + 1) * LANES
    got = lax.all_to_all(z_send.reshape(n, 1, line), "modes", split_axis=0, concat_axis=0, tiled=True)

    update, basis_next = pl.pallas_call(
        functools.partial(combine_kernel, parts, tiles),
        out_shape=[sds(rhs.shape, F32)] * 2,
        in_specs=[smem] + [VMEM] * (2 + plane),
        out_specs=[VMEM] * 2,
        compiler_params=PARAMS,
        name="combine",
    )(place, rhs, got.reshape(n * (tiles * S + 1), LANES), *w_own)
    return (update, basis_next)


def solution(mesh):
    return jax.shard_map(
        local,
        mesh=mesh,
        in_specs=(
            P(("groups", "modes"), None, None),
            P(),
            P(None, None, None, "modes"),
            P(),
            P(),
            P(),
            P(),
        ),
        out_specs=(P(("groups", "modes"), None, None), P(("groups", "modes"), None, None)),
        check_vma=False,
    )
```

```python
import functools

import jax
import jax.numpy as jnp
from jax import lax
from jax.experimental import pallas as pl
from jax.experimental.pallas import tpu as pltpu
from jax.sharding import PartitionSpec as P

NCOEF = 9
GY = 32
S = 8
LANES = 128
F32 = jnp.float32
BF16 = jnp.bfloat16
VMEM = pl.BlockSpec(memory_space=pltpu.VMEM)
PARAMS = pltpu.CompilerParams(vmem_limit_bytes=40 * 1024 * 1024)


def lane_iota():
    return lax.broadcasted_iota(jnp.int32, (S, LANES), 1)


def arrange_kernel(parts, early, place_ref, rhs_ref, out_ref, *refs):
    own, _, total = rhs_ref.shape
    cells = total // parts
    tiles = cells // LANES
    plane = 8 // own
    low = lane_iota() < LANES // 2
    for q in range(parts // plane):
        base = jnp.bitwise_xor(place_ref[0], q) * plane
        for k in range(plane):
            for m in range(own):
                for ct in range(early):
                    at = pl.multiple_of((base + k) * cells + ct * LANES, LANES)
                    refs[q][k, m, ct * S : (ct + 1) * S, :] = rhs_ref[m, :, pl.ds(at, LANES)]
    for d in range(parts):
        after = ((d + 1) * cells) % total
        before = (d * cells - LANES) % total
        for m in range(own):
            for ct in range(early, tiles):
                at = d * cells + ct * LANES
                out_ref[d * own + m, ct - early] = rhs_ref[m, :, at : at + LANES]
            out_ref[d * own + m, tiles - early] = jnp.where(
                low, rhs_ref[m, :, after : after + LANES], rhs_ref[m, :, before : before + LANES]
            )


def pack_kernel(first_ref, last_ref, _, head_ref, tail_ref):
    piece = lane_iota() // GY
    for i in range(NCOEF):
        for q in range(S // 4):
            head = first_ref[i, q * 4]
            tail = pltpu.roll(last_ref[i, q * 4], GY, 1)
            for p in range(1, 4):
                head = jnp.where(piece == p, pltpu.roll(first_ref[i, q * 4 + p], GY * p, 1), head)
                moved = last_ref[i, q * 4 + p]
                if p < 3:
                    moved = pltpu.roll(moved, GY * (p + 1), 1)
                tail = jnp.where(piece == p, moved, tail)
            head_ref[i, q] = head
            tail_ref[i, q] = tail


def coupling_kernel(modes, coef_ref, row_ref, col_ref, mult_ref, out_ref, stencil_ref):
    rows, cols = out_ref.shape
    triples = coef_ref.shape[1]
    key = coef_ref[...] * modes + row_ref[...]
    weight = 0.25 * mult_ref[...].astype(F32)
    row = lax.broadcasted_iota(jnp.int32, (rows, triples), 0)
    left = jnp.where(row == key, weight, 0.0).astype(BF16)
    col = lax.rem(lax.broadcasted_iota(jnp.int32, (cols, triples), 0), modes)
    right = jnp.where(col == col_ref[...], 1.0, 0.0).astype(BF16)
    dense = lax.dot_general(left, right, (((1,), (1,)), ((), ())), preferred_element_type=F32)
    r = lax.broadcasted_iota(jnp.int32, (rows, cols), 0)
    c = lax.broadcasted_iota(jnp.int32, (rows, cols), 1)
    dense = dense + jnp.where(r == lax.rem(c, modes), 1.0, 0.0)
    high = dense.astype(BF16)
    low = (dense - high.astype(F32)).astype(BF16)
    out_ref[...] = jnp.where(c < 2 * modes, high.astype(F32), low.astype(F32)).astype(BF16)

    a = lax.broadcasted_iota(jnp.int32, (LANES, LANES), 0)
    b = lax.broadcasted_iota(jnp.int32, (LANES, LANES), 1)
    step = jnp.bitwise_and(a - b, GY - 1)
    same = (a // GY == b // GY) & ((step == 1) | (step == GY - 1))
    apart = jnp.abs(a - b)
    inner = jnp.where(apart == 0, 4.0, jnp.where(same | (apart == GY), -1.0, 0.0)).astype(BF16)
    outer = jnp.where(apart == LANES - GY, -1.0, 0.0).astype(BF16)
    stencil_ref[0:LANES] = inner
    stencil_ref[LANES : 2 * LANES] = inner
    stencil_ref[2 * LANES : 3 * LANES] = outer
    stencil_ref[3 * LANES :] = outer


def split(x):
    high = x.astype(BF16)
    return high, (x - high.astype(F32)).astype(BF16)


def ratio(a, b):
    return jnp.where(b > 0.0, a / jnp.where(b > 0.0, b, 1.0), 0.0)


def unpack_kernel(next_ref, prev_ref, out_ref):
    lane = lane_iota()
    for i in range(NCOEF):
        for q in range(S // 4):
            after, before = next_ref[i, q], prev_ref[i, q]
            for p in range(4):
                a = after if p == 0 else pltpu.roll(after, LANES - GY * p, 1)
                b = before if p == 3 else pltpu.roll(before, LANES - GY - GY * p, 1)
                out_ref[i * S + q * 4 + p] = jnp.where(lane < LANES // 2, a, b)


def mix(get, ct, slot, coup_ref, vs_ref, mx_ref):
    n = vs_ref.shape[1] // 3
    for t in range(S):
        at = slice(t * LANES, (t + 1) * LANES)
        high, low = split(get(ct, t))
        vs_ref[slot, 0:n, at] = high
        vs_ref[slot, n : 2 * n, at] = low
        vs_ref[slot, 2 * n : 3 * n, at] = high
    mx_ref[slot] = jnp.dot(coup_ref[...], vs_ref[slot], preferred_element_type=F32)


def spread(get, ct, slot, every, stencil_ref, xs_ref, bs_ref):
    n = bs_ref.shape[1] // S
    wide = lax.broadcasted_iota(jnp.int32, (n, LANES), 1) < LANES // 2
    before, after = (ct - 1) % every, (ct + 1) % every
    for t in range(S):
        to = slice(t * n, (t + 1) * n)
        high, low = split(get(ct, t))
        xs_ref[slot, to, 0:LANES] = high
        xs_ref[slot, to, LANES : 2 * LANES] = low
        high, low = split(jnp.where(wide, get(after, t), get(before, t)))
        xs_ref[slot, to, 2 * LANES : 3 * LANES] = high
        xs_ref[slot, to, 3 * LANES :] = low
    bs_ref[slot] = jnp.dot(xs_ref[slot], stencil_ref[...], preferred_element_type=F32)


def react(n, jac, slot, mx_ref, finish):
    for kb in range(0, n, 32):
        acc = [None] * 32
        for i in range(NCOEF):
            for t in range(S):
                m = [
                    mx_ref[slot, i * n + kb + kt * 8 : i * n + kb + kt * 8 + 8, t * LANES : (t + 1) * LANES]
                    for kt in range(4)
                ]
                for s in range(S):
                    j = jnp.broadcast_to(jac(i * S + s, t), (8, LANES))
                    for kt in range(4):
                        term = j * m[kt]
                        at = s * 4 + kt
                        acc[at] = term if acc[at] is None else acc[at] + term
        for s in range(S):
            for kt in range(4):
                finish(s, kb + kt * 8, acc[s * 4 + kt])


def tile_of(jac_ref, ct):
    return lambda row, t: jac_ref[row, t : t + 1, ct * LANES : (ct + 1) * LANES]


class Sums:
    def __init__(self):
        self.parts = {}

    def add(self, name, at, term):
        mine = self.parts.setdefault(name, {})
        mine[at % 4] = mine[at % 4] + term if at % 4 in mine else term

    def total(self, name):
        x = functools.reduce(lambda a, b: a + b, self.parts[name].values())
        return jnp.broadcast_to(jnp.sum(x, axis=(0, 1), keepdims=True), (8, LANES))


def early_kernel(n, plane, place_ref, jac_ref, coup_ref, *refs):
    near_refs, (v_ref, a_ref, gather_ref, vs_ref, mx_ref) = refs[:plane], refs[plane:]
    early = v_ref.shape[0]
    for k in range(plane):
        for q in range(near_refs[k].shape[0]):
            d = jnp.bitwise_xor(place_ref[0], q) * plane + jnp.bitwise_xor(place_ref[1], k)
            gather_ref[d] = near_refs[k][q]
    flat = gather_ref.reshape(n * early * S, LANES)
    for ct in range(early):
        for s in range(S):
            v_ref[ct, s] = flat[pl.ds(ct * S + s, n, stride=early * S), :]

    def get(ct, t):
        return v_ref[ct, t]

    def finisher(ct):
        def finish(s, k, acc):
            a_ref[ct, s, k : k + 8] = acc

        return finish

    mix(get, 0, 0, coup_ref, vs_ref, mx_ref)
    for ct in range(early):
        if ct + 1 < early:
            mix(get, ct + 1, (ct + 1) % 2, coup_ref, vs_ref, mx_ref)
        react(n, tile_of(jac_ref, ct), ct % 2, mx_ref, finisher(ct))


def first_kernel(n, tiles, place_ref, dif_ref, r_ref, ve_ref, ae_ref, jac_ref, coup_ref, stencil_ref, _, *refs):
    every = tiles + 1
    (v_ref, w_ref, sum_ref), refs = refs[:3], refs[3:]
    send_refs, (vs_ref, xs_ref, mx_ref, bs_ref) = refs[: n // 8], refs[n // 8 :]
    early = ve_ref.shape[0]
    for ct in range(early):
        v_ref[ct] = ve_ref[ct]
    for ct in range(early, every):
        for s in range(S):
            v_ref[ct, s] = r_ref[pl.ds((ct - early) * S + s, n, stride=(every - early) * S), :]
    sums = Sums()

    def get(ct, t):
        return v_ref[ct, t]

    def finisher(ct):
        def finish(s, k, acc):
            w = dif_ref[s] * bs_ref[ct % 2, s * n + k : s * n + k + 8] - acc
            w_ref[ct, s, k : k + 8] = w
            v = v_ref[ct, s, k : k + 8]
            sums.add("rr", k // 8, v * v)
            sums.add("rw", k // 8, v * w)

        return finish

    if early < tiles:
        mix(get, early, early % 2, coup_ref, vs_ref, mx_ref)
    for ct in range(tiles):
        spread(get, ct, ct % 2, every, stencil_ref, xs_ref, bs_ref)
        if early <= ct and ct + 1 < tiles:
            mix(get, ct + 1, (ct + 1) % 2, coup_ref, vs_ref, mx_ref)
        if ct < early:
            for s in range(S):
                for k in range(0, n, 8):
                    finisher(ct)(s, k, ae_ref[ct, s, k : k + 8])
        else:
            react(n, tile_of(jac_ref, ct), ct % 2, mx_ref, finisher(ct))
    for q in range(n // 8):
        at = pl.multiple_of(jnp.bitwise_xor(place_ref[0], q) * 8, 8)
        flat = send_refs[q].reshape(8 * tiles * S, LANES)
        for ct in range(tiles):
            for s in range(S):
                flat[pl.ds(ct * S + s, 8, stride=tiles * S), :] = w_ref[ct, s, pl.ds(at, 8)]
    sum_ref[0:8] = sums.total("rr")
    sum_ref[8:16] = sums.total("rw")


def second_kernel(
    n,
    tiles,
    dif_ref,
    v_ref,
    w_ref,
    sum_ref,
    jac_ref,
    edge_ref,
    coup_ref,
    stencil_ref,
    out_ref,
    z_ref,
    wh_ref,
    vs_ref,
    xs_ref,
    mx_ref,
    bs_ref,
):
    every = tiles + 1
    per = tiles * S + 1
    rr, rw = sum_ref[0:8], sum_ref[8:16]
    c1 = ratio(rw, rr)
    sums = Sums()

    def get_v(ct, t):
        return v_ref[ct, t]

    def get_w(ct, t):
        return w_ref[ct, t] if ct < tiles else wh_ref[t]

    def finish_edge(s, k, acc):
        wh_ref[s, k : k + 8] = dif_ref[s] * bs_ref[tiles % 2, s * n + k : s * n + k + 8] - acc

    def finisher(ct):
        def finish(s, k, acc):
            z = dif_ref[s] * bs_ref[ct % 2, s * n + k : s * n + k + 8] - acc
            v, w = v_ref[ct, s, k : k + 8], w_ref[ct, s, k : k + 8]
            z_ref[ct, s, k : k + 8] = z
            out_ref[pl.ds(k * per + ct * S + s, 8, stride=per), :] = z
            u = w - c1 * v
            sums.add("uu", k // 8, u * u)
            sums.add("ur", k // 8, u * v)
            sums.add("uz", k // 8, u * z)
            sums.add("rz", k // 8, v * z)

        return finish

    slot = tiles % 2
    mix(get_v, tiles, slot, coup_ref, vs_ref, mx_ref)
    spread(get_v, tiles, slot, every, stencil_ref, xs_ref, bs_ref)
    order = list(range(1, tiles)) + [0]
    mix(get_w, order[0], 1 - slot, coup_ref, vs_ref, mx_ref)
    react(n, tile_of(edge_ref, 0), slot, mx_ref, finish_edge)
    for at, ct in enumerate(order):
        now = (1 - slot + at) % 2
        spread(get_w, ct, ct % 2, every, stencil_ref, xs_ref, bs_ref)
        if at + 1 < tiles:
            mix(get_w, order[at + 1], 1 - now, coup_ref, vs_ref, mx_ref)
        react(n, tile_of(jac_ref, ct), now, mx_ref, finisher(ct))
    uu, ur, uz, rz = (sums.total(name) for name in ("uu", "ur", "uz", "rz"))
    c2 = ratio(rz, rr)
    c3 = ratio(uz - c2 * ur, uu)
    for ct in range(tiles):
        for s in range(S):
            for k in range(0, n, 8):
                v, w, z = (ref[ct, s, k : k + 8] for ref in (v_ref, w_ref, z_ref))
                x = (z - c2 * v) - c3 * (w - c1 * v)
                sums.add("xx", k // 8, x * x)
    xx = sums.total("xx")
    lane = lane_iota()
    tile = jnp.zeros((8, LANES), F32)
    for q, value in enumerate((rr, c1, uu, c2, c3, xx)):
        tile = jnp.where(lane == q, value, tile)
    for k in range(0, n, 8):
        out_ref[pl.ds(k * per + tiles * S, 8, stride=per), :] = tile


def relay_kernel(own, place_ref, *refs):
    parts = 8 // own
    count = len(refs) - parts
    for k in range(parts):
        at = jnp.bitwise_xor(place_ref[1], k)
        for q in range(count):
            refs[count + k][q] = refs[q][at]


def combine_kernel(parts, tiles, place_ref, rhs_ref, got_ref, *refs):
    own = rhs_ref.shape[0]
    plane = 8 // own
    w_refs, (update_ref, basis_ref) = refs[:plane], refs[plane:]
    per = tiles * S + 1
    stats = got_ref[pl.ds(tiles * S, parts, stride=own * per), :]

    def stat(q):
        return jnp.broadcast_to(stats[:, q : q + 1], (parts, LANES))

    def add(x):
        return jnp.sum(x, axis=0, keepdims=True)

    rr, c1, uu, c2, c3, xx = (stat(q) for q in range(6))
    all_rr = add(rr)
    g1 = add(rr * c1) / all_rr
    g2 = add(rr * c2) / all_rr
    e1, e2 = c1 - g1, c2 - g2
    all_uu = add(uu + e1 * e1 * rr)
    g3 = add(c3 * uu + e1 * e2 * rr) / all_uu
    e3 = c3 - g3
    f = e2 - g3 * e1
    all_xx = add(xx + e3 * e3 * uu + f * f * rr)
    beta, nu, nx = jnp.sqrt(all_rr), jnp.sqrt(all_uu), jnp.sqrt(all_xx)
    h11 = 1.0 + g1
    h21 = nu / beta
    h12 = (g2 - g1 * g1) * beta / nu
    h22 = 1.0 + (g3 - g1)
    h32 = nx / nu
    m11 = h11 * h11 + h21 * h21
    m12 = h11 * h12 + h21 * h22
    m22 = h12 * h12 + h22 * h22 + h32 * h32
    b1, b2 = beta * h11, beta * h12
    determ = m11 * m22 - m12 * m12
    y1 = (m22 * b1 - m12 * b2) / determ
    y2 = (m11 * b2 - m12 * b1) / determ
    uw = y2 / nu
    ur = y1 / beta - uw * g1
    bz = 1.0 / nx
    bw = -g3 * bz
    br = (g3 * g1 - g2) * bz
    ur, uw, br, bw, bz = (jnp.broadcast_to(x, (S, LANES)) for x in (ur, uw, br, bw, bz))
    for d in range(parts):
        for m in range(own):
            for ct in range(tiles):
                at = slice((d * tiles + ct) * LANES, (d * tiles + ct + 1) * LANES)
                base = (d * own + m) * per + ct * S
                basis_ref[m, :, at] = br * rhs_ref[m, :, at] + bz * got_ref[base : base + S, :]
    for k in range(plane):
        for q in range(parts // plane):
            d = jnp.bitwise_xor(place_ref[0], q) * plane + jnp.bitwise_xor(place_ref[1], k)
            for m in range(own):
                for ct in range(tiles):
                    at = pl.ds(pl.multiple_of(d * (tiles * LANES) + ct * LANES, LANES), LANES)
                    w = w_refs[k][q, m, ct * S : (ct + 1) * S, :]
                    update_ref[m, :, at] = ur * rhs_ref[m, :, at] + uw * w
                    basis_ref[m, :, at] += bw * w


def local(rhs, diffusivity, jac_coef, coef_index, row_mode, col_mode, multiplicity):
    parts = lax.axis_size("modes")
    own, _, total = rhs.shape
    n = own * parts
    cells = total // parts
    tiles = cells // LANES
    plane = 8 // own
    sds = jax.ShapeDtypeStruct
    smem = pl.BlockSpec(memory_space=pltpu.SMEM)
    index = lax.axis_index("modes")
    place = jnp.stack([index // plane, index % plane]).astype(jnp.int32)

    early = (tiles + 1) // 2
    block = (plane, own, early * S, LANES)

    def across(arrays):
        lead, rows = len(arrays), arrays[0].shape[2]
        come = [arrays[0]]
        for q in range(1, lead):
            come.append(lax.ppermute(arrays[q], "modes", [(i, i ^ (q * plane)) for i in range(parts)]))
        relayed = pl.pallas_call(
            functools.partial(relay_kernel, own),
            out_shape=[sds((lead, own, rows, LANES), F32)] * plane,
            in_specs=[smem] + [VMEM] * lead,
            out_specs=[VMEM] * plane,
            compiler_params=PARAMS,
            cost_estimate=pl.CostEstimate(flops=10**11, bytes_accessed=1 << 20, transcendentals=0),
            name="relay",
        )(place, *come)
        out = [relayed[0]]
        for k in range(1, plane):
            out.append(lax.ppermute(relayed[k], "modes", [(i, i ^ k) for i in range(parts)]))
        return out, relayed[0]

    late_send, *early_send = pl.pallas_call(
        functools.partial(arrange_kernel, parts, early),
        out_shape=[sds((n, tiles + 1 - early, S, LANES), F32)] + [sds(block, F32)] * (parts // plane),
        in_specs=[smem, VMEM],
        out_specs=[VMEM] * (1 + parts // plane),
        compiler_params=PARAMS,
        name="arrange",
    )(place, rhs)
    near, relayed = across(early_send)
    vector = lax.all_to_all(late_send, "modes", split_axis=0, concat_axis=0, tiled=True)

    edge = (NCOEF, S, S, LANES)
    head, tail = pl.pallas_call(
        pack_kernel,
        grid=(1,),
        out_shape=[sds((NCOEF, S // 4, S, LANES), F32)] * 2,
        in_specs=[
            pl.BlockSpec(edge, lambda g: (0, 0, 0, 0)),
            pl.BlockSpec(edge, lambda g: (0, 0, 0, tiles - 1)),
            pl.BlockSpec(memory_space=pl.ANY),
        ],
        compiler_params=PARAMS,
        name="pack",
    )(jac_coef, jac_coef, relayed)
    up = [(i, (i + 1) % parts) for i in range(parts)]
    down = [(j, i) for i, j in up]
    after = lax.ppermute(head, "modes", down)
    before = lax.ppermute(tail, "modes", up)
    edges = pl.pallas_call(
        unpack_kernel,
        out_shape=sds((NCOEF * S, S, LANES), F32),
        in_specs=[VMEM] * 2,
        out_specs=VMEM,
        compiler_params=PARAMS,
        name="unpack",
    )(after, before)

    coupling, stencil = pl.pallas_call(
        functools.partial(coupling_kernel, n),
        out_shape=[sds((NCOEF * n, 3 * n), BF16), sds((4 * LANES, LANES), BF16)],
        in_specs=[VMEM] * 4,
        out_specs=[VMEM] * 2,
        compiler_params=PARAMS,
        name="coupling",
    )(*(x.reshape(1, -1) for x in (coef_index, row_mode, col_mode, multiplicity)))

    jac = jac_coef.reshape(NCOEF * S, S, cells)
    field = (tiles + 1, S, n, LANES)
    work = [
        pltpu.VMEM((2, 3 * n, S * LANES), BF16),
        pltpu.VMEM((2, S * n, 4 * LANES), BF16),
        pltpu.VMEM((2, NCOEF * n, S * LANES), F32),
        pltpu.VMEM((2, S * n, LANES), F32),
    ]
    v_early, a_early = pl.pallas_call(
        functools.partial(early_kernel, n, plane),
        out_shape=[sds((early, S, n, LANES), F32)] * 2,
        in_specs=[smem] + [VMEM] * (2 + plane),
        out_specs=[VMEM] * 2,
        scratch_shapes=[pltpu.VMEM((parts, own, early * S, LANES), F32), work[0], work[2]],
        compiler_params=PARAMS,
        name="early",
    )(place, jac, coupling, *near)
    v, w, sums, *w_send = pl.pallas_call(
        functools.partial(first_kernel, n, tiles),
        out_shape=[sds(field, F32), sds((tiles, S, n, LANES), F32), sds((16, LANES), F32)]
        + [sds((plane, own, tiles * S, LANES), F32)] * (n // 8),
        in_specs=[smem] * 2 + [VMEM] * 6 + [pl.BlockSpec(memory_space=pl.ANY)],
        out_specs=[VMEM] * (3 + n // 8),
        scratch_shapes=work,
        compiler_params=PARAMS,
        name="first",
    )(
        place,
        diffusivity,
        vector.reshape(n * (tiles + 1 - early) * S, LANES),
        v_early,
        a_early,
        jac,
        coupling,
        stencil,
        edges,
    )

    w_own, _ = across(w_send)

    z_send = pl.pallas_call(
        functools.partial(second_kernel, n, tiles),
        out_shape=sds((n * (tiles * S + 1), LANES), F32),
        in_specs=[smem] + [VMEM] * 7,
        out_specs=VMEM,
        scratch_shapes=[pltpu.VMEM((tiles, S, n, LANES), F32), pltpu.VMEM((S, n, LANES), F32)] + work,
        compiler_params=PARAMS,
        cost_estimate=pl.CostEstimate(flops=2 * NCOEF * S * n * n * cells, bytes_accessed=16 << 20, transcendentals=0),
        name="second",
    )(diffusivity, v, w, sums, jac, edges, coupling, stencil)
    line = (tiles * S + 1) * LANES
    got = lax.all_to_all(z_send.reshape(n, 1, line), "modes", split_axis=0, concat_axis=0, tiled=True)

    update, basis_next = pl.pallas_call(
        functools.partial(combine_kernel, parts, tiles),
        out_shape=[sds(rhs.shape, F32)] * 2,
        in_specs=[smem] + [VMEM] * (2 + plane),
        out_specs=[VMEM] * 2,
        compiler_params=PARAMS,
        name="combine",
    )(place, rhs, got.reshape(n * (tiles * S + 1), LANES), *w_own)
    return (update, basis_next)


def solution(mesh):
    return jax.shard_map(
        local,
        mesh=mesh,
        in_specs=(
            P(("groups", "modes"), None, None),
            P(),
            P(None, None, None, "modes"),
            P(),
            P(),
            P(),
            P(),
        ),
        out_specs=(P(("groups", "modes"), None, None), P(("groups", "modes"), None, None)),
        check_vma=False,
    )
```

```python
import functools

import jax
import jax.numpy as jnp
from jax import lax
from jax.experimental import pallas as pl
from jax.experimental.pallas import tpu as pltpu
from jax.sharding import PartitionSpec as P

NCOEF = 9
GY = 32
S = 8
LANES = 128
F32 = jnp.float32
BF16 = jnp.bfloat16
VMEM = pl.BlockSpec(memory_space=pltpu.VMEM)
PARAMS = pltpu.CompilerParams(vmem_limit_bytes=40 * 1024 * 1024)


def lane_iota():
    return lax.broadcasted_iota(jnp.int32, (S, LANES), 1)


def arrange_kernel(parts, early, place_ref, rhs_ref, out_ref, *refs):
    own, _, total = rhs_ref.shape
    cells = total // parts
    tiles = cells // LANES
    plane = 8 // own
    low = lane_iota() < LANES // 2
    for q in range(parts // plane):
        base = jnp.bitwise_xor(place_ref[0], q) * plane
        for k in range(plane):
            for m in range(own):
                for ct in range(early):
                    at = pl.multiple_of((base + k) * cells + ct * LANES, LANES)
                    refs[q][k, m, ct * S : (ct + 1) * S, :] = rhs_ref[m, :, pl.ds(at, LANES)]
    for d in range(parts):
        after = ((d + 1) * cells) % total
        before = (d * cells - LANES) % total
        for m in range(own):
            for ct in range(early, tiles):
                at = d * cells + ct * LANES
                out_ref[d * own + m, ct - early] = rhs_ref[m, :, at : at + LANES]
            out_ref[d * own + m, tiles - early] = jnp.where(
                low, rhs_ref[m, :, after : after + LANES], rhs_ref[m, :, before : before + LANES]
            )


def pack_kernel(first_ref, last_ref, _, head_ref, tail_ref):
    piece = lane_iota() // GY
    for i in range(NCOEF):
        for q in range(S // 4):
            head = first_ref[i, q * 4]
            tail = pltpu.roll(last_ref[i, q * 4], GY, 1)
            for p in range(1, 4):
                head = jnp.where(piece == p, pltpu.roll(first_ref[i, q * 4 + p], GY * p, 1), head)
                moved = last_ref[i, q * 4 + p]
                if p < 3:
                    moved = pltpu.roll(moved, GY * (p + 1), 1)
                tail = jnp.where(piece == p, moved, tail)
            head_ref[i, q] = head
            tail_ref[i, q] = tail


def coupling_kernel(modes, coef_ref, row_ref, col_ref, mult_ref, out_ref, stencil_ref):
    rows, cols = out_ref.shape
    triples = coef_ref.shape[1]
    key = coef_ref[...] * modes + row_ref[...]
    weight = 0.25 * mult_ref[...].astype(F32)
    row = lax.broadcasted_iota(jnp.int32, (rows, triples), 0)
    left = jnp.where(row == key, weight, 0.0).astype(BF16)
    col = lax.rem(lax.broadcasted_iota(jnp.int32, (cols, triples), 0), modes)
    right = jnp.where(col == col_ref[...], 1.0, 0.0).astype(BF16)
    dense = lax.dot_general(left, right, (((1,), (1,)), ((), ())), preferred_element_type=F32)
    r = lax.broadcasted_iota(jnp.int32, (rows, cols), 0)
    c = lax.broadcasted_iota(jnp.int32, (rows, cols), 1)
    dense = dense + jnp.where(r == lax.rem(c, modes), 1.0, 0.0)
    high = dense.astype(BF16)
    low = (dense - high.astype(F32)).astype(BF16)
    out_ref[...] = jnp.where(c < 2 * modes, high.astype(F32), low.astype(F32)).astype(BF16)

    a = lax.broadcasted_iota(jnp.int32, (LANES, LANES), 0)
    b = lax.broadcasted_iota(jnp.int32, (LANES, LANES), 1)
    step = jnp.bitwise_and(a - b, GY - 1)
    same = (a // GY == b // GY) & ((step == 1) | (step == GY - 1))
    apart = jnp.abs(a - b)
    inner = jnp.where(apart == 0, 4.0, jnp.where(same | (apart == GY), -1.0, 0.0)).astype(BF16)
    outer = jnp.where(apart == LANES - GY, -1.0, 0.0).astype(BF16)
    stencil_ref[0:LANES] = inner
    stencil_ref[LANES : 2 * LANES] = inner
    stencil_ref[2 * LANES : 3 * LANES] = outer
    stencil_ref[3 * LANES :] = outer


def split(x):
    high = x.astype(BF16)
    return high, (x - high.astype(F32)).astype(BF16)


def ratio(a, b):
    return jnp.where(b > 0.0, a / jnp.where(b > 0.0, b, 1.0), 0.0)


def unpack_kernel(next_ref, prev_ref, out_ref):
    lane = lane_iota()
    for i in range(NCOEF):
        for q in range(S // 4):
            after, before = next_ref[i, q], prev_ref[i, q]
            for p in range(4):
                a = after if p == 0 else pltpu.roll(after, LANES - GY * p, 1)
                b = before if p == 3 else pltpu.roll(before, LANES - GY - GY * p, 1)
                out_ref[i * S + q * 4 + p] = jnp.where(lane < LANES // 2, a, b)


def mix(get, ct, slot, coup_ref, vs_ref, mx_ref):
    n = vs_ref.shape[1] // 3

    def step(first):
        for t in (first, first + 1):
            at = slice(t * LANES, (t + 1) * LANES)
            high, low = split(get(ct, t))
            vs_ref[slot, 0:n, at] = high
            vs_ref[slot, n : 2 * n, at] = low
            vs_ref[slot, 2 * n : 3 * n, at] = high
        at = slice(first * LANES, (first + 2) * LANES)
        mx_ref[slot, :, at] = jnp.dot(coup_ref[...], vs_ref[slot, :, at], preferred_element_type=F32)

    return [functools.partial(step, first) for first in range(0, S, 2)]


def spread(get, ct, slot, every, stencil_ref, xs_ref, bs_ref):
    n = bs_ref.shape[1] // S
    before, after = (ct - 1) % every, (ct + 1) % every

    def fill(first):
        wide = lax.broadcasted_iota(jnp.int32, (n, LANES), 1) < LANES // 2
        for t in (first, first + 1):
            to = slice(t * n, (t + 1) * n)
            high, low = split(get(ct, t))
            xs_ref[slot, to, 0:LANES] = high
            xs_ref[slot, to, LANES : 2 * LANES] = low
            high, low = split(jnp.where(wide, get(after, t), get(before, t)))
            xs_ref[slot, to, 2 * LANES : 3 * LANES] = high
            xs_ref[slot, to, 3 * LANES :] = low
        if first + 2 == S:
            bs_ref[slot] = jnp.dot(xs_ref[slot], stencil_ref[...], preferred_element_type=F32)

    return [functools.partial(fill, first) for first in range(0, S, 2)]


def run(steps):
    for step in steps:
        step()


def react(n, jac, slot, mx_ref, finish, steps=()):
    steps = list(steps)
    for kb in range(0, n, 32):
        acc = [None] * 32
        for i in range(NCOEF):
            if steps:
                steps.pop(0)()
            for t in range(S):
                m = [
                    mx_ref[slot, i * n + kb + kt * 8 : i * n + kb + kt * 8 + 8, t * LANES : (t + 1) * LANES]
                    for kt in range(4)
                ]
                for s in range(S):
                    j = jnp.broadcast_to(jac(i * S + s, t), (8, LANES))
                    for kt in range(4):
                        term = j * m[kt]
                        at = s * 4 + kt
                        acc[at] = term if acc[at] is None else acc[at] + term
        for s in range(S):
            for kt in range(4):
                finish(s, kb + kt * 8, acc[s * 4 + kt])
    run(steps)


def tile_of(jac_ref, ct):
    return lambda row, t: jac_ref[row, t : t + 1, ct * LANES : (ct + 1) * LANES]


class Sums:
    def __init__(self):
        self.parts = {}

    def add(self, name, at, term):
        mine = self.parts.setdefault(name, {})
        mine[at % 4] = mine[at % 4] + term if at % 4 in mine else term

    def total(self, name):
        x = functools.reduce(lambda a, b: a + b, self.parts[name].values())
        return jnp.broadcast_to(jnp.sum(x, axis=(0, 1), keepdims=True), (8, LANES))


def early_kernel(n, plane, place_ref, jac_ref, coup_ref, *refs):
    near_refs, (v_ref, a_ref, gather_ref, vs_ref, mx_ref) = refs[:plane], refs[plane:]
    early = v_ref.shape[0]
    for k in range(plane):
        for q in range(near_refs[k].shape[0]):
            d = jnp.bitwise_xor(place_ref[0], q) * plane + jnp.bitwise_xor(place_ref[1], k)
            gather_ref[d] = near_refs[k][q]
    flat = gather_ref.reshape(n * early * S, LANES)
    for ct in range(early):
        for s in range(S):
            v_ref[ct, s] = flat[pl.ds(ct * S + s, n, stride=early * S), :]

    def get(ct, t):
        return v_ref[ct, t]

    def finisher(ct):
        def finish(s, k, acc):
            a_ref[ct, s, k : k + 8] = acc

        return finish

    run(mix(get, 0, 0, coup_ref, vs_ref, mx_ref))
    for ct in range(early):
        steps = mix(get, ct + 1, (ct + 1) % 2, coup_ref, vs_ref, mx_ref) if ct + 1 < early else []
        react(n, tile_of(jac_ref, ct), ct % 2, mx_ref, finisher(ct), steps)


def first_kernel(n, tiles, place_ref, dif_ref, r_ref, ve_ref, ae_ref, jac_ref, coup_ref, stencil_ref, _, *refs):
    every = tiles + 1
    (v_ref, w_ref, sum_ref), refs = refs[:3], refs[3:]
    send_refs, (vs_ref, xs_ref, mx_ref, bs_ref) = refs[: n // 8], refs[n // 8 :]
    early = ve_ref.shape[0]
    for ct in range(early):
        v_ref[ct] = ve_ref[ct]
    for ct in range(early, every):
        for s in range(S):
            v_ref[ct, s] = r_ref[pl.ds((ct - early) * S + s, n, stride=(every - early) * S), :]
    sums = Sums()

    def get(ct, t):
        return v_ref[ct, t]

    def finisher(ct, slot):
        def finish(s, k, acc):
            w = dif_ref[s] * bs_ref[slot, s * n + k : s * n + k + 8] - acc
            w_ref[ct, s, k : k + 8] = w
            v = v_ref[ct, s, k : k + 8]
            sums.add("rr", k // 8, v * v)
            sums.add("rw", k // 8, v * w)

        return finish

    def prepare(ct):
        return mix(get, ct, ct % 2, coup_ref, vs_ref, mx_ref) + sides(ct, ct % 2)

    def sides(ct, slot):
        return spread(get, ct, slot, every, stencil_ref, xs_ref, bs_ref)

    def close(ct, slot):
        for s in range(S):
            for k in range(0, n, 8):
                finisher(ct, slot)(s, k, ae_ref[ct, s, k : k + 8])

    spare = tiles % 2
    rest = []
    for ct in range(early):
        rest += sides(ct, spare) + [functools.partial(close, ct, spare)]
    if early < tiles:
        run(prepare(early))
    for ct in range(early, tiles):
        steps = prepare(ct + 1) if ct + 1 < tiles else rest
        react(n, tile_of(jac_ref, ct), ct % 2, mx_ref, finisher(ct, ct % 2), steps)
    if early == tiles:
        run(rest)
    for q in range(n // 8):
        at = pl.multiple_of(jnp.bitwise_xor(place_ref[0], q) * 8, 8)
        flat = send_refs[q].reshape(8 * tiles * S, LANES)
        for ct in range(tiles):
            for s in range(S):
                flat[pl.ds(ct * S + s, 8, stride=tiles * S), :] = w_ref[ct, s, pl.ds(at, 8)]
    sum_ref[0:8] = sums.total("rr")
    sum_ref[8:16] = sums.total("rw")


def second_kernel(
    n,
    tiles,
    dif_ref,
    v_ref,
    w_ref,
    sum_ref,
    jac_ref,
    edge_ref,
    coup_ref,
    stencil_ref,
    out_ref,
    z_ref,
    wh_ref,
    vs_ref,
    xs_ref,
    mx_ref,
    bs_ref,
):
    every = tiles + 1
    per = tiles * S + 1
    rr, rw = sum_ref[0:8], sum_ref[8:16]
    c1 = ratio(rw, rr)
    sums = Sums()

    def get_v(ct, t):
        return v_ref[ct, t]

    def get_w(ct, t):
        return w_ref[ct, t] if ct < tiles else wh_ref[t]

    def finish_edge(s, k, acc):
        wh_ref[s, k : k + 8] = dif_ref[s] * bs_ref[0, s * n + k : s * n + k + 8] - acc

    def finisher(ct, slot):
        def finish(s, k, acc):
            z = dif_ref[s] * bs_ref[slot, s * n + k : s * n + k + 8] - acc
            v, w = v_ref[ct, s, k : k + 8], w_ref[ct, s, k : k + 8]
            z_ref[ct, s, k : k + 8] = z
            out_ref[pl.ds(k * per + ct * S + s, 8, stride=per), :] = z
            u = w - c1 * v
            sums.add("uu", k // 8, u * u)
            sums.add("ur", k // 8, u * v)
            sums.add("uz", k // 8, u * z)
            sums.add("rz", k // 8, v * z)

        return finish

    order = list(range(1, tiles)) + [0]

    def mixed(get, ct, slot):
        return mix(get, ct, slot, coup_ref, vs_ref, mx_ref)

    def sides(get, ct, slot):
        return spread(get, ct, slot, every, stencil_ref, xs_ref, bs_ref)

    run(mixed(get_v, tiles, 0) + sides(get_v, tiles, 0))
    inside = tiles > 2
    steps = mixed(get_w, order[0], 1) + (sides(get_w, order[0], 1) if inside else [])
    react(n, tile_of(edge_ref, 0), 0, mx_ref, finish_edge, steps)
    if not inside:
        run(sides(get_w, order[0], 1))
    for at, ct in enumerate(order):
        slot = (at + 1) % 2
        steps = []
        if at + 1 < tiles:
            steps = mixed(get_w, order[at + 1], 1 - slot) + sides(get_w, order[at + 1], 1 - slot)
        react(n, tile_of(jac_ref, ct), slot, mx_ref, finisher(ct, slot), steps)
    uu, ur, uz, rz = (sums.total(name) for name in ("uu", "ur", "uz", "rz"))
    c2 = ratio(rz, rr)
    c3 = ratio(uz - c2 * ur, uu)
    for ct in range(tiles):
        for s in range(S):
            for k in range(0, n, 8):
                v, w, z = (ref[ct, s, k : k + 8] for ref in (v_ref, w_ref, z_ref))
                x = (z - c2 * v) - c3 * (w - c1 * v)
                sums.add("xx", k // 8, x * x)
    xx = sums.total("xx")
    lane = lane_iota()
    tile = jnp.zeros((8, LANES), F32)
    for q, value in enumerate((rr, c1, uu, c2, c3, xx)):
        tile = jnp.where(lane == q, value, tile)
    for k in range(0, n, 8):
        out_ref[pl.ds(k * per + tiles * S, 8, stride=per), :] = tile


def relay_kernel(own, place_ref, *refs):
    parts = 8 // own
    count = len(refs) - parts
    for k in range(parts):
        at = jnp.bitwise_xor(place_ref[1], k)
        for q in range(count):
            refs[count + k][q] = refs[q][at]


def combine_kernel(parts, tiles, place_ref, rhs_ref, got_ref, *refs):
    own = rhs_ref.shape[0]
    plane = 8 // own
    w_refs, (update_ref, basis_ref) = refs[:plane], refs[plane:]
    per = tiles * S + 1
    stats = got_ref[pl.ds(tiles * S, parts, stride=own * per), :]

    def stat(q):
        return jnp.broadcast_to(stats[:, q : q + 1], (parts, LANES))

    def add(x):
        return jnp.sum(x, axis=0, keepdims=True)

    rr, c1, uu, c2, c3, xx = (stat(q) for q in range(6))
    all_rr = add(rr)
    g1 = add(rr * c1) / all_rr
    g2 = add(rr * c2) / all_rr
    e1, e2 = c1 - g1, c2 - g2
    all_uu = add(uu + e1 * e1 * rr)
    g3 = add(c3 * uu + e1 * e2 * rr) / all_uu
    e3 = c3 - g3
    f = e2 - g3 * e1
    all_xx = add(xx + e3 * e3 * uu + f * f * rr)
    beta, nu, nx = jnp.sqrt(all_rr), jnp.sqrt(all_uu), jnp.sqrt(all_xx)
    h11 = 1.0 + g1
    h21 = nu / beta
    h12 = (g2 - g1 * g1) * beta / nu
    h22 = 1.0 + (g3 - g1)
    h32 = nx / nu
    m11 = h11 * h11 + h21 * h21
    m12 = h11 * h12 + h21 * h22
    m22 = h12 * h12 + h22 * h22 + h32 * h32
    b1, b2 = beta * h11, beta * h12
    determ = m11 * m22 - m12 * m12
    y1 = (m22 * b1 - m12 * b2) / determ
    y2 = (m11 * b2 - m12 * b1) / determ
    uw = y2 / nu
    ur = y1 / beta - uw * g1
    bz = 1.0 / nx
    bw = -g3 * bz
    br = (g3 * g1 - g2) * bz
    ur, uw, br, bw, bz = (jnp.broadcast_to(x, (S, LANES)) for x in (ur, uw, br, bw, bz))
    for d in range(parts):
        for m in range(own):
            for ct in range(tiles):
                at = slice((d * tiles + ct) * LANES, (d * tiles + ct + 1) * LANES)
                base = (d * own + m) * per + ct * S
                basis_ref[m, :, at] = br * rhs_ref[m, :, at] + bz * got_ref[base : base + S, :]
    for k in range(plane):
        for q in range(parts // plane):
            d = jnp.bitwise_xor(place_ref[0], q) * plane + jnp.bitwise_xor(place_ref[1], k)
            for m in range(own):
                for ct in range(tiles):
                    at = pl.ds(pl.multiple_of(d * (tiles * LANES) + ct * LANES, LANES), LANES)
                    w = w_refs[k][q, m, ct * S : (ct + 1) * S, :]
                    update_ref[m, :, at] = ur * rhs_ref[m, :, at] + uw * w
                    basis_ref[m, :, at] += bw * w


def local(rhs, diffusivity, jac_coef, coef_index, row_mode, col_mode, multiplicity):
    parts = lax.axis_size("modes")
    own, _, total = rhs.shape
    n = own * parts
    cells = total // parts
    tiles = cells // LANES
    plane = 8 // own
    sds = jax.ShapeDtypeStruct
    smem = pl.BlockSpec(memory_space=pltpu.SMEM)
    index = lax.axis_index("modes")
    place = jnp.stack([index // plane, index % plane]).astype(jnp.int32)

    early = (tiles + 1) // 2
    block = (plane, own, early * S, LANES)

    def across(arrays):
        lead, rows = len(arrays), arrays[0].shape[2]
        come = [arrays[0]]
        for q in range(1, lead):
            come.append(lax.ppermute(arrays[q], "modes", [(i, i ^ (q * plane)) for i in range(parts)]))
        relayed = pl.pallas_call(
            functools.partial(relay_kernel, own),
            out_shape=[sds((lead, own, rows, LANES), F32)] * plane,
            in_specs=[smem] + [VMEM] * lead,
            out_specs=[VMEM] * plane,
            compiler_params=PARAMS,
            cost_estimate=pl.CostEstimate(flops=10**11, bytes_accessed=1 << 20, transcendentals=0),
            name="relay",
        )(place, *come)
        out = [relayed[0]]
        for k in range(1, plane):
            out.append(lax.ppermute(relayed[k], "modes", [(i, i ^ k) for i in range(parts)]))
        return out, relayed[0]

    late_send, *early_send = pl.pallas_call(
        functools.partial(arrange_kernel, parts, early),
        out_shape=[sds((n, tiles + 1 - early, S, LANES), F32)] + [sds(block, F32)] * (parts // plane),
        in_specs=[smem, VMEM],
        out_specs=[VMEM] * (1 + parts // plane),
        compiler_params=PARAMS,
        name="arrange",
    )(place, rhs)
    near, relayed = across(early_send)
    vector = lax.all_to_all(late_send, "modes", split_axis=0, concat_axis=0, tiled=True)

    edge = (NCOEF, S, S, LANES)
    head, tail = pl.pallas_call(
        pack_kernel,
        grid=(1,),
        out_shape=[sds((NCOEF, S // 4, S, LANES), F32)] * 2,
        in_specs=[
            pl.BlockSpec(edge, lambda g: (0, 0, 0, 0)),
            pl.BlockSpec(edge, lambda g: (0, 0, 0, tiles - 1)),
            pl.BlockSpec(memory_space=pl.ANY),
        ],
        compiler_params=PARAMS,
        name="pack",
    )(jac_coef, jac_coef, relayed)
    up = [(i, (i + 1) % parts) for i in range(parts)]
    down = [(j, i) for i, j in up]
    after = lax.ppermute(head, "modes", down)
    before = lax.ppermute(tail, "modes", up)
    edges = pl.pallas_call(
        unpack_kernel,
        out_shape=sds((NCOEF * S, S, LANES), F32),
        in_specs=[VMEM] * 2,
        out_specs=VMEM,
        compiler_params=PARAMS,
        name="unpack",
    )(after, before)

    coupling, stencil = pl.pallas_call(
        functools.partial(coupling_kernel, n),
        out_shape=[sds((NCOEF * n, 3 * n), BF16), sds((4 * LANES, LANES), BF16)],
        in_specs=[VMEM] * 4,
        out_specs=[VMEM] * 2,
        compiler_params=PARAMS,
        name="coupling",
    )(*(x.reshape(1, -1) for x in (coef_index, row_mode, col_mode, multiplicity)))

    jac = jac_coef.reshape(NCOEF * S, S, cells)
    field = (tiles + 1, S, n, LANES)
    work = [
        pltpu.VMEM((2, 3 * n, S * LANES), BF16),
        pltpu.VMEM((2, S * n, 4 * LANES), BF16),
        pltpu.VMEM((2, NCOEF * n, S * LANES), F32),
        pltpu.VMEM((2, S * n, LANES), F32),
    ]
    v_early, a_early = pl.pallas_call(
        functools.partial(early_kernel, n, plane),
        out_shape=[sds((early, S, n, LANES), F32)] * 2,
        in_specs=[smem] + [VMEM] * (2 + plane),
        out_specs=[VMEM] * 2,
        scratch_shapes=[pltpu.VMEM((parts, own, early * S, LANES), F32), work[0], work[2]],
        compiler_params=PARAMS,
        cost_estimate=pl.CostEstimate(flops=2 * 10**9, bytes_accessed=1 << 20, transcendentals=0),
        name="early",
    )(place, jac, coupling, *near)
    v, w, sums, *w_send = pl.pallas_call(
        functools.partial(first_kernel, n, tiles),
        out_shape=[sds(field, F32), sds((tiles, S, n, LANES), F32), sds((16, LANES), F32)]
        + [sds((plane, own, tiles * S, LANES), F32)] * (n // 8),
        in_specs=[smem] * 2 + [VMEM] * 6 + [pl.BlockSpec(memory_space=pl.ANY)],
        out_specs=[VMEM] * (3 + n // 8),
        scratch_shapes=work,
        compiler_params=PARAMS,
        name="first",
    )(
        place,
        diffusivity,
        vector.reshape(n * (tiles + 1 - early) * S, LANES),
        v_early,
        a_early,
        jac,
        coupling,
        stencil,
        edges,
    )

    w_own, _ = across(w_send)

    z_send = pl.pallas_call(
        functools.partial(second_kernel, n, tiles),
        out_shape=sds((n * (tiles * S + 1), LANES), F32),
        in_specs=[smem] + [VMEM] * 7,
        out_specs=VMEM,
        scratch_shapes=[pltpu.VMEM((tiles, S, n, LANES), F32), pltpu.VMEM((S, n, LANES), F32)] + work,
        compiler_params=PARAMS,
        cost_estimate=pl.CostEstimate(flops=2 * NCOEF * S * n * n * cells, bytes_accessed=16 << 20, transcendentals=0),
        name="second",
    )(diffusivity, v, w, sums, jac, edges, coupling, stencil)
    line = (tiles * S + 1) * LANES
    got = lax.all_to_all(z_send.reshape(n, 1, line), "modes", split_axis=0, concat_axis=0, tiled=True)

    update, basis_next = pl.pallas_call(
        functools.partial(combine_kernel, parts, tiles),
        out_shape=[sds(rhs.shape, F32)] * 2,
        in_specs=[smem] + [VMEM] * (2 + plane),
        out_specs=[VMEM] * 2,
        compiler_params=PARAMS,
        name="combine",
    )(place, rhs, got.reshape(n * (tiles * S + 1), LANES), *w_own)
    return (update, basis_next)


def solution(mesh):
    return jax.shard_map(
        local,
        mesh=mesh,
        in_specs=(
            P(("groups", "modes"), None, None),
            P(),
            P(None, None, None, "modes"),
            P(),
            P(),
            P(),
            P(),
        ),
        out_specs=(P(("groups", "modes"), None, None), P(("groups", "modes"), None, None)),
        check_vma=False,
    )
```

```python
import functools

import jax
import jax.numpy as jnp
from jax import lax
from jax.experimental import pallas as pl
from jax.experimental.pallas import tpu as pltpu
from jax.sharding import PartitionSpec as P

NCOEF = 9
GY = 32
S = 8
LANES = 128
GROUP = 16
F32 = jnp.float32
BF16 = jnp.bfloat16
VMEM = pl.BlockSpec(memory_space=pltpu.VMEM)
PARAMS = pltpu.CompilerParams(vmem_limit_bytes=40 * 1024 * 1024)


def lane_iota():
    return lax.broadcasted_iota(jnp.int32, (S, LANES), 1)


def arrange_kernel(parts, early, place_ref, rhs_ref, out_ref, *refs):
    own, _, total = rhs_ref.shape
    cells = total // parts
    tiles = cells // LANES
    plane = GROUP // own
    low = lane_iota() < LANES // 2
    for q in range(parts // plane):
        base = jnp.bitwise_xor(place_ref[0], q) * plane
        for k in range(plane):
            for m in range(own):
                for ct in range(early):
                    at = pl.multiple_of((base + k) * cells + ct * LANES, LANES)
                    refs[q][k, m, ct * S : (ct + 1) * S, :] = rhs_ref[m, :, pl.ds(at, LANES)]
    for d in range(parts):
        after = ((d + 1) * cells) % total
        before = (d * cells - LANES) % total
        for m in range(own):
            for ct in range(early, tiles):
                at = d * cells + ct * LANES
                out_ref[d * own + m, ct - early] = rhs_ref[m, :, at : at + LANES]
            out_ref[d * own + m, tiles - early] = jnp.where(
                low, rhs_ref[m, :, after : after + LANES], rhs_ref[m, :, before : before + LANES]
            )


def pack_kernel(first_ref, last_ref, _, head_ref, tail_ref):
    piece = lane_iota() // GY
    for i in range(NCOEF):
        for q in range(S // 4):
            head = first_ref[i, q * 4]
            tail = pltpu.roll(last_ref[i, q * 4], GY, 1)
            for p in range(1, 4):
                head = jnp.where(piece == p, pltpu.roll(first_ref[i, q * 4 + p], GY * p, 1), head)
                moved = last_ref[i, q * 4 + p]
                if p < 3:
                    moved = pltpu.roll(moved, GY * (p + 1), 1)
                tail = jnp.where(piece == p, moved, tail)
            head_ref[i, q] = head
            tail_ref[i, q] = tail


def coupling_kernel(modes, coef_ref, row_ref, col_ref, mult_ref, out_ref, stencil_ref):
    rows, cols = out_ref.shape
    triples = coef_ref.shape[1]
    key = coef_ref[...] * modes + row_ref[...]
    weight = 0.25 * mult_ref[...].astype(F32)
    row = lax.broadcasted_iota(jnp.int32, (rows, triples), 0)
    left = jnp.where(row == key, weight, 0.0).astype(BF16)
    col = lax.rem(lax.broadcasted_iota(jnp.int32, (cols, triples), 0), modes)
    right = jnp.where(col == col_ref[...], 1.0, 0.0).astype(BF16)
    dense = lax.dot_general(left, right, (((1,), (1,)), ((), ())), preferred_element_type=F32)
    r = lax.broadcasted_iota(jnp.int32, (rows, cols), 0)
    c = lax.broadcasted_iota(jnp.int32, (rows, cols), 1)
    dense = dense + jnp.where(r == lax.rem(c, modes), 1.0, 0.0)
    high = dense.astype(BF16)
    low = (dense - high.astype(F32)).astype(BF16)
    out_ref[...] = jnp.where(c < 2 * modes, high.astype(F32), low.astype(F32)).astype(BF16)

    a = lax.broadcasted_iota(jnp.int32, (LANES, LANES), 0)
    b = lax.broadcasted_iota(jnp.int32, (LANES, LANES), 1)
    step = jnp.bitwise_and(a - b, GY - 1)
    same = (a // GY == b // GY) & ((step == 1) | (step == GY - 1))
    apart = jnp.abs(a - b)
    inner = jnp.where(apart == 0, 4.0, jnp.where(same | (apart == GY), -1.0, 0.0)).astype(BF16)
    outer = jnp.where(apart == LANES - GY, -1.0, 0.0).astype(BF16)
    stencil_ref[0:LANES] = inner
    stencil_ref[LANES : 2 * LANES] = inner
    stencil_ref[2 * LANES : 3 * LANES] = outer
    stencil_ref[3 * LANES :] = outer


def split(x):
    high = x.astype(BF16)
    return high, (x - high.astype(F32)).astype(BF16)


def ratio(a, b):
    return jnp.where(b > 0.0, a / jnp.where(b > 0.0, b, 1.0), 0.0)


def unpack_kernel(next_ref, prev_ref, out_ref):
    lane = lane_iota()
    for i in range(NCOEF):
        for q in range(S // 4):
            after, before = next_ref[i, q], prev_ref[i, q]
            for p in range(4):
                a = after if p == 0 else pltpu.roll(after, LANES - GY * p, 1)
                b = before if p == 3 else pltpu.roll(before, LANES - GY - GY * p, 1)
                out_ref[i * S + q * 4 + p] = jnp.where(lane < LANES // 2, a, b)


def mix(get, ct, slot, coup_ref, vs_ref, mx_ref):
    n = vs_ref.shape[1] // 3

    def step(first):
        for t in (first, first + 1):
            at = slice(t * LANES, (t + 1) * LANES)
            high, low = split(get(ct, t))
            vs_ref[slot, 0:n, at] = high
            vs_ref[slot, n : 2 * n, at] = low
            vs_ref[slot, 2 * n : 3 * n, at] = high
        at = slice(first * LANES, (first + 2) * LANES)
        mx_ref[slot, :, at] = jnp.dot(coup_ref[...], vs_ref[slot, :, at], preferred_element_type=F32)

    return [functools.partial(step, first) for first in range(0, S, 2)]


def spread(get, ct, slot, every, stencil_ref, xs_ref, bs_ref):
    n = bs_ref.shape[1] // S
    before, after = (ct - 1) % every, (ct + 1) % every

    def fill(first):
        wide = lax.broadcasted_iota(jnp.int32, (n, LANES), 1) < LANES // 2
        for t in (first, first + 1):
            to = slice(t * n, (t + 1) * n)
            high, low = split(get(ct, t))
            xs_ref[slot, to, 0:LANES] = high
            xs_ref[slot, to, LANES : 2 * LANES] = low
            high, low = split(jnp.where(wide, get(after, t), get(before, t)))
            xs_ref[slot, to, 2 * LANES : 3 * LANES] = high
            xs_ref[slot, to, 3 * LANES :] = low
        if first + 2 == S:
            bs_ref[slot] = jnp.dot(xs_ref[slot], stencil_ref[...], preferred_element_type=F32)

    return [functools.partial(fill, first) for first in range(0, S, 2)]


def run(steps):
    for step in steps:
        step()


def react(n, jac, slot, mx_ref, finish, steps=()):
    steps = list(steps)
    for kb in range(0, n, 32):
        acc = [None] * 32
        for i in range(NCOEF):
            if steps:
                steps.pop(0)()
            for t in range(S):
                m = [
                    mx_ref[slot, i * n + kb + kt * 8 : i * n + kb + kt * 8 + 8, t * LANES : (t + 1) * LANES]
                    for kt in range(4)
                ]
                for s in range(S):
                    j = jnp.broadcast_to(jac(i * S + s, t), (8, LANES))
                    for kt in range(4):
                        term = j * m[kt]
                        at = s * 4 + kt
                        acc[at] = term if acc[at] is None else acc[at] + term
        for s in range(S):
            for kt in range(4):
                finish(s, kb + kt * 8, acc[s * 4 + kt])
    run(steps)


def tile_of(jac_ref, ct):
    return lambda row, t: jac_ref[row, t : t + 1, ct * LANES : (ct + 1) * LANES]


class Sums:
    def __init__(self):
        self.parts = {}

    def add(self, name, at, term):
        mine = self.parts.setdefault(name, {})
        mine[at % 4] = mine[at % 4] + term if at % 4 in mine else term

    def total(self, name):
        x = functools.reduce(lambda a, b: a + b, self.parts[name].values())
        return jnp.broadcast_to(jnp.sum(x, axis=(0, 1), keepdims=True), (8, LANES))


def early_kernel(n, plane, place_ref, jac_ref, coup_ref, *refs):
    near_refs, (v_ref, a_ref, gather_ref, vs_ref, mx_ref) = refs[:plane], refs[plane:]
    early = v_ref.shape[0]
    gather_kernel(place_ref, *near_refs, gather_ref)
    flat = gather_ref.reshape(n * early * S, LANES)
    for ct in range(early):
        for s in range(S):
            v_ref[ct, s] = flat[pl.ds(ct * S + s, n, stride=early * S), :]

    def get(ct, t):
        return v_ref[ct, t]

    def finisher(ct):
        def finish(s, k, acc):
            a_ref[ct, s, k : k + 8] = acc

        return finish

    run(mix(get, 0, 0, coup_ref, vs_ref, mx_ref))
    for ct in range(early):
        steps = mix(get, ct + 1, (ct + 1) % 2, coup_ref, vs_ref, mx_ref) if ct + 1 < early else []
        react(n, tile_of(jac_ref, ct), ct % 2, mx_ref, finisher(ct), steps)


def first_kernel(n, tiles, place_ref, dif_ref, r_ref, ve_ref, ae_ref, jac_ref, coup_ref, stencil_ref, _, *refs):
    every = tiles + 1
    (v_ref, w_ref, sum_ref), refs = refs[:3], refs[3:]
    send_refs, (vs_ref, xs_ref, mx_ref, bs_ref) = refs[: n // GROUP], refs[n // GROUP :]
    early = ve_ref.shape[0]
    for ct in range(early):
        v_ref[ct] = ve_ref[ct]
    for ct in range(early, every):
        for s in range(S):
            v_ref[ct, s] = r_ref[pl.ds((ct - early) * S + s, n, stride=(every - early) * S), :]
    sums = Sums()

    def get(ct, t):
        return v_ref[ct, t]

    def finisher(ct, slot):
        def finish(s, k, acc):
            w = dif_ref[s] * bs_ref[slot, s * n + k : s * n + k + 8] - acc
            w_ref[ct, s, k : k + 8] = w
            v = v_ref[ct, s, k : k + 8]
            sums.add("rr", k // 8, v * v)
            sums.add("rw", k // 8, v * w)

        return finish

    def prepare(ct):
        return mix(get, ct, ct % 2, coup_ref, vs_ref, mx_ref) + sides(ct, ct % 2)

    def sides(ct, slot):
        return spread(get, ct, slot, every, stencil_ref, xs_ref, bs_ref)

    def close(ct, slot):
        for s in range(S):
            for k in range(0, n, 8):
                finisher(ct, slot)(s, k, ae_ref[ct, s, k : k + 8])

    spare = tiles % 2
    rest = []
    for ct in range(early):
        rest += sides(ct, spare) + [functools.partial(close, ct, spare)]
    if early < tiles:
        run(prepare(early))
    for ct in range(early, tiles):
        steps = prepare(ct + 1) if ct + 1 < tiles else rest
        react(n, tile_of(jac_ref, ct), ct % 2, mx_ref, finisher(ct, ct % 2), steps)
    if early == tiles:
        run(rest)
    for q in range(n // GROUP):
        at = pl.multiple_of(jnp.bitwise_xor(place_ref[0], q) * GROUP, GROUP)
        flat = send_refs[q].reshape(GROUP * tiles * S, LANES)
        for ct in range(tiles):
            for s in range(S):
                flat[pl.ds(ct * S + s, GROUP, stride=tiles * S), :] = w_ref[ct, s, pl.ds(at, GROUP)]
    sum_ref[0:8] = sums.total("rr")
    sum_ref[8:16] = sums.total("rw")


def second_kernel(
    n,
    tiles,
    dif_ref,
    v_ref,
    w_ref,
    sum_ref,
    jac_ref,
    edge_ref,
    coup_ref,
    stencil_ref,
    out_ref,
    z_ref,
    wh_ref,
    vs_ref,
    xs_ref,
    mx_ref,
    bs_ref,
):
    every = tiles + 1
    per = tiles * S + 1
    rr, rw = sum_ref[0:8], sum_ref[8:16]
    c1 = ratio(rw, rr)
    sums = Sums()

    def get_v(ct, t):
        return v_ref[ct, t]

    def get_w(ct, t):
        return w_ref[ct, t] if ct < tiles else wh_ref[t]

    def finish_edge(s, k, acc):
        wh_ref[s, k : k + 8] = dif_ref[s] * bs_ref[0, s * n + k : s * n + k + 8] - acc

    def finisher(ct, slot):
        def finish(s, k, acc):
            z = dif_ref[s] * bs_ref[slot, s * n + k : s * n + k + 8] - acc
            v, w = v_ref[ct, s, k : k + 8], w_ref[ct, s, k : k + 8]
            z_ref[ct, s, k : k + 8] = z
            out_ref[pl.ds(k * per + ct * S + s, 8, stride=per), :] = z
            u = w - c1 * v
            sums.add("uu", k // 8, u * u)
            sums.add("ur", k // 8, u * v)
            sums.add("uz", k // 8, u * z)
            sums.add("rz", k // 8, v * z)

        return finish

    order = list(range(1, tiles)) + [0]

    def mixed(get, ct, slot):
        return mix(get, ct, slot, coup_ref, vs_ref, mx_ref)

    def sides(get, ct, slot):
        return spread(get, ct, slot, every, stencil_ref, xs_ref, bs_ref)

    run(mixed(get_v, tiles, 0) + sides(get_v, tiles, 0))
    inside = tiles > 2
    steps = mixed(get_w, order[0], 1) + (sides(get_w, order[0], 1) if inside else [])
    react(n, tile_of(edge_ref, 0), 0, mx_ref, finish_edge, steps)
    if not inside:
        run(sides(get_w, order[0], 1))
    for at, ct in enumerate(order):
        slot = (at + 1) % 2
        steps = []
        if at + 1 < tiles:
            steps = mixed(get_w, order[at + 1], 1 - slot) + sides(get_w, order[at + 1], 1 - slot)
        react(n, tile_of(jac_ref, ct), slot, mx_ref, finisher(ct, slot), steps)
    uu, ur, uz, rz = (sums.total(name) for name in ("uu", "ur", "uz", "rz"))
    c2 = ratio(rz, rr)
    c3 = ratio(uz - c2 * ur, uu)
    for ct in range(tiles):
        for s in range(S):
            for k in range(0, n, 8):
                v, w, z = (ref[ct, s, k : k + 8] for ref in (v_ref, w_ref, z_ref))
                x = (z - c2 * v) - c3 * (w - c1 * v)
                sums.add("xx", k // 8, x * x)
    xx = sums.total("xx")
    lane = lane_iota()
    tile = jnp.zeros((8, LANES), F32)
    for q, value in enumerate((rr, c1, uu, c2, c3, xx)):
        tile = jnp.where(lane == q, value, tile)
    for k in range(0, n, 8):
        out_ref[pl.ds(k * per + tiles * S, 8, stride=per), :] = tile


def relay_kernel(own, place_ref, *refs):
    parts = GROUP // own
    count = len(refs) - parts
    for k in range(parts):
        at = jnp.bitwise_xor(place_ref[1], k)
        for q in range(count):
            refs[count + k][q] = refs[q][at]


def gather_kernel(place_ref, *refs):
    near_refs, out_ref = refs[:-1], refs[-1]
    plane = len(near_refs)
    for k in range(plane):
        for q in range(near_refs[k].shape[0]):
            d = jnp.bitwise_xor(place_ref[0], q) * plane + jnp.bitwise_xor(place_ref[1], k)
            out_ref[d] = near_refs[k][q]


def combine_kernel(parts, tiles, rhs_ref, got_ref, w_ref, update_ref, basis_ref):
    own = rhs_ref.shape[0]
    per = tiles * S + 1
    stats = got_ref[pl.ds(tiles * S, parts, stride=own * per), :]

    def stat(q):
        return jnp.broadcast_to(stats[:, q : q + 1], (parts, LANES))

    def add(x):
        return jnp.sum(x, axis=0, keepdims=True)

    rr, c1, uu, c2, c3, xx = (stat(q) for q in range(6))
    all_rr = add(rr)
    g1 = add(rr * c1) / all_rr
    g2 = add(rr * c2) / all_rr
    e1, e2 = c1 - g1, c2 - g2
    all_uu = add(uu + e1 * e1 * rr)
    g3 = add(c3 * uu + e1 * e2 * rr) / all_uu
    e3 = c3 - g3
    f = e2 - g3 * e1
    all_xx = add(xx + e3 * e3 * uu + f * f * rr)
    beta, nu, nx = jnp.sqrt(all_rr), jnp.sqrt(all_uu), jnp.sqrt(all_xx)
    h11 = 1.0 + g1
    h21 = nu / beta
    h12 = (g2 - g1 * g1) * beta / nu
    h22 = 1.0 + (g3 - g1)
    h32 = nx / nu
    m11 = h11 * h11 + h21 * h21
    m12 = h11 * h12 + h21 * h22
    m22 = h12 * h12 + h22 * h22 + h32 * h32
    b1, b2 = beta * h11, beta * h12
    determ = m11 * m22 - m12 * m12
    y1 = (m22 * b1 - m12 * b2) / determ
    y2 = (m11 * b2 - m12 * b1) / determ
    uw = y2 / nu
    ur = y1 / beta - uw * g1
    bz = 1.0 / nx
    bw = -g3 * bz
    br = (g3 * g1 - g2) * bz
    ur, uw, br, bw, bz = (jnp.broadcast_to(x, (S, LANES)) for x in (ur, uw, br, bw, bz))
    for d in range(parts):
        for m in range(own):
            for ct in range(tiles):
                at = slice((d * tiles + ct) * LANES, (d * tiles + ct + 1) * LANES)
                base = (d * own + m) * per + ct * S
                r = rhs_ref[m, :, at]
                w = w_ref[d, m, ct * S : (ct + 1) * S, :]
                update_ref[m, :, at] = ur * r + uw * w
                basis_ref[m, :, at] = br * r + bw * w + bz * got_ref[base : base + S, :]


def local(rhs, diffusivity, jac_coef, coef_index, row_mode, col_mode, multiplicity):
    parts = lax.axis_size("modes")
    own, _, total = rhs.shape
    n = own * parts
    cells = total // parts
    tiles = cells // LANES
    plane = GROUP // own
    sds = jax.ShapeDtypeStruct
    smem = pl.BlockSpec(memory_space=pltpu.SMEM)
    index = lax.axis_index("modes")
    place = jnp.stack([index // plane, index % plane]).astype(jnp.int32)

    early = (tiles + 1) // 2
    block = (plane, own, early * S, LANES)

    def across(arrays):
        lead, rows = len(arrays), arrays[0].shape[2]
        come = [arrays[0]]
        for q in range(1, lead):
            come.append(lax.ppermute(arrays[q], "modes", [(i, i ^ (q * plane)) for i in range(parts)]))
        relayed = pl.pallas_call(
            functools.partial(relay_kernel, own),
            out_shape=[sds((lead, own, rows, LANES), F32)] * plane,
            in_specs=[smem] + [VMEM] * lead,
            out_specs=[VMEM] * plane,
            compiler_params=PARAMS,
            cost_estimate=pl.CostEstimate(flops=10**11, bytes_accessed=1 << 20, transcendentals=0),
            name="relay",
        )(place, *come)
        out = [relayed[0]]
        for k in range(1, plane):
            out.append(lax.ppermute(relayed[k], "modes", [(i, i ^ k) for i in range(parts)]))
        return out, relayed[0]

    late_send, *early_send = pl.pallas_call(
        functools.partial(arrange_kernel, parts, early),
        out_shape=[sds((n, tiles + 1 - early, S, LANES), F32)] + [sds(block, F32)] * (parts // plane),
        in_specs=[smem, VMEM],
        out_specs=[VMEM] * (1 + parts // plane),
        compiler_params=PARAMS,
        name="arrange",
    )(place, rhs)
    near, relayed = across(early_send)
    vector = lax.all_to_all(late_send, "modes", split_axis=0, concat_axis=0, tiled=True)

    edge = (NCOEF, S, S, LANES)
    head, tail = pl.pallas_call(
        pack_kernel,
        grid=(1,),
        out_shape=[sds((NCOEF, S // 4, S, LANES), F32)] * 2,
        in_specs=[
            pl.BlockSpec(edge, lambda g: (0, 0, 0, 0)),
            pl.BlockSpec(edge, lambda g: (0, 0, 0, tiles - 1)),
            pl.BlockSpec(memory_space=pl.ANY),
        ],
        compiler_params=PARAMS,
        name="pack",
    )(jac_coef, jac_coef, relayed)
    up = [(i, (i + 1) % parts) for i in range(parts)]
    down = [(j, i) for i, j in up]
    after = lax.ppermute(head, "modes", down)
    before = lax.ppermute(tail, "modes", up)
    edges = pl.pallas_call(
        unpack_kernel,
        out_shape=sds((NCOEF * S, S, LANES), F32),
        in_specs=[VMEM] * 2,
        out_specs=VMEM,
        compiler_params=PARAMS,
        name="unpack",
    )(after, before)

    coupling, stencil = pl.pallas_call(
        functools.partial(coupling_kernel, n),
        out_shape=[sds((NCOEF * n, 3 * n), BF16), sds((4 * LANES, LANES), BF16)],
        in_specs=[VMEM] * 4,
        out_specs=[VMEM] * 2,
        compiler_params=PARAMS,
        name="coupling",
    )(*(x.reshape(1, -1) for x in (coef_index, row_mode, col_mode, multiplicity)))

    jac = jac_coef.reshape(NCOEF * S, S, cells)
    field = (tiles + 1, S, n, LANES)
    work = [
        pltpu.VMEM((2, 3 * n, S * LANES), BF16),
        pltpu.VMEM((2, S * n, 4 * LANES), BF16),
        pltpu.VMEM((2, NCOEF * n, S * LANES), F32),
        pltpu.VMEM((2, S * n, LANES), F32),
    ]
    v_early, a_early = pl.pallas_call(
        functools.partial(early_kernel, n, plane),
        out_shape=[sds((early, S, n, LANES), F32)] * 2,
        in_specs=[smem] + [VMEM] * (2 + plane),
        out_specs=[VMEM] * 2,
        scratch_shapes=[pltpu.VMEM((parts, own, early * S, LANES), F32), work[0], work[2]],
        compiler_params=PARAMS,
        cost_estimate=pl.CostEstimate(flops=2 * 10**9, bytes_accessed=1 << 20, transcendentals=0),
        name="early",
    )(place, jac, coupling, *near)
    v, w, sums, *w_send = pl.pallas_call(
        functools.partial(first_kernel, n, tiles),
        out_shape=[sds(field, F32), sds((tiles, S, n, LANES), F32), sds((16, LANES), F32)]
        + [sds((plane, own, tiles * S, LANES), F32)] * (n // GROUP),
        in_specs=[smem] * 2 + [VMEM] * 6 + [pl.BlockSpec(memory_space=pl.ANY)],
        out_specs=[VMEM] * (3 + n // GROUP),
        scratch_shapes=work,
        compiler_params=PARAMS,
        name="first",
    )(
        place,
        diffusivity,
        vector.reshape(n * (tiles + 1 - early) * S, LANES),
        v_early,
        a_early,
        jac,
        coupling,
        stencil,
        edges,
    )

    w_own, _ = across(w_send)

    z_send = pl.pallas_call(
        functools.partial(second_kernel, n, tiles),
        out_shape=sds((n * (tiles * S + 1), LANES), F32),
        in_specs=[smem] + [VMEM] * 7,
        out_specs=VMEM,
        scratch_shapes=[pltpu.VMEM((tiles, S, n, LANES), F32), pltpu.VMEM((S, n, LANES), F32)] + work,
        compiler_params=PARAMS,
        cost_estimate=pl.CostEstimate(flops=2 * NCOEF * S * n * n * cells, bytes_accessed=16 << 20, transcendentals=0),
        name="second",
    )(diffusivity, v, w, sums, jac, edges, coupling, stencil)
    line = (tiles * S + 1) * LANES
    got = lax.all_to_all(z_send.reshape(n, 1, line), "modes", split_axis=0, concat_axis=0, tiled=True)

    w_all = pl.pallas_call(
        gather_kernel,
        out_shape=sds((parts, own, tiles * S, LANES), F32),
        in_specs=[smem] + [VMEM] * plane,
        out_specs=VMEM,
        compiler_params=PARAMS,
        name="gather",
    )(place, *w_own)
    update, basis_next = pl.pallas_call(
        functools.partial(combine_kernel, parts, tiles),
        out_shape=[sds(rhs.shape, F32)] * 2,
        in_specs=[VMEM] * 3,
        out_specs=[VMEM] * 2,
        compiler_params=PARAMS,
        name="combine",
    )(rhs, got.reshape(n * (tiles * S + 1), LANES), w_all)
    return (update, basis_next)


def solution(mesh):
    return jax.shard_map(
        local,
        mesh=mesh,
        in_specs=(
            P(("groups", "modes"), None, None),
            P(),
            P(None, None, None, "modes"),
            P(),
            P(),
            P(),
            P(),
        ),
        out_specs=(P(("groups", "modes"), None, None), P(("groups", "modes"), None, None)),
        check_vma=False,
    )
```

```python
import functools

import jax
import jax.numpy as jnp
from jax import lax
from jax.experimental import pallas as pl
from jax.experimental.pallas import tpu as pltpu
from jax.sharding import PartitionSpec as P

NCOEF = 9
GY = 32
S = 8
LANES = 128
GROUP = 8
F32 = jnp.float32
BF16 = jnp.bfloat16
VMEM = pl.BlockSpec(memory_space=pltpu.VMEM)
PARAMS = pltpu.CompilerParams(vmem_limit_bytes=40 * 1024 * 1024)


def lane_iota():
    return lax.broadcasted_iota(jnp.int32, (S, LANES), 1)


def arrange_kernel(parts, early, place_ref, rhs_ref, out_ref, *refs):
    own, _, total = rhs_ref.shape
    cells = total // parts
    tiles = cells // LANES
    plane = GROUP // own
    low = lane_iota() < LANES // 2
    for q in range(parts // plane):
        base = jnp.bitwise_xor(place_ref[0], q) * plane
        for k in range(plane):
            for m in range(own):
                for ct in range(early):
                    at = pl.multiple_of((base + k) * cells + ct * LANES, LANES)
                    refs[q][k, m, ct * S : (ct + 1) * S, :] = rhs_ref[m, :, pl.ds(at, LANES)]
    for d in range(parts):
        after = ((d + 1) * cells) % total
        before = (d * cells - LANES) % total
        for m in range(own):
            for ct in range(early, tiles):
                at = d * cells + ct * LANES
                out_ref[d * own + m, ct - early] = rhs_ref[m, :, at : at + LANES]
            out_ref[d * own + m, tiles - early] = jnp.where(
                low, rhs_ref[m, :, after : after + LANES], rhs_ref[m, :, before : before + LANES]
            )


def pack_kernel(first_ref, last_ref, _, head_ref, tail_ref):
    piece = lane_iota() // GY
    for i in range(NCOEF):
        for q in range(S // 4):
            head = first_ref[i, q * 4]
            tail = pltpu.roll(last_ref[i, q * 4], GY, 1)
            for p in range(1, 4):
                head = jnp.where(piece == p, pltpu.roll(first_ref[i, q * 4 + p], GY * p, 1), head)
                moved = last_ref[i, q * 4 + p]
                if p < 3:
                    moved = pltpu.roll(moved, GY * (p + 1), 1)
                tail = jnp.where(piece == p, moved, tail)
            head_ref[i, q] = head
            tail_ref[i, q] = tail


def coupling_kernel(modes, coef_ref, row_ref, col_ref, mult_ref, out_ref, stencil_ref):
    rows, cols = out_ref.shape
    triples = coef_ref.shape[1]
    key = coef_ref[...] * modes + row_ref[...]
    weight = 0.25 * mult_ref[...].astype(F32)
    row = lax.broadcasted_iota(jnp.int32, (rows, triples), 0)
    left = jnp.where(row == key, weight, 0.0).astype(BF16)
    col = lax.rem(lax.broadcasted_iota(jnp.int32, (cols, triples), 0), modes)
    right = jnp.where(col == col_ref[...], 1.0, 0.0).astype(BF16)
    dense = lax.dot_general(left, right, (((1,), (1,)), ((), ())), preferred_element_type=F32)
    r = lax.broadcasted_iota(jnp.int32, (rows, cols), 0)
    c = lax.broadcasted_iota(jnp.int32, (rows, cols), 1)
    dense = dense + jnp.where(r == lax.rem(c, modes), 1.0, 0.0)
    high = dense.astype(BF16)
    low = (dense - high.astype(F32)).astype(BF16)
    out_ref[...] = jnp.where(c < 2 * modes, high.astype(F32), low.astype(F32)).astype(BF16)

    a = lax.broadcasted_iota(jnp.int32, (LANES, LANES), 0)
    b = lax.broadcasted_iota(jnp.int32, (LANES, LANES), 1)
    step = jnp.bitwise_and(a - b, GY - 1)
    same = (a // GY == b // GY) & ((step == 1) | (step == GY - 1))
    apart = jnp.abs(a - b)
    inner = jnp.where(apart == 0, 4.0, jnp.where(same | (apart == GY), -1.0, 0.0)).astype(BF16)
    outer = jnp.where(apart == LANES - GY, -1.0, 0.0).astype(BF16)
    stencil_ref[0:LANES] = inner
    stencil_ref[LANES : 2 * LANES] = inner
    stencil_ref[2 * LANES : 3 * LANES] = outer
    stencil_ref[3 * LANES :] = outer


def split(x):
    high = x.astype(BF16)
    return high, (x - high.astype(F32)).astype(BF16)


def ratio(a, b):
    return jnp.where(b > 0.0, a / jnp.where(b > 0.0, b, 1.0), 0.0)


def unpack_kernel(next_ref, prev_ref, _, out_ref):
    lane = lane_iota()
    for i in range(NCOEF):
        for q in range(S // 4):
            after, before = next_ref[i, q], prev_ref[i, q]
            for p in range(4):
                a = after if p == 0 else pltpu.roll(after, LANES - GY * p, 1)
                b = before if p == 3 else pltpu.roll(before, LANES - GY - GY * p, 1)
                out_ref[i * S + q * 4 + p] = jnp.where(lane < LANES // 2, a, b)


def mix(get, ct, slot, coup_ref, vs_ref, mx_ref):
    n = vs_ref.shape[1] // 3

    def step(first):
        for t in (first, first + 1):
            at = slice(t * LANES, (t + 1) * LANES)
            high, low = split(get(ct, t))
            vs_ref[slot, 0:n, at] = high
            vs_ref[slot, n : 2 * n, at] = low
            vs_ref[slot, 2 * n : 3 * n, at] = high
        at = slice(first * LANES, (first + 2) * LANES)
        mx_ref[slot, :, at] = jnp.dot(coup_ref[...], vs_ref[slot, :, at], preferred_element_type=F32)

    return [functools.partial(step, first) for first in range(0, S, 2)]


def spread(get, ct, slot, every, stencil_ref, xs_ref, bs_ref):
    n = bs_ref.shape[1] // S
    before, after = (ct - 1) % every, (ct + 1) % every

    def fill(first):
        wide = lax.broadcasted_iota(jnp.int32, (n, LANES), 1) < LANES // 2
        for t in (first, first + 1):
            to = slice(t * n, (t + 1) * n)
            high, low = split(get(ct, t))
            xs_ref[slot, to, 0:LANES] = high
            xs_ref[slot, to, LANES : 2 * LANES] = low
            high, low = split(jnp.where(wide, get(after, t), get(before, t)))
            xs_ref[slot, to, 2 * LANES : 3 * LANES] = high
            xs_ref[slot, to, 3 * LANES :] = low
        if first + 2 == S:
            bs_ref[slot] = jnp.dot(xs_ref[slot], stencil_ref[...], preferred_element_type=F32)

    return [functools.partial(fill, first) for first in range(0, S, 2)]


def run(steps):
    for step in steps:
        step()


def react(n, jac, slot, mx_ref, finish, steps=()):
    steps = list(steps)
    for kb in range(0, n, 32):
        acc = [None] * 32
        for i in range(NCOEF):
            if steps:
                steps.pop(0)()
            for t in range(S):
                m = [
                    mx_ref[slot, i * n + kb + kt * 8 : i * n + kb + kt * 8 + 8, t * LANES : (t + 1) * LANES]
                    for kt in range(4)
                ]
                for s in range(S):
                    j = jnp.broadcast_to(jac(i * S + s, t), (8, LANES))
                    for kt in range(4):
                        term = j * m[kt]
                        at = s * 4 + kt
                        acc[at] = term if acc[at] is None else acc[at] + term
        for s in range(S):
            for kt in range(4):
                finish(s, kb + kt * 8, acc[s * 4 + kt])
    run(steps)


def tile_of(jac_ref, ct):
    return lambda row, t: jac_ref[row, t : t + 1, ct * LANES : (ct + 1) * LANES]


class Sums:
    def __init__(self):
        self.parts = {}

    def add(self, name, at, term):
        mine = self.parts.setdefault(name, {})
        mine[at % 4] = mine[at % 4] + term if at % 4 in mine else term

    def total(self, name):
        x = functools.reduce(lambda a, b: a + b, self.parts[name].values())
        return jnp.broadcast_to(jnp.sum(x, axis=(0, 1), keepdims=True), (8, LANES))


def early_kernel(n, plane, place_ref, jac_ref, coup_ref, *refs):
    near_refs, (v_ref, a_ref, gather_ref, vs_ref, mx_ref) = refs[:plane], refs[plane:]
    early = v_ref.shape[0]
    gather_kernel(place_ref, *near_refs, gather_ref)
    flat = gather_ref.reshape(n * early * S, LANES)
    for ct in range(early):
        for s in range(S):
            v_ref[ct, s] = flat[pl.ds(ct * S + s, n, stride=early * S), :]

    def get(ct, t):
        return v_ref[ct, t]

    def finisher(ct):
        def finish(s, k, acc):
            a_ref[ct, s, k : k + 8] = acc

        return finish

    run(mix(get, 0, 0, coup_ref, vs_ref, mx_ref))
    for ct in range(early):
        steps = mix(get, ct + 1, (ct + 1) % 2, coup_ref, vs_ref, mx_ref) if ct + 1 < early else []
        react(n, tile_of(jac_ref, ct), ct % 2, mx_ref, finisher(ct), steps)


def first_kernel(n, tiles, place_ref, dif_ref, r_ref, ve_ref, ae_ref, jac_ref, coup_ref, stencil_ref, *refs):
    every = tiles + 1
    (v_ref, w_ref, sum_ref), refs = refs[:3], refs[3:]
    send_refs, (vs_ref, xs_ref, mx_ref, bs_ref) = refs[: n // GROUP], refs[n // GROUP :]
    early = ve_ref.shape[0]
    for ct in range(early):
        v_ref[ct] = ve_ref[ct]
    for ct in range(early, every):
        for s in range(S):
            v_ref[ct, s] = r_ref[pl.ds((ct - early) * S + s, n, stride=(every - early) * S), :]
    sums = Sums()

    def get(ct, t):
        return v_ref[ct, t]

    def finisher(ct, slot):
        def finish(s, k, acc):
            w = dif_ref[s] * bs_ref[slot, s * n + k : s * n + k + 8] - acc
            w_ref[ct, s, k : k + 8] = w
            v = v_ref[ct, s, k : k + 8]
            sums.add("rr", k // 8, v * v)
            sums.add("rw", k // 8, v * w)

        return finish

    def prepare(ct):
        return mix(get, ct, ct % 2, coup_ref, vs_ref, mx_ref) + sides(ct, ct % 2)

    def sides(ct, slot):
        return spread(get, ct, slot, every, stencil_ref, xs_ref, bs_ref)

    def close(ct, slot):
        for s in range(S):
            for k in range(0, n, 8):
                finisher(ct, slot)(s, k, ae_ref[ct, s, k : k + 8])

    spare = tiles % 2
    rest = []
    for ct in range(early):
        rest += sides(ct, spare) + [functools.partial(close, ct, spare)]
    if early < tiles:
        run(prepare(early))
    for ct in range(early, tiles):
        steps = prepare(ct + 1) if ct + 1 < tiles else rest
        react(n, tile_of(jac_ref, ct), ct % 2, mx_ref, finisher(ct, ct % 2), steps)
    if early == tiles:
        run(rest)
    for q in range(n // GROUP):
        at = pl.multiple_of(jnp.bitwise_xor(place_ref[0], q) * GROUP, GROUP)
        flat = send_refs[q].reshape(GROUP * tiles * S, LANES)
        for ct in range(tiles):
            for s in range(S):
                flat[pl.ds(ct * S + s, GROUP, stride=tiles * S), :] = w_ref[ct, s, pl.ds(at, GROUP)]
    sum_ref[0:8] = sums.total("rr")
    sum_ref[8:16] = sums.total("rw")


def second_kernel(
    n,
    tiles,
    dif_ref,
    v_ref,
    w_ref,
    sum_ref,
    jac_ref,
    edge_ref,
    coup_ref,
    stencil_ref,
    out_ref,
    z_ref,
    wh_ref,
    vs_ref,
    xs_ref,
    mx_ref,
    bs_ref,
):
    every = tiles + 1
    per = tiles * S + 1
    rr, rw = sum_ref[0:8], sum_ref[8:16]
    c1 = ratio(rw, rr)
    sums = Sums()

    def get_v(ct, t):
        return v_ref[ct, t]

    def get_w(ct, t):
        return w_ref[ct, t] if ct < tiles else wh_ref[t]

    def finish_edge(s, k, acc):
        wh_ref[s, k : k + 8] = dif_ref[s] * bs_ref[0, s * n + k : s * n + k + 8] - acc

    def finisher(ct, slot):
        def finish(s, k, acc):
            z = dif_ref[s] * bs_ref[slot, s * n + k : s * n + k + 8] - acc
            v, w = v_ref[ct, s, k : k + 8], w_ref[ct, s, k : k + 8]
            z_ref[ct, s, k : k + 8] = z
            out_ref[pl.ds(k * per + ct * S + s, 8, stride=per), :] = z
            u = w - c1 * v
            sums.add("uu", k // 8, u * u)
            sums.add("ur", k // 8, u * v)
            sums.add("uz", k // 8, u * z)
            sums.add("rz", k // 8, v * z)

        return finish

    order = list(range(1, tiles)) + [0]

    def mixed(get, ct, slot):
        return mix(get, ct, slot, coup_ref, vs_ref, mx_ref)

    def sides(get, ct, slot):
        return spread(get, ct, slot, every, stencil_ref, xs_ref, bs_ref)

    run(mixed(get_v, tiles, 0) + sides(get_v, tiles, 0))
    inside = tiles > 2
    steps = mixed(get_w, order[0], 1) + (sides(get_w, order[0], 1) if inside else [])
    react(n, tile_of(edge_ref, 0), 0, mx_ref, finish_edge, steps)
    if not inside:
        run(sides(get_w, order[0], 1))
    for at, ct in enumerate(order):
        slot = (at + 1) % 2
        steps = []
        if at + 1 < tiles:
            steps = mixed(get_w, order[at + 1], 1 - slot) + sides(get_w, order[at + 1], 1 - slot)
        react(n, tile_of(jac_ref, ct), slot, mx_ref, finisher(ct, slot), steps)
    uu, ur, uz, rz = (sums.total(name) for name in ("uu", "ur", "uz", "rz"))
    c2 = ratio(rz, rr)
    c3 = ratio(uz - c2 * ur, uu)
    for ct in range(tiles):
        for s in range(S):
            for k in range(0, n, 8):
                v, w, z = (ref[ct, s, k : k + 8] for ref in (v_ref, w_ref, z_ref))
                x = (z - c2 * v) - c3 * (w - c1 * v)
                sums.add("xx", k // 8, x * x)
    xx = sums.total("xx")
    lane = lane_iota()
    tile = jnp.zeros((8, LANES), F32)
    for q, value in enumerate((rr, c1, uu, c2, c3, xx)):
        tile = jnp.where(lane == q, value, tile)
    for k in range(0, n, 8):
        out_ref[pl.ds(k * per + tiles * S, 8, stride=per), :] = tile


def relay_kernel(own, place_ref, *refs):
    parts = GROUP // own
    count = len(refs) - parts
    for k in range(parts):
        at = jnp.bitwise_xor(place_ref[1], k)
        for q in range(count):
            refs[count + k][q] = refs[q][at]


def gather_kernel(place_ref, *refs):
    near_refs, out_ref = refs[:-1], refs[-1]
    plane = len(near_refs)
    for k in range(plane):
        for q in range(near_refs[k].shape[0]):
            d = jnp.bitwise_xor(place_ref[0], q) * plane + jnp.bitwise_xor(place_ref[1], k)
            out_ref[d] = near_refs[k][q]


def combine_kernel(parts, tiles, rhs_ref, got_ref, w_ref, update_ref, basis_ref):
    own = rhs_ref.shape[0]
    per = tiles * S + 1
    stats = got_ref[pl.ds(tiles * S, parts, stride=own * per), :]

    def stat(q):
        return jnp.broadcast_to(stats[:, q : q + 1], (parts, LANES))

    def add(x):
        return jnp.sum(x, axis=0, keepdims=True)

    rr, c1, uu, c2, c3, xx = (stat(q) for q in range(6))
    all_rr = add(rr)
    g1 = add(rr * c1) / all_rr
    g2 = add(rr * c2) / all_rr
    e1, e2 = c1 - g1, c2 - g2
    all_uu = add(uu + e1 * e1 * rr)
    g3 = add(c3 * uu + e1 * e2 * rr) / all_uu
    e3 = c3 - g3
    f = e2 - g3 * e1
    all_xx = add(xx + e3 * e3 * uu + f * f * rr)
    beta, nu, nx = jnp.sqrt(all_rr), jnp.sqrt(all_uu), jnp.sqrt(all_xx)
    h11 = 1.0 + g1
    h21 = nu / beta
    h12 = (g2 - g1 * g1) * beta / nu
    h22 = 1.0 + (g3 - g1)
    h32 = nx / nu
    m11 = h11 * h11 + h21 * h21
    m12 = h11 * h12 + h21 * h22
    m22 = h12 * h12 + h22 * h22 + h32 * h32
    b1, b2 = beta * h11, beta * h12
    determ = m11 * m22 - m12 * m12
    y1 = (m22 * b1 - m12 * b2) / determ
    y2 = (m11 * b2 - m12 * b1) / determ
    uw = y2 / nu
    ur = y1 / beta - uw * g1
    bz = 1.0 / nx
    bw = -g3 * bz
    br = (g3 * g1 - g2) * bz
    ur, uw, br, bw, bz = (jnp.broadcast_to(x, (S, LANES)) for x in (ur, uw, br, bw, bz))
    for d in range(parts):
        for m in range(own):
            for ct in range(tiles):
                at = slice((d * tiles + ct) * LANES, (d * tiles + ct + 1) * LANES)
                base = (d * own + m) * per + ct * S
                r = rhs_ref[m, :, at]
                w = w_ref[d, m, ct * S : (ct + 1) * S, :]
                update_ref[m, :, at] = ur * r + uw * w
                basis_ref[m, :, at] = br * r + bw * w + bz * got_ref[base : base + S, :]


def local(rhs, diffusivity, jac_coef, coef_index, row_mode, col_mode, multiplicity):
    parts = lax.axis_size("modes")
    own, _, total = rhs.shape
    n = own * parts
    cells = total // parts
    tiles = cells // LANES
    plane = GROUP // own
    sds = jax.ShapeDtypeStruct
    smem = pl.BlockSpec(memory_space=pltpu.SMEM)
    index = lax.axis_index("modes")
    place = jnp.stack([index // plane, index % plane]).astype(jnp.int32)

    early = (tiles + 1) // 2
    block = (plane, own, early * S, LANES)

    def across(arrays):
        lead, rows = len(arrays), arrays[0].shape[2]
        come = [arrays[0]]
        for q in range(1, lead):
            come.append(lax.ppermute(arrays[q], "modes", [(i, i ^ (q * plane)) for i in range(parts)]))
        relayed = pl.pallas_call(
            functools.partial(relay_kernel, own),
            out_shape=[sds((lead, own, rows, LANES), F32)] * plane,
            in_specs=[smem] + [VMEM] * lead,
            out_specs=[VMEM] * plane,
            compiler_params=PARAMS,
            cost_estimate=pl.CostEstimate(flops=10**11, bytes_accessed=1 << 20, transcendentals=0),
            name="relay",
        )(place, *come)
        out = [relayed[0]]
        for k in range(1, plane):
            out.append(lax.ppermute(relayed[k], "modes", [(i, i ^ k) for i in range(parts)]))
        return out, relayed[0]

    late_send, *early_send = pl.pallas_call(
        functools.partial(arrange_kernel, parts, early),
        out_shape=[sds((n, tiles + 1 - early, S, LANES), F32)] + [sds(block, F32)] * (parts // plane),
        in_specs=[smem, VMEM],
        out_specs=[VMEM] * (1 + parts // plane),
        compiler_params=PARAMS,
        name="arrange",
    )(place, rhs)
    near, relayed = across(early_send)
    vector = lax.all_to_all(late_send, "modes", split_axis=0, concat_axis=0, tiled=True)

    edge = (NCOEF, S, S, LANES)
    head, tail = pl.pallas_call(
        pack_kernel,
        grid=(1,),
        out_shape=[sds((NCOEF, S // 4, S, LANES), F32)] * 2,
        in_specs=[
            pl.BlockSpec(edge, lambda g: (0, 0, 0, 0)),
            pl.BlockSpec(edge, lambda g: (0, 0, 0, tiles - 1)),
            pl.BlockSpec(memory_space=pl.ANY),
        ],
        compiler_params=PARAMS,
        name="pack",
    )(jac_coef, jac_coef, relayed)
    up = [(i, (i + 1) % parts) for i in range(parts)]
    down = [(j, i) for i, j in up]
    after = lax.ppermute(head, "modes", down)
    before = lax.ppermute(tail, "modes", up)
    coupling, stencil = pl.pallas_call(
        functools.partial(coupling_kernel, n),
        out_shape=[sds((NCOEF * n, 3 * n), BF16), sds((4 * LANES, LANES), BF16)],
        in_specs=[VMEM] * 4,
        out_specs=[VMEM] * 2,
        compiler_params=PARAMS,
        name="coupling",
    )(*(x.reshape(1, -1) for x in (coef_index, row_mode, col_mode, multiplicity)))

    jac = jac_coef.reshape(NCOEF * S, S, cells)
    field = (tiles + 1, S, n, LANES)
    work = [
        pltpu.VMEM((2, 3 * n, S * LANES), BF16),
        pltpu.VMEM((2, S * n, 4 * LANES), BF16),
        pltpu.VMEM((2, NCOEF * n, S * LANES), F32),
        pltpu.VMEM((2, S * n, LANES), F32),
    ]
    v_early, a_early = pl.pallas_call(
        functools.partial(early_kernel, n, plane),
        out_shape=[sds((early, S, n, LANES), F32)] * 2,
        in_specs=[smem] + [VMEM] * (2 + plane),
        out_specs=[VMEM] * 2,
        scratch_shapes=[pltpu.VMEM((parts, own, early * S, LANES), F32), work[0], work[2]],
        compiler_params=PARAMS,
        cost_estimate=pl.CostEstimate(flops=2 * 10**9, bytes_accessed=1 << 20, transcendentals=0),
        name="early",
    )(place, jac, coupling, *near)
    v, w, sums, *w_send = pl.pallas_call(
        functools.partial(first_kernel, n, tiles),
        out_shape=[sds(field, F32), sds((tiles, S, n, LANES), F32), sds((16, LANES), F32)]
        + [sds((plane, own, tiles * S, LANES), F32)] * (n // GROUP),
        in_specs=[smem] * 2 + [VMEM] * 6,
        out_specs=[VMEM] * (3 + n // GROUP),
        scratch_shapes=work,
        compiler_params=PARAMS,
        name="first",
    )(
        place,
        diffusivity,
        vector.reshape(n * (tiles + 1 - early) * S, LANES),
        v_early,
        a_early,
        jac,
        coupling,
        stencil,
    )

    edges = pl.pallas_call(
        unpack_kernel,
        out_shape=sds((NCOEF * S, S, LANES), F32),
        in_specs=[VMEM] * 2 + [pl.BlockSpec(memory_space=pl.ANY)],
        out_specs=VMEM,
        compiler_params=PARAMS,
        name="unpack",
    )(after, before, sums)
    w_own, _ = across(w_send)

    z_send = pl.pallas_call(
        functools.partial(second_kernel, n, tiles),
        out_shape=sds((n * (tiles * S + 1), LANES), F32),
        in_specs=[smem] + [VMEM] * 7,
        out_specs=VMEM,
        scratch_shapes=[pltpu.VMEM((tiles, S, n, LANES), F32), pltpu.VMEM((S, n, LANES), F32)] + work,
        compiler_params=PARAMS,
        cost_estimate=pl.CostEstimate(flops=10**10, bytes_accessed=16 << 20, transcendentals=0),
        name="second",
    )(diffusivity, v, w, sums, jac, edges, coupling, stencil)
    line = (tiles * S + 1) * LANES
    got = lax.all_to_all(z_send.reshape(n, 1, line), "modes", split_axis=0, concat_axis=0, tiled=True)

    w_all = pl.pallas_call(
        gather_kernel,
        out_shape=sds((parts, own, tiles * S, LANES), F32),
        in_specs=[smem] + [VMEM] * plane,
        out_specs=VMEM,
        compiler_params=PARAMS,
        name="gather",
    )(place, *w_own)
    update, basis_next = pl.pallas_call(
        functools.partial(combine_kernel, parts, tiles),
        out_shape=[sds(rhs.shape, F32)] * 2,
        in_specs=[VMEM] * 3,
        out_specs=[VMEM] * 2,
        compiler_params=PARAMS,
        name="combine",
    )(rhs, got.reshape(n * (tiles * S + 1), LANES), w_all)
    return (update, basis_next)


def solution(mesh):
    return jax.shard_map(
        local,
        mesh=mesh,
        in_specs=(
            P(("groups", "modes"), None, None),
            P(),
            P(None, None, None, "modes"),
            P(),
            P(),
            P(),
            P(),
        ),
        out_specs=(P(("groups", "modes"), None, None), P(("groups", "modes"), None, None)),
        check_vma=False,
    )
```

```python
import functools

import jax
import jax.numpy as jnp
from jax import lax
from jax.experimental import pallas as pl
from jax.experimental.pallas import tpu as pltpu
from jax.sharding import PartitionSpec as P

NCOEF = 9
GY = 32
S = 8
LANES = 128
GROUP = 8
F32 = jnp.float32
BF16 = jnp.bfloat16
VMEM = pl.BlockSpec(memory_space=pltpu.VMEM)
PARAMS = pltpu.CompilerParams(vmem_limit_bytes=40 * 1024 * 1024)


def lane_iota():
    return lax.broadcasted_iota(jnp.int32, (S, LANES), 1)


def arrange_kernel(parts, early, place_ref, rhs_ref, out_ref, *refs):
    refs, (buf_ref, sems) = refs[:-2], refs[-2:]
    own, _, total = buf_ref.shape
    cells = total // parts
    tiles = cells // LANES
    plane = GROUP // own
    low = lane_iota() < LANES // 2
    copies = []
    for q in range(parts // plane):
        at = pl.ds(pl.multiple_of(jnp.bitwise_xor(place_ref[0], q) * (plane * cells), LANES), plane * cells)
        copies.append(pltpu.make_async_copy(rhs_ref.at[:, :, at], buf_ref.at[:, :, at], sems.at[q]))
        copies[q].start()
    for q in range(parts // plane):
        base = jnp.bitwise_xor(place_ref[0], q) * plane
        copies[q].wait()
        for k in range(plane):
            for m in range(own):
                for ct in range(tiles):
                    at = pl.multiple_of((base + k) * cells + ct * LANES, LANES)
                    tile = buf_ref[m, :, pl.ds(at, LANES)]
                    if ct < early:
                        refs[q][k, m, ct * S : (ct + 1) * S, :] = tile
                    else:
                        out_ref[(base + k) * own + m, ct - early] = tile
    for d in range(parts):
        after = ((d + 1) * cells) % total
        before = (d * cells - LANES) % total
        for m in range(own):
            out_ref[d * own + m, tiles - early] = jnp.where(
                low, buf_ref[m, :, after : after + LANES], buf_ref[m, :, before : before + LANES]
            )


def pack_kernel(first_ref, last_ref, _, head_ref, tail_ref):
    piece = lane_iota() // GY
    for i in range(NCOEF):
        for q in range(S // 4):
            head = first_ref[i, q * 4]
            tail = pltpu.roll(last_ref[i, q * 4], GY, 1)
            for p in range(1, 4):
                head = jnp.where(piece == p, pltpu.roll(first_ref[i, q * 4 + p], GY * p, 1), head)
                moved = last_ref[i, q * 4 + p]
                if p < 3:
                    moved = pltpu.roll(moved, GY * (p + 1), 1)
                tail = jnp.where(piece == p, moved, tail)
            head_ref[i, q] = head
            tail_ref[i, q] = tail


def coupling_kernel(modes, coef_ref, row_ref, col_ref, mult_ref, out_ref, stencil_ref):
    rows, cols = out_ref.shape
    triples = coef_ref.shape[1]
    key = coef_ref[...] * modes + row_ref[...]
    weight = 0.25 * mult_ref[...].astype(F32)
    row = lax.broadcasted_iota(jnp.int32, (rows, triples), 0)
    left = jnp.where(row == key, weight, 0.0).astype(BF16)
    col = lax.rem(lax.broadcasted_iota(jnp.int32, (cols, triples), 0), modes)
    right = jnp.where(col == col_ref[...], 1.0, 0.0).astype(BF16)
    dense = lax.dot_general(left, right, (((1,), (1,)), ((), ())), preferred_element_type=F32)
    r = lax.broadcasted_iota(jnp.int32, (rows, cols), 0)
    c = lax.broadcasted_iota(jnp.int32, (rows, cols), 1)
    dense = dense + jnp.where(r == lax.rem(c, modes), 1.0, 0.0)
    high = dense.astype(BF16)
    low = (dense - high.astype(F32)).astype(BF16)
    out_ref[...] = jnp.where(c < 2 * modes, high.astype(F32), low.astype(F32)).astype(BF16)

    a = lax.broadcasted_iota(jnp.int32, (LANES, LANES), 0)
    b = lax.broadcasted_iota(jnp.int32, (LANES, LANES), 1)
    step = jnp.bitwise_and(a - b, GY - 1)
    same = (a // GY == b // GY) & ((step == 1) | (step == GY - 1))
    apart = jnp.abs(a - b)
    inner = jnp.where(apart == 0, 4.0, jnp.where(same | (apart == GY), -1.0, 0.0)).astype(BF16)
    outer = jnp.where(apart == LANES - GY, -1.0, 0.0).astype(BF16)
    stencil_ref[0:LANES] = inner
    stencil_ref[LANES : 2 * LANES] = inner
    stencil_ref[2 * LANES : 3 * LANES] = outer
    stencil_ref[3 * LANES :] = outer


def split(x):
    high = x.astype(BF16)
    return high, (x - high.astype(F32)).astype(BF16)


def ratio(a, b):
    return jnp.where(b > 0.0, a / jnp.where(b > 0.0, b, 1.0), 0.0)


def unpack_kernel(next_ref, prev_ref, _, out_ref):
    lane = lane_iota()
    for i in range(NCOEF):
        for q in range(S // 4):
            after, before = next_ref[i, q], prev_ref[i, q]
            for p in range(4):
                a = after if p == 0 else pltpu.roll(after, LANES - GY * p, 1)
                b = before if p == 3 else pltpu.roll(before, LANES - GY - GY * p, 1)
                out_ref[i * S + q * 4 + p] = jnp.where(lane < LANES // 2, a, b)


def mix(get, ct, slot, coup_ref, vs_ref, mx_ref):
    n = vs_ref.shape[1] // 3

    def step(first):
        for t in (first, first + 1):
            at = slice(t * LANES, (t + 1) * LANES)
            high, low = split(get(ct, t))
            vs_ref[slot, 0:n, at] = high
            vs_ref[slot, n : 2 * n, at] = low
            vs_ref[slot, 2 * n : 3 * n, at] = high
        at = slice(first * LANES, (first + 2) * LANES)
        mx_ref[slot, :, at] = jnp.dot(coup_ref[...], vs_ref[slot, :, at], preferred_element_type=F32)

    return [functools.partial(step, first) for first in range(0, S, 2)]


def spread(get, ct, slot, every, stencil_ref, xs_ref, bs_ref):
    n = bs_ref.shape[1] // S
    before, after = (ct - 1) % every, (ct + 1) % every

    def fill(first):
        wide = lax.broadcasted_iota(jnp.int32, (n, LANES), 1) < LANES // 2
        for t in (first, first + 1):
            to = slice(t * n, (t + 1) * n)
            high, low = split(get(ct, t))
            xs_ref[slot, to, 0:LANES] = high
            xs_ref[slot, to, LANES : 2 * LANES] = low
            high, low = split(jnp.where(wide, get(after, t), get(before, t)))
            xs_ref[slot, to, 2 * LANES : 3 * LANES] = high
            xs_ref[slot, to, 3 * LANES :] = low
        if first + 2 == S:
            bs_ref[slot] = jnp.dot(xs_ref[slot], stencil_ref[...], preferred_element_type=F32)

    return [functools.partial(fill, first) for first in range(0, S, 2)]


def prepare(get, ct, slot, every, coup_ref, stencil_ref, vs_ref, xs_ref, mx_ref, bs_ref):
    n = bs_ref.shape[1] // S
    before, after = (ct - 1) % every, (ct + 1) % every

    def step(first):
        wide = lax.broadcasted_iota(jnp.int32, (n, LANES), 1) < LANES // 2
        for t in (first, first + 1):
            at = slice(t * LANES, (t + 1) * LANES)
            to = slice(t * n, (t + 1) * n)
            high, low = split(get(ct, t))
            vs_ref[slot, 0:n, at] = high
            vs_ref[slot, n : 2 * n, at] = low
            vs_ref[slot, 2 * n : 3 * n, at] = high
            xs_ref[slot, to, 0:LANES] = high
            xs_ref[slot, to, LANES : 2 * LANES] = low
            high, low = split(jnp.where(wide, get(after, t), get(before, t)))
            xs_ref[slot, to, 2 * LANES : 3 * LANES] = high
            xs_ref[slot, to, 3 * LANES :] = low
        at = slice(first * LANES, (first + 2) * LANES)
        mx_ref[slot, :, at] = jnp.dot(coup_ref[...], vs_ref[slot, :, at], preferred_element_type=F32)
        if first + 2 == S:
            bs_ref[slot] = jnp.dot(xs_ref[slot], stencil_ref[...], preferred_element_type=F32)

    return [functools.partial(step, first) for first in range(0, S, 2)]


def run(steps):
    for step in steps:
        step()


def react(n, jac, slot, mx_ref, finish, steps=()):
    steps = list(steps)
    for kb in range(0, n, 32):
        acc = [None] * 32
        for i in range(NCOEF):
            if steps:
                steps.pop(0)()
            for t in range(S):
                m = [
                    mx_ref[slot, i * n + kb + kt * 8 : i * n + kb + kt * 8 + 8, t * LANES : (t + 1) * LANES]
                    for kt in range(4)
                ]
                for s in range(S):
                    j = jnp.broadcast_to(jac(i * S + s, t), (8, LANES))
                    for kt in range(4):
                        term = j * m[kt]
                        at = s * 4 + kt
                        acc[at] = term if acc[at] is None else acc[at] + term
        for s in range(S):
            for kt in range(4):
                finish(s, kb + kt * 8, acc[s * 4 + kt])
    run(steps)


def tile_of(jac_ref, ct):
    return lambda row, t: jac_ref[row, t : t + 1, ct * LANES : (ct + 1) * LANES]


class Sums:
    def __init__(self):
        self.parts = {}

    def add(self, name, at, term):
        mine = self.parts.setdefault(name, {})
        mine[at % 4] = mine[at % 4] + term if at % 4 in mine else term

    def total(self, name):
        x = functools.reduce(lambda a, b: a + b, self.parts[name].values())
        return jnp.broadcast_to(jnp.sum(x, axis=(0, 1), keepdims=True), (8, LANES))


def early_kernel(n, plane, place_ref, jac_ref, coup_ref, *refs):
    near_refs, (v_ref, a_ref, gather_ref, vs_ref, mx_ref) = refs[:plane], refs[plane:]
    early = v_ref.shape[0]
    gather_kernel(place_ref, *near_refs, gather_ref)
    flat = gather_ref.reshape(n * early * S, LANES)
    for ct in range(early):
        for s in range(S):
            v_ref[ct, s] = flat[pl.ds(ct * S + s, n, stride=early * S), :]

    def get(ct, t):
        return v_ref[ct, t]

    def finisher(ct):
        def finish(s, k, acc):
            a_ref[ct, s, k : k + 8] = acc

        return finish

    run(mix(get, 0, 0, coup_ref, vs_ref, mx_ref))
    for ct in range(early):
        steps = mix(get, ct + 1, (ct + 1) % 2, coup_ref, vs_ref, mx_ref) if ct + 1 < early else []
        react(n, tile_of(jac_ref, ct), ct % 2, mx_ref, finisher(ct), steps)


def first_kernel(n, tiles, place_ref, dif_ref, r_ref, ve_ref, ae_ref, jac_ref, coup_ref, stencil_ref, *refs):
    every = tiles + 1
    (v_ref, w_ref, sum_ref), refs = refs[:3], refs[3:]
    send_refs, (vs_ref, xs_ref, mx_ref, bs_ref) = refs[: n // GROUP], refs[n // GROUP :]
    early = ve_ref.shape[0]
    for ct in range(early):
        v_ref[ct] = ve_ref[ct]
    for ct in range(early, every):
        for s in range(S):
            v_ref[ct, s] = r_ref[pl.ds((ct - early) * S + s, n, stride=(every - early) * S), :]
    sums = Sums()

    def get(ct, t):
        return v_ref[ct, t]

    def finisher(ct, slot):
        def finish(s, k, acc):
            w = dif_ref[s] * bs_ref[slot, s * n + k : s * n + k + 8] - acc
            w_ref[ct, s, k : k + 8] = w
            v = v_ref[ct, s, k : k + 8]
            sums.add("rr", k // 8, v * v)
            sums.add("rw", k // 8, v * w)

        return finish

    def ready(ct):
        return prepare(get, ct, ct % 2, every, coup_ref, stencil_ref, vs_ref, xs_ref, mx_ref, bs_ref)

    def sides(ct, slot):
        return spread(get, ct, slot, every, stencil_ref, xs_ref, bs_ref)

    def close(ct, slot):
        for s in range(S):
            for k in range(0, n, 8):
                finisher(ct, slot)(s, k, ae_ref[ct, s, k : k + 8])

    spare = tiles % 2
    rest = []
    for ct in range(early):
        rest += sides(ct, spare) + [functools.partial(close, ct, spare)]
    if early < tiles:
        run(ready(early))
    for ct in range(early, tiles):
        steps = ready(ct + 1) if ct + 1 < tiles else rest
        react(n, tile_of(jac_ref, ct), ct % 2, mx_ref, finisher(ct, ct % 2), steps)
    if early == tiles:
        run(rest)
    for q in range(n // GROUP):
        at = pl.multiple_of(jnp.bitwise_xor(place_ref[0], q) * GROUP, GROUP)
        flat = send_refs[q].reshape(GROUP * tiles * S, LANES)
        for ct in range(tiles):
            for s in range(S):
                flat[pl.ds(ct * S + s, GROUP, stride=tiles * S), :] = w_ref[ct, s, pl.ds(at, GROUP)]
    sum_ref[0:8] = sums.total("rr")
    sum_ref[8:16] = sums.total("rw")


def second_kernel(
    n,
    tiles,
    dif_ref,
    v_ref,
    w_ref,
    sum_ref,
    jac_ref,
    edge_ref,
    coup_ref,
    stencil_ref,
    out_ref,
    z_ref,
    wh_ref,
    vs_ref,
    xs_ref,
    mx_ref,
    bs_ref,
):
    every = tiles + 1
    per = tiles * S + 1
    rr, rw = sum_ref[0:8], sum_ref[8:16]
    c1 = ratio(rw, rr)
    sums = Sums()

    def get_v(ct, t):
        return v_ref[ct, t]

    def get_w(ct, t):
        return w_ref[ct, t] if ct < tiles else wh_ref[t]

    def finish_edge(s, k, acc):
        wh_ref[s, k : k + 8] = dif_ref[s] * bs_ref[0, s * n + k : s * n + k + 8] - acc

    def finisher(ct, slot):
        def finish(s, k, acc):
            z = dif_ref[s] * bs_ref[slot, s * n + k : s * n + k + 8] - acc
            v, w = v_ref[ct, s, k : k + 8], w_ref[ct, s, k : k + 8]
            z_ref[ct, s, k : k + 8] = z
            out_ref[pl.ds(k * per + ct * S + s, 8, stride=per), :] = z
            u = w - c1 * v
            sums.add("uu", k // 8, u * u)
            sums.add("ur", k // 8, u * v)
            sums.add("uz", k // 8, u * z)
            sums.add("rz", k // 8, v * z)

        return finish

    order = list(range(1, tiles)) + [0]

    def ready(get, ct, slot):
        return prepare(get, ct, slot, every, coup_ref, stencil_ref, vs_ref, xs_ref, mx_ref, bs_ref)

    run(ready(get_v, tiles, 0))
    inside = tiles > 2
    steps = ready(get_w, order[0], 1) if inside else []
    react(n, tile_of(edge_ref, 0), 0, mx_ref, finish_edge, steps)
    if not inside:
        run(ready(get_w, order[0], 1))
    for at, ct in enumerate(order):
        slot = (at + 1) % 2
        steps = ready(get_w, order[at + 1], 1 - slot) if at + 1 < tiles else []
        react(n, tile_of(jac_ref, ct), slot, mx_ref, finisher(ct, slot), steps)
    uu, ur, uz, rz = (sums.total(name) for name in ("uu", "ur", "uz", "rz"))
    c2 = ratio(rz, rr)
    c3 = ratio(uz - c2 * ur, uu)
    for ct in range(tiles):
        for s in range(S):
            for k in range(0, n, 8):
                v, w, z = (ref[ct, s, k : k + 8] for ref in (v_ref, w_ref, z_ref))
                x = (z - c2 * v) - c3 * (w - c1 * v)
                sums.add("xx", k // 8, x * x)
    xx = sums.total("xx")
    lane = lane_iota()
    tile = jnp.zeros((8, LANES), F32)
    for q, value in enumerate((rr, c1, uu, c2, c3, xx)):
        tile = jnp.where(lane == q, value, tile)
    for k in range(0, n, 8):
        out_ref[pl.ds(k * per + tiles * S, 8, stride=per), :] = tile


def relay_kernel(own, place_ref, *refs):
    parts = GROUP // own
    count = len(refs) - parts
    for k in range(parts):
        at = jnp.bitwise_xor(place_ref[1], k)
        for q in range(count):
            refs[count + k][q] = refs[q][at]


def gather_kernel(place_ref, *refs):
    near_refs, out_ref = refs[:-1], refs[-1]
    plane = len(near_refs)
    for k in range(plane):
        for q in range(near_refs[k].shape[0]):
            d = jnp.bitwise_xor(place_ref[0], q) * plane + jnp.bitwise_xor(place_ref[1], k)
            out_ref[d] = near_refs[k][q]


def combine_kernel(parts, tiles, rhs_ref, got_ref, w_ref, update_ref, basis_ref):
    own = rhs_ref.shape[0]
    per = tiles * S + 1
    stats = got_ref[pl.ds(tiles * S, parts, stride=own * per), :]

    def stat(q):
        return jnp.broadcast_to(stats[:, q : q + 1], (parts, LANES))

    def add(x):
        return jnp.sum(x, axis=0, keepdims=True)

    rr, c1, uu, c2, c3, xx = (stat(q) for q in range(6))
    all_rr = add(rr)
    g1 = add(rr * c1) / all_rr
    g2 = add(rr * c2) / all_rr
    e1, e2 = c1 - g1, c2 - g2
    all_uu = add(uu + e1 * e1 * rr)
    g3 = add(c3 * uu + e1 * e2 * rr) / all_uu
    e3 = c3 - g3
    f = e2 - g3 * e1
    all_xx = add(xx + e3 * e3 * uu + f * f * rr)
    beta, nu, nx = jnp.sqrt(all_rr), jnp.sqrt(all_uu), jnp.sqrt(all_xx)
    h11 = 1.0 + g1
    h21 = nu / beta
    h12 = (g2 - g1 * g1) * beta / nu
    h22 = 1.0 + (g3 - g1)
    h32 = nx / nu
    m11 = h11 * h11 + h21 * h21
    m12 = h11 * h12 + h21 * h22
    m22 = h12 * h12 + h22 * h22 + h32 * h32
    b1, b2 = beta * h11, beta * h12
    determ = m11 * m22 - m12 * m12
    y1 = (m22 * b1 - m12 * b2) / determ
    y2 = (m11 * b2 - m12 * b1) / determ
    uw = y2 / nu
    ur = y1 / beta - uw * g1
    bz = 1.0 / nx
    bw = -g3 * bz
    br = (g3 * g1 - g2) * bz
    ur, uw, br, bw, bz = (jnp.broadcast_to(x, (S, LANES)) for x in (ur, uw, br, bw, bz))
    for d in range(parts):
        for m in range(own):
            for ct in range(tiles):
                at = slice((d * tiles + ct) * LANES, (d * tiles + ct + 1) * LANES)
                base = (d * own + m) * per + ct * S
                r = rhs_ref[m, :, at]
                w = w_ref[d, m, ct * S : (ct + 1) * S, :]
                update_ref[m, :, at] = ur * r + uw * w
                basis_ref[m, :, at] = br * r + bw * w + bz * got_ref[base : base + S, :]


def local(rhs, diffusivity, jac_coef, coef_index, row_mode, col_mode, multiplicity):
    parts = lax.axis_size("modes")
    own, _, total = rhs.shape
    n = own * parts
    cells = total // parts
    tiles = cells // LANES
    plane = GROUP // own
    sds = jax.ShapeDtypeStruct
    smem = pl.BlockSpec(memory_space=pltpu.SMEM)
    index = lax.axis_index("modes")
    place = jnp.stack([index // plane, index % plane]).astype(jnp.int32)

    early = (tiles + 1) // 2
    block = (plane, own, early * S, LANES)

    def across(arrays):
        lead, rows = len(arrays), arrays[0].shape[2]
        come = [arrays[0]]
        for q in range(1, lead):
            come.append(lax.ppermute(arrays[q], "modes", [(i, i ^ (q * plane)) for i in range(parts)]))
        relayed = pl.pallas_call(
            functools.partial(relay_kernel, own),
            out_shape=[sds((lead, own, rows, LANES), F32)] * plane,
            in_specs=[smem] + [VMEM] * lead,
            out_specs=[VMEM] * plane,
            compiler_params=PARAMS,
            cost_estimate=pl.CostEstimate(flops=10**11, bytes_accessed=1 << 20, transcendentals=0),
            name="relay",
        )(place, *come)
        out = [relayed[0]]
        for k in range(1, plane):
            out.append(lax.ppermute(relayed[k], "modes", [(i, i ^ k) for i in range(parts)]))
        return out, relayed[0]

    late_send, *early_send = pl.pallas_call(
        functools.partial(arrange_kernel, parts, early),
        out_shape=[sds((n, tiles + 1 - early, S, LANES), F32)] + [sds(block, F32)] * (parts // plane),
        in_specs=[smem, pl.BlockSpec(memory_space=pltpu.HBM)],
        out_specs=[VMEM] * (1 + parts // plane),
        scratch_shapes=[pltpu.VMEM(rhs.shape, F32), pltpu.SemaphoreType.DMA((parts // plane,))],
        compiler_params=pltpu.CompilerParams(vmem_limit_bytes=60 * 1024 * 1024),
        name="arrange",
    )(place, rhs)
    near, relayed = across(early_send)
    vector = lax.all_to_all(late_send, "modes", split_axis=0, concat_axis=0, tiled=True)

    edge = (NCOEF, S, S, LANES)
    head, tail = pl.pallas_call(
        pack_kernel,
        grid=(1,),
        out_shape=[sds((NCOEF, S // 4, S, LANES), F32)] * 2,
        in_specs=[
            pl.BlockSpec(edge, lambda g: (0, 0, 0, 0)),
            pl.BlockSpec(edge, lambda g: (0, 0, 0, tiles - 1)),
            pl.BlockSpec(memory_space=pl.ANY),
        ],
        compiler_params=PARAMS,
        name="pack",
    )(jac_coef, jac_coef, relayed)
    up = [(i, (i + 1) % parts) for i in range(parts)]
    down = [(j, i) for i, j in up]
    after = lax.ppermute(head, "modes", down)
    before = lax.ppermute(tail, "modes", up)
    coupling, stencil = pl.pallas_call(
        functools.partial(coupling_kernel, n),
        out_shape=[sds((NCOEF * n, 3 * n), BF16), sds((4 * LANES, LANES), BF16)],
        in_specs=[VMEM] * 4,
        out_specs=[VMEM] * 2,
        compiler_params=PARAMS,
        name="coupling",
    )(*(x.reshape(1, -1) for x in (coef_index, row_mode, col_mode, multiplicity)))

    jac = jac_coef.reshape(NCOEF * S, S, cells)
    field = (tiles + 1, S, n, LANES)
    work = [
        pltpu.VMEM((2, 3 * n, S * LANES), BF16),
        pltpu.VMEM((2, S * n, 4 * LANES), BF16),
        pltpu.VMEM((2, NCOEF * n, S * LANES), F32),
        pltpu.VMEM((2, S * n, LANES), F32),
    ]
    v_early, a_early = pl.pallas_call(
        functools.partial(early_kernel, n, plane),
        out_shape=[sds((early, S, n, LANES), F32)] * 2,
        in_specs=[smem] + [VMEM] * (2 + plane),
        out_specs=[VMEM] * 2,
        scratch_shapes=[pltpu.VMEM((parts, own, early * S, LANES), F32), work[0], work[2]],
        compiler_params=PARAMS,
        cost_estimate=pl.CostEstimate(flops=2 * 10**9, bytes_accessed=1 << 20, transcendentals=0),
        name="early",
    )(place, jac, coupling, *near)
    v, w, sums, *w_send = pl.pallas_call(
        functools.partial(first_kernel, n, tiles),
        out_shape=[sds(field, F32), sds((tiles, S, n, LANES), F32), sds((16, LANES), F32)]
        + [sds((plane, own, tiles * S, LANES), F32)] * (n // GROUP),
        in_specs=[smem] * 2 + [VMEM] * 6,
        out_specs=[VMEM] * (3 + n // GROUP),
        scratch_shapes=work,
        compiler_params=PARAMS,
        name="first",
    )(
        place,
        diffusivity,
        vector.reshape(n * (tiles + 1 - early) * S, LANES),
        v_early,
        a_early,
        jac,
        coupling,
        stencil,
    )

    edges = pl.pallas_call(
        unpack_kernel,
        out_shape=sds((NCOEF * S, S, LANES), F32),
        in_specs=[VMEM] * 2 + [pl.BlockSpec(memory_space=pl.ANY)],
        out_specs=VMEM,
        compiler_params=PARAMS,
        name="unpack",
    )(after, before, sums)
    w_own, _ = across(w_send)

    z_send = pl.pallas_call(
        functools.partial(second_kernel, n, tiles),
        out_shape=sds((n * (tiles * S + 1), LANES), F32),
        in_specs=[smem] + [VMEM] * 7,
        out_specs=VMEM,
        scratch_shapes=[pltpu.VMEM((tiles, S, n, LANES), F32), pltpu.VMEM((S, n, LANES), F32)] + work,
        compiler_params=PARAMS,
        cost_estimate=pl.CostEstimate(flops=10**10, bytes_accessed=16 << 20, transcendentals=0),
        name="second",
    )(diffusivity, v, w, sums, jac, edges, coupling, stencil)
    line = (tiles * S + 1) * LANES
    got = lax.all_to_all(z_send.reshape(n, 1, line), "modes", split_axis=0, concat_axis=0, tiled=True)

    w_all = pl.pallas_call(
        gather_kernel,
        out_shape=sds((parts, own, tiles * S, LANES), F32),
        in_specs=[smem] + [VMEM] * plane,
        out_specs=VMEM,
        compiler_params=PARAMS,
        name="gather",
    )(place, *w_own)
    update, basis_next = pl.pallas_call(
        functools.partial(combine_kernel, parts, tiles),
        out_shape=[sds(rhs.shape, F32)] * 2,
        in_specs=[VMEM] * 3,
        out_specs=[VMEM] * 2,
        compiler_params=PARAMS,
        name="combine",
    )(rhs, got.reshape(n * (tiles * S + 1), LANES), w_all)
    return (update, basis_next)


def solution(mesh):
    return jax.shard_map(
        local,
        mesh=mesh,
        in_specs=(
            P(("groups", "modes"), None, None),
            P(),
            P(None, None, None, "modes"),
            P(),
            P(),
            P(),
            P(),
        ),
        out_specs=(P(("groups", "modes"), None, None), P(("groups", "modes"), None, None)),
        check_vma=False,
    )
```

```python
import functools

import jax
import jax.numpy as jnp
from jax import lax
from jax.experimental import pallas as pl
from jax.experimental.pallas import tpu as pltpu
from jax.sharding import PartitionSpec as P

NCOEF = 9
GY = 32
S = 8
LANES = 128
GROUP = 8
F32 = jnp.float32
BF16 = jnp.bfloat16
VMEM = pl.BlockSpec(memory_space=pltpu.VMEM)
PARAMS = pltpu.CompilerParams(vmem_limit_bytes=40 * 1024 * 1024)


def lane_iota():
    return lax.broadcasted_iota(jnp.int32, (S, LANES), 1)


def arrange_kernel(parts, early, place_ref, rhs_ref, out_ref, *refs):
    own, _, total = rhs_ref.shape
    cells = total // parts
    tiles = cells // LANES
    plane = GROUP // own
    low = lane_iota() < LANES // 2
    for q in range(parts // plane):
        base = jnp.bitwise_xor(place_ref[0], q) * plane
        for k in range(plane):
            for m in range(own):
                for ct in range(early):
                    at = pl.multiple_of((base + k) * cells + ct * LANES, LANES)
                    refs[q][k, m, ct * S : (ct + 1) * S, :] = rhs_ref[m, :, pl.ds(at, LANES)]
    for d in range(parts):
        after = ((d + 1) * cells) % total
        before = (d * cells - LANES) % total
        for m in range(own):
            for ct in range(early, tiles):
                at = d * cells + ct * LANES
                out_ref[d * own + m, ct - early] = rhs_ref[m, :, at : at + LANES]
            out_ref[d * own + m, tiles - early] = jnp.where(
                low, rhs_ref[m, :, after : after + LANES], rhs_ref[m, :, before : before + LANES]
            )


def pack_kernel(first_ref, last_ref, _, head_ref, tail_ref):
    piece = lane_iota() // GY
    for i in range(NCOEF):
        for q in range(S // 4):
            head = first_ref[i, q * 4]
            tail = pltpu.roll(last_ref[i, q * 4], GY, 1)
            for p in range(1, 4):
                head = jnp.where(piece == p, pltpu.roll(first_ref[i, q * 4 + p], GY * p, 1), head)
                moved = last_ref[i, q * 4 + p]
                if p < 3:
                    moved = pltpu.roll(moved, GY * (p + 1), 1)
                tail = jnp.where(piece == p, moved, tail)
            head_ref[i, q] = head
            tail_ref[i, q] = tail


def coupling_kernel(modes, coef_ref, row_ref, col_ref, mult_ref, _, out_ref, stencil_ref):
    rows, cols = out_ref.shape
    triples = coef_ref.shape[1]
    key = coef_ref[...] * modes + row_ref[...]
    weight = 0.25 * mult_ref[...].astype(F32)
    row = lax.broadcasted_iota(jnp.int32, (rows, triples), 0)
    left = jnp.where(row == key, weight, 0.0).astype(BF16)
    col = lax.rem(lax.broadcasted_iota(jnp.int32, (cols, triples), 0), modes)
    right = jnp.where(col == col_ref[...], 1.0, 0.0).astype(BF16)
    dense = lax.dot_general(left, right, (((1,), (1,)), ((), ())), preferred_element_type=F32)
    r = lax.broadcasted_iota(jnp.int32, (rows, cols), 0)
    c = lax.broadcasted_iota(jnp.int32, (rows, cols), 1)
    dense = dense + jnp.where(r == lax.rem(c, modes), 1.0, 0.0)
    high = dense.astype(BF16)
    low = (dense - high.astype(F32)).astype(BF16)
    out_ref[...] = jnp.where(c < 2 * modes, high.astype(F32), low.astype(F32)).astype(BF16)

    a = lax.broadcasted_iota(jnp.int32, (LANES, LANES), 0)
    b = lax.broadcasted_iota(jnp.int32, (LANES, LANES), 1)
    step = jnp.bitwise_and(a - b, GY - 1)
    same = (a // GY == b // GY) & ((step == 1) | (step == GY - 1))
    apart = jnp.abs(a - b)
    inner = jnp.where(apart == 0, 4.0, jnp.where(same | (apart == GY), -1.0, 0.0)).astype(BF16)
    outer = jnp.where(apart == LANES - GY, -1.0, 0.0).astype(BF16)
    stencil_ref[0:LANES] = inner
    stencil_ref[LANES : 2 * LANES] = inner
    stencil_ref[2 * LANES : 3 * LANES] = outer
    stencil_ref[3 * LANES :] = outer


def split(x):
    high = x.astype(BF16)
    return high, (x - high.astype(F32)).astype(BF16)


def ratio(a, b):
    return jnp.where(b > 0.0, a / jnp.where(b > 0.0, b, 1.0), 0.0)


def unpack_kernel(next_ref, prev_ref, _, out_ref):
    lane = lane_iota()
    for i in range(NCOEF):
        for q in range(S // 4):
            after, before = next_ref[i, q], prev_ref[i, q]
            for p in range(4):
                a = after if p == 0 else pltpu.roll(after, LANES - GY * p, 1)
                b = before if p == 3 else pltpu.roll(before, LANES - GY - GY * p, 1)
                out_ref[i * S + q * 4 + p] = jnp.where(lane < LANES // 2, a, b)


def mix(get, ct, slot, coup_ref, vs_ref, mx_ref):
    n = vs_ref.shape[1] // 3

    def step(first):
        for t in (first, first + 1):
            at = slice(t * LANES, (t + 1) * LANES)
            high, low = split(get(ct, t))
            vs_ref[slot, 0:n, at] = high
            vs_ref[slot, n : 2 * n, at] = low
            vs_ref[slot, 2 * n : 3 * n, at] = high
        at = slice(first * LANES, (first + 2) * LANES)
        mx_ref[slot, :, at] = jnp.dot(coup_ref[...], vs_ref[slot, :, at], preferred_element_type=F32)

    return [functools.partial(step, first) for first in range(0, S, 2)]


def spread(get, ct, slot, every, stencil_ref, xs_ref, bs_ref):
    n = bs_ref.shape[1] // S
    before, after = (ct - 1) % every, (ct + 1) % every

    def fill(first):
        wide = lax.broadcasted_iota(jnp.int32, (n, LANES), 1) < LANES // 2
        for t in (first, first + 1):
            to = slice(t * n, (t + 1) * n)
            high, low = split(get(ct, t))
            xs_ref[slot, to, 0:LANES] = high
            xs_ref[slot, to, LANES : 2 * LANES] = low
            high, low = split(jnp.where(wide, get(after, t), get(before, t)))
            xs_ref[slot, to, 2 * LANES : 3 * LANES] = high
            xs_ref[slot, to, 3 * LANES :] = low
        if first + 2 == S:
            bs_ref[slot] = jnp.dot(xs_ref[slot], stencil_ref[...], preferred_element_type=F32)

    return [functools.partial(fill, first) for first in range(0, S, 2)]


def run(steps):
    for step in steps:
        step()


def react(n, jac, slot, mx_ref, finish, steps=()):
    steps = list(steps)
    for kb in range(0, n, 32):
        acc = [None] * 32
        for i in range(NCOEF):
            if steps:
                steps.pop(0)()
            for t in range(S):
                m = [
                    mx_ref[slot, i * n + kb + kt * 8 : i * n + kb + kt * 8 + 8, t * LANES : (t + 1) * LANES]
                    for kt in range(4)
                ]
                for s in range(S):
                    j = jnp.broadcast_to(jac(i * S + s, t), (8, LANES))
                    for kt in range(4):
                        term = j * m[kt]
                        at = s * 4 + kt
                        acc[at] = term if acc[at] is None else acc[at] + term
        for s in range(S):
            for kt in range(4):
                finish(s, kb + kt * 8, acc[s * 4 + kt])
    run(steps)


def tile_of(jac_ref, ct):
    return lambda row, t: jac_ref[row, t : t + 1, ct * LANES : (ct + 1) * LANES]


class Sums:
    def __init__(self):
        self.parts = {}

    def add(self, name, at, term):
        mine = self.parts.setdefault(name, {})
        mine[at % 4] = mine[at % 4] + term if at % 4 in mine else term

    def total(self, name):
        x = functools.reduce(lambda a, b: a + b, self.parts[name].values())
        return jnp.broadcast_to(jnp.sum(x, axis=(0, 1), keepdims=True), (8, LANES))


def late_kernel(n, early, jac_ref, coup_ref, r_ref, v_ref, a_ref, vs_ref, mx_ref):
    late = v_ref.shape[0]
    for ct in range(late):
        for s in range(S):
            v_ref[ct, s] = r_ref[pl.ds(ct * S + s, n, stride=late * S), :]

    def get(ct, t):
        return v_ref[ct, t]

    def finisher(ct):
        def finish(s, k, acc):
            a_ref[ct, s, k : k + 8] = acc

        return finish

    if late > 1:
        run(mix(get, 0, 0, coup_ref, vs_ref, mx_ref))
    for ct in range(late - 1):
        steps = mix(get, ct + 1, (ct + 1) % 2, coup_ref, vs_ref, mx_ref) if ct + 2 < late else []
        react(n, tile_of(jac_ref, early + ct), ct % 2, mx_ref, finisher(ct), steps)


def first_kernel(n, tiles, plane, place_ref, dif_ref, vl_ref, al_ref, jac_ref, coup_ref, stencil_ref, *refs):
    every = tiles + 1
    near_refs, (v_ref, w_ref, sum_ref), refs = refs[:plane], refs[plane : plane + 3], refs[plane + 3 :]
    send_refs, (gather_ref, vs_ref, xs_ref, mx_ref, bs_ref) = refs[: n // GROUP], refs[n // GROUP :]
    early = every - vl_ref.shape[0]
    gather_kernel(place_ref, *near_refs, gather_ref)
    flat = gather_ref.reshape(n * early * S, LANES)
    for ct in range(early):
        for s in range(S):
            v_ref[ct, s] = flat[pl.ds(ct * S + s, n, stride=early * S), :]
    for ct in range(early, every):
        v_ref[ct] = vl_ref[ct - early]
    sums = Sums()

    def get(ct, t):
        return v_ref[ct, t]

    def finisher(ct, slot):
        def finish(s, k, acc):
            w = dif_ref[s] * bs_ref[slot, s * n + k : s * n + k + 8] - acc
            w_ref[ct, s, k : k + 8] = w
            v = v_ref[ct, s, k : k + 8]
            sums.add("rr", k // 8, v * v)
            sums.add("rw", k // 8, v * w)

        return finish

    def prepare(ct):
        return mix(get, ct, ct % 2, coup_ref, vs_ref, mx_ref) + sides(ct, ct % 2)

    def sides(ct, slot):
        return spread(get, ct, slot, every, stencil_ref, xs_ref, bs_ref)

    def close(ct, slot):
        for s in range(S):
            for k in range(0, n, 8):
                finisher(ct, slot)(s, k, al_ref[ct - early, s, k : k + 8])

    spare = early % 2
    rest = []
    for ct in range(early, tiles):
        rest += sides(ct, spare) + [functools.partial(close, ct, spare)]
    run(prepare(0))
    for ct in range(early):
        steps = prepare(ct + 1) if ct + 1 < early else rest
        react(n, tile_of(jac_ref, ct), ct % 2, mx_ref, finisher(ct, ct % 2), steps)
    for q in range(n // GROUP):
        at = pl.multiple_of(jnp.bitwise_xor(place_ref[0], q) * GROUP, GROUP)
        flat = send_refs[q].reshape(GROUP * tiles * S, LANES)
        for ct in range(tiles):
            for s in range(S):
                flat[pl.ds(ct * S + s, GROUP, stride=tiles * S), :] = w_ref[ct, s, pl.ds(at, GROUP)]
    sum_ref[0:8] = sums.total("rr")
    sum_ref[8:16] = sums.total("rw")


def second_kernel(
    n,
    tiles,
    dif_ref,
    v_ref,
    w_ref,
    sum_ref,
    jac_ref,
    edge_ref,
    coup_ref,
    stencil_ref,
    out_ref,
    z_ref,
    wh_ref,
    vs_ref,
    xs_ref,
    mx_ref,
    bs_ref,
):
    every = tiles + 1
    per = tiles * S + 1
    rr, rw = sum_ref[0:8], sum_ref[8:16]
    c1 = ratio(rw, rr)
    sums = Sums()

    def get_v(ct, t):
        return v_ref[ct, t]

    def get_w(ct, t):
        return w_ref[ct, t] if ct < tiles else wh_ref[t]

    def finish_edge(s, k, acc):
        wh_ref[s, k : k + 8] = dif_ref[s] * bs_ref[0, s * n + k : s * n + k + 8] - acc

    def finisher(ct, slot):
        def finish(s, k, acc):
            z = dif_ref[s] * bs_ref[slot, s * n + k : s * n + k + 8] - acc
            v, w = v_ref[ct, s, k : k + 8], w_ref[ct, s, k : k + 8]
            z_ref[ct, s, k : k + 8] = z
            out_ref[pl.ds(k * per + ct * S + s, 8, stride=per), :] = z
            u = w - c1 * v
            sums.add("uu", k // 8, u * u)
            sums.add("ur", k // 8, u * v)
            sums.add("uz", k // 8, u * z)
            sums.add("rz", k // 8, v * z)

        return finish

    order = list(range(1, tiles)) + [0]

    def mixed(get, ct, slot):
        return mix(get, ct, slot, coup_ref, vs_ref, mx_ref)

    def sides(get, ct, slot):
        return spread(get, ct, slot, every, stencil_ref, xs_ref, bs_ref)

    run(mixed(get_v, tiles, 0) + sides(get_v, tiles, 0))
    inside = tiles > 2
    steps = mixed(get_w, order[0], 1) + (sides(get_w, order[0], 1) if inside else [])
    react(n, tile_of(edge_ref, 0), 0, mx_ref, finish_edge, steps)
    if not inside:
        run(sides(get_w, order[0], 1))
    for at, ct in enumerate(order):
        slot = (at + 1) % 2
        steps = []
        if at + 1 < tiles:
            steps = mixed(get_w, order[at + 1], 1 - slot) + sides(get_w, order[at + 1], 1 - slot)
        react(n, tile_of(jac_ref, ct), slot, mx_ref, finisher(ct, slot), steps)
    uu, ur, uz, rz = (sums.total(name) for name in ("uu", "ur", "uz", "rz"))
    c2 = ratio(rz, rr)
    c3 = ratio(uz - c2 * ur, uu)
    for ct in range(tiles):
        for s in range(S):
            for k in range(0, n, 8):
                v, w, z = (ref[ct, s, k : k + 8] for ref in (v_ref, w_ref, z_ref))
                x = (z - c2 * v) - c3 * (w - c1 * v)
                sums.add("xx", k // 8, x * x)
    xx = sums.total("xx")
    lane = lane_iota()
    tile = jnp.zeros((8, LANES), F32)
    for q, value in enumerate((rr, c1, uu, c2, c3, xx)):
        tile = jnp.where(lane == q, value, tile)
    for k in range(0, n, 8):
        out_ref[pl.ds(k * per + tiles * S, 8, stride=per), :] = tile


def relay_kernel(own, place_ref, *refs):
    parts = GROUP // own
    count = len(refs) - parts
    for k in range(parts):
        at = jnp.bitwise_xor(place_ref[1], k)
        for q in range(count):
            refs[count + k][q] = refs[q][at]


def gather_kernel(place_ref, *refs):
    near_refs, out_ref = refs[:-1], refs[-1]
    plane = len(near_refs)
    for k in range(plane):
        for q in range(near_refs[k].shape[0]):
            d = jnp.bitwise_xor(place_ref[0], q) * plane + jnp.bitwise_xor(place_ref[1], k)
            out_ref[d] = near_refs[k][q]


def combine_kernel(parts, tiles, rhs_ref, got_ref, w_ref, update_ref, basis_ref):
    own = rhs_ref.shape[0]
    per = tiles * S + 1
    stats = got_ref[pl.ds(tiles * S, parts, stride=own * per), :]

    def stat(q):
        return jnp.broadcast_to(stats[:, q : q + 1], (parts, LANES))

    def add(x):
        return jnp.sum(x, axis=0, keepdims=True)

    rr, c1, uu, c2, c3, xx = (stat(q) for q in range(6))
    all_rr = add(rr)
    g1 = add(rr * c1) / all_rr
    g2 = add(rr * c2) / all_rr
    e1, e2 = c1 - g1, c2 - g2
    all_uu = add(uu + e1 * e1 * rr)
    g3 = add(c3 * uu + e1 * e2 * rr) / all_uu
    e3 = c3 - g3
    f = e2 - g3 * e1
    all_xx = add(xx + e3 * e3 * uu + f * f * rr)
    beta, nu, nx = jnp.sqrt(all_rr), jnp.sqrt(all_uu), jnp.sqrt(all_xx)
    h11 = 1.0 + g1
    h21 = nu / beta
    h12 = (g2 - g1 * g1) * beta / nu
    h22 = 1.0 + (g3 - g1)
    h32 = nx / nu
    m11 = h11 * h11 + h21 * h21
    m12 = h11 * h12 + h21 * h22
    m22 = h12 * h12 + h22 * h22 + h32 * h32
    b1, b2 = beta * h11, beta * h12
    determ = m11 * m22 - m12 * m12
    y1 = (m22 * b1 - m12 * b2) / determ
    y2 = (m11 * b2 - m12 * b1) / determ
    uw = y2 / nu
    ur = y1 / beta - uw * g1
    bz = 1.0 / nx
    bw = -g3 * bz
    br = (g3 * g1 - g2) * bz
    ur, uw, br, bw, bz = (jnp.broadcast_to(x, (S, LANES)) for x in (ur, uw, br, bw, bz))
    for d in range(parts):
        for m in range(own):
            for ct in range(tiles):
                at = slice((d * tiles + ct) * LANES, (d * tiles + ct + 1) * LANES)
                base = (d * own + m) * per + ct * S
                r = rhs_ref[m, :, at]
                w = w_ref[d, m, ct * S : (ct + 1) * S, :]
                update_ref[m, :, at] = ur * r + uw * w
                basis_ref[m, :, at] = br * r + bw * w + bz * got_ref[base : base + S, :]


def local(rhs, diffusivity, jac_coef, coef_index, row_mode, col_mode, multiplicity):
    parts = lax.axis_size("modes")
    own, _, total = rhs.shape
    n = own * parts
    cells = total // parts
    tiles = cells // LANES
    plane = GROUP // own
    sds = jax.ShapeDtypeStruct
    smem = pl.BlockSpec(memory_space=pltpu.SMEM)
    index = lax.axis_index("modes")
    place = jnp.stack([index // plane, index % plane]).astype(jnp.int32)

    early = (3 * tiles + 3) // 4
    block = (plane, own, early * S, LANES)

    def across(arrays):
        lead, rows = len(arrays), arrays[0].shape[2]
        come = [arrays[0]]
        for q in range(1, lead):
            come.append(lax.ppermute(arrays[q], "modes", [(i, i ^ (q * plane)) for i in range(parts)]))
        relayed = pl.pallas_call(
            functools.partial(relay_kernel, own),
            out_shape=[sds((lead, own, rows, LANES), F32)] * plane,
            in_specs=[smem] + [VMEM] * lead,
            out_specs=[VMEM] * plane,
            compiler_params=PARAMS,
            cost_estimate=pl.CostEstimate(flops=10**11, bytes_accessed=1 << 20, transcendentals=0),
            name="relay",
        )(place, *come)
        out = [relayed[0]]
        for k in range(1, plane):
            out.append(lax.ppermute(relayed[k], "modes", [(i, i ^ k) for i in range(parts)]))
        return out, relayed[0]

    late_send, *early_send = pl.pallas_call(
        functools.partial(arrange_kernel, parts, early),
        out_shape=[sds((n, tiles + 1 - early, S, LANES), F32)] + [sds(block, F32)] * (parts // plane),
        in_specs=[smem, VMEM],
        out_specs=[VMEM] * (1 + parts // plane),
        compiler_params=PARAMS,
        name="arrange",
    )(place, rhs)
    near, relayed = across(early_send)
    vector = lax.all_to_all(late_send, "modes", split_axis=0, concat_axis=0, tiled=True)

    edge = (NCOEF, S, S, LANES)
    head, tail = pl.pallas_call(
        pack_kernel,
        grid=(1,),
        out_shape=[sds((NCOEF, S // 4, S, LANES), F32)] * 2,
        in_specs=[
            pl.BlockSpec(edge, lambda g: (0, 0, 0, 0)),
            pl.BlockSpec(edge, lambda g: (0, 0, 0, tiles - 1)),
            pl.BlockSpec(memory_space=pl.ANY),
        ],
        compiler_params=PARAMS,
        name="pack",
    )(jac_coef, jac_coef, relayed)
    up = [(i, (i + 1) % parts) for i in range(parts)]
    down = [(j, i) for i, j in up]
    after = lax.ppermute(head, "modes", down)
    before = lax.ppermute(tail, "modes", up)
    coupling, stencil = pl.pallas_call(
        functools.partial(coupling_kernel, n),
        out_shape=[sds((NCOEF * n, 3 * n), BF16), sds((4 * LANES, LANES), BF16)],
        in_specs=[VMEM] * 4 + [pl.BlockSpec(memory_space=pl.ANY)],
        out_specs=[VMEM] * 2,
        compiler_params=PARAMS,
        name="coupling",
    )(*(x.reshape(1, -1) for x in (coef_index, row_mode, col_mode, multiplicity)), relayed)

    jac = jac_coef.reshape(NCOEF * S, S, cells)
    field = (tiles + 1, S, n, LANES)
    work = [
        pltpu.VMEM((2, 3 * n, S * LANES), BF16),
        pltpu.VMEM((2, S * n, 4 * LANES), BF16),
        pltpu.VMEM((2, NCOEF * n, S * LANES), F32),
        pltpu.VMEM((2, S * n, LANES), F32),
    ]
    late = tiles + 1 - early
    v_late, a_late = pl.pallas_call(
        functools.partial(late_kernel, n, early),
        out_shape=[sds((late, S, n, LANES), F32), sds((max(late - 1, 1), S, n, LANES), F32)],
        in_specs=[VMEM] * 3,
        out_specs=[VMEM] * 2,
        scratch_shapes=[work[0], work[2]],
        compiler_params=PARAMS,
        cost_estimate=pl.CostEstimate(flops=2 * 10**9, bytes_accessed=1 << 20, transcendentals=0),
        name="late",
    )(jac, coupling, vector.reshape(n * late * S, LANES))
    v, w, sums, *w_send = pl.pallas_call(
        functools.partial(first_kernel, n, tiles, plane),
        out_shape=[sds(field, F32), sds((tiles, S, n, LANES), F32), sds((16, LANES), F32)]
        + [sds((plane, own, tiles * S, LANES), F32)] * (n // GROUP),
        in_specs=[smem] * 2 + [VMEM] * (5 + plane),
        out_specs=[VMEM] * (3 + n // GROUP),
        scratch_shapes=[pltpu.VMEM((parts, own, early * S, LANES), F32)] + work,
        compiler_params=PARAMS,
        name="first",
    )(place, diffusivity, v_late, a_late, jac, coupling, stencil, *near)
    edges = pl.pallas_call(
        unpack_kernel,
        out_shape=sds((NCOEF * S, S, LANES), F32),
        in_specs=[VMEM] * 2 + [pl.BlockSpec(memory_space=pl.ANY)],
        out_specs=VMEM,
        compiler_params=PARAMS,
        name="unpack",
    )(after, before, sums)
    w_own, _ = across(w_send)

    z_send = pl.pallas_call(
        functools.partial(second_kernel, n, tiles),
        out_shape=sds((n * (tiles * S + 1), LANES), F32),
        in_specs=[smem] + [VMEM] * 7,
        out_specs=VMEM,
        scratch_shapes=[pltpu.VMEM((tiles, S, n, LANES), F32), pltpu.VMEM((S, n, LANES), F32)] + work,
        compiler_params=PARAMS,
        cost_estimate=pl.CostEstimate(flops=10**10, bytes_accessed=16 << 20, transcendentals=0),
        name="second",
    )(diffusivity, v, w, sums, jac, edges, coupling, stencil)
    line = (tiles * S + 1) * LANES
    got = lax.all_to_all(z_send.reshape(n, 1, line), "modes", split_axis=0, concat_axis=0, tiled=True)

    w_all = pl.pallas_call(
        gather_kernel,
        out_shape=sds((parts, own, tiles * S, LANES), F32),
        in_specs=[smem] + [VMEM] * plane,
        out_specs=VMEM,
        compiler_params=PARAMS,
        name="gather",
    )(place, *w_own)
    update, basis_next = pl.pallas_call(
        functools.partial(combine_kernel, parts, tiles),
        out_shape=[sds(rhs.shape, F32)] * 2,
        in_specs=[VMEM] * 3,
        out_specs=[VMEM] * 2,
        compiler_params=PARAMS,
        name="combine",
    )(rhs, got.reshape(n * (tiles * S + 1), LANES), w_all)
    return (update, basis_next)


def solution(mesh):
    return jax.shard_map(
        local,
        mesh=mesh,
        in_specs=(
            P(("groups", "modes"), None, None),
            P(),
            P(None, None, None, "modes"),
            P(),
            P(),
            P(),
            P(),
        ),
        out_specs=(P(("groups", "modes"), None, None), P(("groups", "modes"), None, None)),
        check_vma=False,
    )
```

```python
import functools

import jax
import jax.numpy as jnp
from jax import lax
from jax.experimental import pallas as pl
from jax.experimental.pallas import tpu as pltpu
from jax.sharding import PartitionSpec as P

NCOEF = 9
GY = 32
S = 8
LANES = 128
GROUP = 8
F32 = jnp.float32
BF16 = jnp.bfloat16
VMEM = pl.BlockSpec(memory_space=pltpu.VMEM)
PARAMS = pltpu.CompilerParams(vmem_limit_bytes=40 * 1024 * 1024)


def lane_iota():
    return lax.broadcasted_iota(jnp.int32, (S, LANES), 1)


def arrange_kernel(parts, early, place_ref, rhs_ref, out_ref, *refs):
    own, _, total = rhs_ref.shape
    cells = total // parts
    tiles = cells // LANES
    plane = GROUP // own
    low = lane_iota() < LANES // 2
    for q in range(parts // plane):
        base = jnp.bitwise_xor(place_ref[0], q) * plane
        for k in range(plane):
            for m in range(own):
                for ct in range(early):
                    at = pl.multiple_of((base + k) * cells + ct * LANES, LANES)
                    refs[q][k, m, ct * S : (ct + 1) * S, :] = rhs_ref[m, :, pl.ds(at, LANES)]
    for d in range(parts):
        after = ((d + 1) * cells) % total
        before = (d * cells - LANES) % total
        for m in range(own):
            for ct in range(early, tiles):
                at = d * cells + ct * LANES
                out_ref[d * own + m, ct - early] = rhs_ref[m, :, at : at + LANES]
            out_ref[d * own + m, tiles - early] = jnp.where(
                low, rhs_ref[m, :, after : after + LANES], rhs_ref[m, :, before : before + LANES]
            )


def pack_kernel(first_ref, last_ref, _, head_ref, tail_ref):
    piece = lane_iota() // GY
    for i in range(NCOEF):
        for q in range(S // 4):
            head = first_ref[i, q * 4]
            tail = pltpu.roll(last_ref[i, q * 4], GY, 1)
            for p in range(1, 4):
                head = jnp.where(piece == p, pltpu.roll(first_ref[i, q * 4 + p], GY * p, 1), head)
                moved = last_ref[i, q * 4 + p]
                if p < 3:
                    moved = pltpu.roll(moved, GY * (p + 1), 1)
                tail = jnp.where(piece == p, moved, tail)
            head_ref[i, q] = head
            tail_ref[i, q] = tail


def coupling_kernel(modes, coef_ref, row_ref, col_ref, mult_ref, _, out_ref, stencil_ref):
    rows, cols = out_ref.shape
    triples = coef_ref.shape[1]
    key = coef_ref[...] * modes + row_ref[...]
    weight = 0.25 * mult_ref[...].astype(F32)
    row = lax.broadcasted_iota(jnp.int32, (rows, triples), 0)
    left = jnp.where(row == key, weight, 0.0).astype(BF16)
    col = lax.rem(lax.broadcasted_iota(jnp.int32, (cols, triples), 0), modes)
    right = jnp.where(col == col_ref[...], 1.0, 0.0).astype(BF16)
    dense = lax.dot_general(left, right, (((1,), (1,)), ((), ())), preferred_element_type=F32)
    r = lax.broadcasted_iota(jnp.int32, (rows, cols), 0)
    c = lax.broadcasted_iota(jnp.int32, (rows, cols), 1)
    dense = dense + jnp.where(r == lax.rem(c, modes), 1.0, 0.0)
    high = dense.astype(BF16)
    low = (dense - high.astype(F32)).astype(BF16)
    out_ref[...] = jnp.where(c < 2 * modes, high.astype(F32), low.astype(F32)).astype(BF16)

    a = lax.broadcasted_iota(jnp.int32, (LANES, LANES), 0)
    b = lax.broadcasted_iota(jnp.int32, (LANES, LANES), 1)
    step = jnp.bitwise_and(a - b, GY - 1)
    same = (a // GY == b // GY) & ((step == 1) | (step == GY - 1))
    apart = jnp.abs(a - b)
    inner = jnp.where(apart == 0, 4.0, jnp.where(same | (apart == GY), -1.0, 0.0)).astype(BF16)
    outer = jnp.where(apart == LANES - GY, -1.0, 0.0).astype(BF16)
    stencil_ref[0:LANES] = inner
    stencil_ref[LANES : 2 * LANES] = inner
    stencil_ref[2 * LANES : 3 * LANES] = outer
    stencil_ref[3 * LANES :] = outer


def split(x):
    high = x.astype(BF16)
    return high, (x - high.astype(F32)).astype(BF16)


def ratio(a, b):
    return jnp.where(b > 0.0, a / jnp.where(b > 0.0, b, 1.0), 0.0)


def unpack_kernel(next_ref, prev_ref, _, out_ref):
    lane = lane_iota()
    for i in range(NCOEF):
        for q in range(S // 4):
            after, before = next_ref[i, q], prev_ref[i, q]
            for p in range(4):
                a = after if p == 0 else pltpu.roll(after, LANES - GY * p, 1)
                b = before if p == 3 else pltpu.roll(before, LANES - GY - GY * p, 1)
                out_ref[i * S + q * 4 + p] = jnp.where(lane < LANES // 2, a, b)


def mix(get, ct, slot, coup_ref, vs_ref, mx_ref):
    n = vs_ref.shape[1] // 3

    def step(first):
        for t in (first, first + 1):
            at = slice(t * LANES, (t + 1) * LANES)
            high, low = split(get(ct, t))
            vs_ref[slot, 0:n, at] = high
            vs_ref[slot, n : 2 * n, at] = low
            vs_ref[slot, 2 * n : 3 * n, at] = high
        at = slice(first * LANES, (first + 2) * LANES)
        mx_ref[slot, :, at] = jnp.dot(coup_ref[...], vs_ref[slot, :, at], preferred_element_type=F32)

    return [functools.partial(step, first) for first in range(0, S, 2)]


def spread(get, ct, slot, every, stencil_ref, xs_ref, bs_ref):
    n = bs_ref.shape[1] // S
    before, after = (ct - 1) % every, (ct + 1) % every

    def fill(first):
        wide = lax.broadcasted_iota(jnp.int32, (n, LANES), 1) < LANES // 2
        for t in (first, first + 1):
            to = slice(t * n, (t + 1) * n)
            high, low = split(get(ct, t))
            xs_ref[slot, to, 0:LANES] = high
            xs_ref[slot, to, LANES : 2 * LANES] = low
            high, low = split(jnp.where(wide, get(after, t), get(before, t)))
            xs_ref[slot, to, 2 * LANES : 3 * LANES] = high
            xs_ref[slot, to, 3 * LANES :] = low
        if first + 2 == S:
            bs_ref[slot] = jnp.dot(xs_ref[slot], stencil_ref[...], preferred_element_type=F32)

    return [functools.partial(fill, first) for first in range(0, S, 2)]


def run(steps):
    for step in steps:
        step()


def react(n, jac, slot, mx_ref, finish, steps=()):
    steps = list(steps)
    for kb in range(0, n, 32):
        acc = [None] * 32
        for i in range(NCOEF):
            if steps:
                steps.pop(0)()
            for t in range(S):
                m = [
                    mx_ref[slot, i * n + kb + kt * 8 : i * n + kb + kt * 8 + 8, t * LANES : (t + 1) * LANES]
                    for kt in range(4)
                ]
                for s in range(S):
                    j = jnp.broadcast_to(jac(i * S + s, t), (8, LANES))
                    for kt in range(4):
                        term = j * m[kt]
                        at = s * 4 + kt
                        acc[at] = term if acc[at] is None else acc[at] + term
        for s in range(S):
            for kt in range(4):
                finish(s, kb + kt * 8, acc[s * 4 + kt])
    run(steps)


def tile_of(jac_ref, ct):
    return lambda row, t: jac_ref[row, t : t + 1, ct * LANES : (ct + 1) * LANES]


def spread_sum(x):
    return jnp.broadcast_to(jnp.sum(x, axis=(0, 1), keepdims=True), (8, LANES))


class Sums:
    def __init__(self):
        self.parts = {}

    def add(self, name, at, term):
        mine = self.parts.setdefault(name, {})
        mine[at % 4] = mine[at % 4] + term if at % 4 in mine else term

    def partial(self, name):
        return functools.reduce(lambda a, b: a + b, self.parts[name].values())

    def total(self, name):
        return spread_sum(self.partial(name))


def late_kernel(n, early, jac_ref, coup_ref, r_ref, v_ref, a_ref, vs_ref, mx_ref):
    late = v_ref.shape[0]
    for ct in range(late):
        for s in range(S):
            v_ref[ct, s] = r_ref[pl.ds(ct * S + s, n, stride=late * S), :]

    def get(ct, t):
        return v_ref[ct, t]

    def finisher(ct):
        def finish(s, k, acc):
            a_ref[ct, s, k : k + 8] = acc

        return finish

    if late > 1:
        run(mix(get, 0, 0, coup_ref, vs_ref, mx_ref))
    for ct in range(late - 1):
        steps = mix(get, ct + 1, (ct + 1) % 2, coup_ref, vs_ref, mx_ref) if ct + 2 < late else []
        react(n, tile_of(jac_ref, early + ct), ct % 2, mx_ref, finisher(ct), steps)


def first_kernel(n, tiles, plane, place_ref, dif_ref, vl_ref, al_ref, jac_ref, coup_ref, stencil_ref, *refs):
    every = tiles + 1
    near_refs, (v_ref, w_ref, sum_ref), refs = refs[:plane], refs[plane : plane + 3], refs[plane + 3 :]
    send_refs, (gather_ref, vs_ref, xs_ref, mx_ref, bs_ref) = refs[: n // GROUP], refs[n // GROUP :]
    early = every - vl_ref.shape[0]
    gather_kernel(place_ref, *near_refs, gather_ref)
    flat = gather_ref.reshape(n * early * S, LANES)
    for ct in range(early):
        for s in range(S):
            v_ref[ct, s] = flat[pl.ds(ct * S + s, n, stride=early * S), :]
    for ct in range(early, every):
        v_ref[ct] = vl_ref[ct - early]
    sums = Sums()

    def get(ct, t):
        return v_ref[ct, t]

    def finisher(ct, slot):
        def finish(s, k, acc):
            w = dif_ref[s] * bs_ref[slot, s * n + k : s * n + k + 8] - acc
            w_ref[ct, s, k : k + 8] = w
            v = v_ref[ct, s, k : k + 8]
            sums.add("rr", k // 8, v * v)
            sums.add("rw", k // 8, v * w)

        return finish

    def prepare(ct):
        return mix(get, ct, ct % 2, coup_ref, vs_ref, mx_ref) + sides(ct, ct % 2)

    def sides(ct, slot):
        return spread(get, ct, slot, every, stencil_ref, xs_ref, bs_ref)

    def close(ct, slot):
        for s in range(S):
            for k in range(0, n, 8):
                finisher(ct, slot)(s, k, al_ref[ct - early, s, k : k + 8])

    def pack(ct):
        for q in range(n // GROUP):
            at = pl.multiple_of(jnp.bitwise_xor(place_ref[0], q) * GROUP, GROUP)
            flat = send_refs[q].reshape(GROUP * tiles * S, LANES)
            for s in range(S):
                flat[pl.ds(ct * S + s, GROUP, stride=tiles * S), :] = w_ref[ct, s, pl.ds(at, GROUP)]

    spare = early % 2
    rest = []
    for ct in range(early, tiles):
        rest += sides(ct, spare) + [functools.partial(close, ct, spare), functools.partial(pack, ct)]
    run(prepare(0))
    for ct in range(early):
        steps = prepare(ct + 1) if ct + 1 < early else rest
        react(n, tile_of(jac_ref, ct), ct % 2, mx_ref, finisher(ct, ct % 2), steps)
        pack(ct)
    sum_ref[0:8] = sums.partial("rr")
    sum_ref[8:16] = sums.partial("rw")


def second_kernel(
    n,
    tiles,
    dif_ref,
    v_ref,
    w_ref,
    sum_ref,
    jac_ref,
    edge_ref,
    coup_ref,
    stencil_ref,
    out_ref,
    z_ref,
    wh_ref,
    vs_ref,
    xs_ref,
    mx_ref,
    bs_ref,
):
    every = tiles + 1
    per = tiles * S + 1
    rr, rw = spread_sum(sum_ref[0:8]), spread_sum(sum_ref[8:16])
    c1 = ratio(rw, rr)
    sums = Sums()

    def get_v(ct, t):
        return v_ref[ct, t]

    def get_w(ct, t):
        return w_ref[ct, t] if ct < tiles else wh_ref[t]

    def finish_edge(s, k, acc):
        wh_ref[s, k : k + 8] = dif_ref[s] * bs_ref[0, s * n + k : s * n + k + 8] - acc

    def finisher(ct, slot):
        def finish(s, k, acc):
            z = dif_ref[s] * bs_ref[slot, s * n + k : s * n + k + 8] - acc
            v, w = v_ref[ct, s, k : k + 8], w_ref[ct, s, k : k + 8]
            z_ref[ct, s, k : k + 8] = z
            out_ref[pl.ds(k * per + ct * S + s, 8, stride=per), :] = z
            u = w - c1 * v
            sums.add("uu", k // 8, u * u)
            sums.add("ur", k // 8, u * v)
            sums.add("uz", k // 8, u * z)
            sums.add("rz", k // 8, v * z)

        return finish

    order = list(range(1, tiles)) + [0]

    def mixed(get, ct, slot):
        return mix(get, ct, slot, coup_ref, vs_ref, mx_ref)

    def sides(get, ct, slot):
        return spread(get, ct, slot, every, stencil_ref, xs_ref, bs_ref)

    run(mixed(get_v, tiles, 0) + sides(get_v, tiles, 0))
    inside = tiles > 2
    steps = mixed(get_w, order[0], 1) + (sides(get_w, order[0], 1) if inside else [])
    react(n, tile_of(edge_ref, 0), 0, mx_ref, finish_edge, steps)
    if not inside:
        run(sides(get_w, order[0], 1))
    for at, ct in enumerate(order):
        slot = (at + 1) % 2
        steps = []
        if at + 1 < tiles:
            steps = mixed(get_w, order[at + 1], 1 - slot) + sides(get_w, order[at + 1], 1 - slot)
        react(n, tile_of(jac_ref, ct), slot, mx_ref, finisher(ct, slot), steps)
    uu, ur, uz, rz = (sums.total(name) for name in ("uu", "ur", "uz", "rz"))
    c2 = ratio(rz, rr)
    c3 = ratio(uz - c2 * ur, uu)
    for ct in range(tiles):
        for s in range(S):
            for k in range(0, n, 8):
                v, w, z = (ref[ct, s, k : k + 8] for ref in (v_ref, w_ref, z_ref))
                x = (z - c2 * v) - c3 * (w - c1 * v)
                sums.add("xx", k // 8, x * x)
    xx = sums.total("xx")
    lane = lane_iota()
    tile = jnp.zeros((8, LANES), F32)
    for q, value in enumerate((rr, c1, uu, c2, c3, xx)):
        tile = jnp.where(lane == q, value, tile)
    for k in range(0, n, 8):
        out_ref[pl.ds(k * per + tiles * S, 8, stride=per), :] = tile


def relay_kernel(own, place_ref, *refs):
    parts = GROUP // own
    count = len(refs) - parts
    for k in range(parts):
        at = jnp.bitwise_xor(place_ref[1], k)
        for q in range(count):
            refs[count + k][q] = refs[q][at]


def gather_kernel(place_ref, *refs):
    near_refs, out_ref = refs[:-1], refs[-1]
    plane = len(near_refs)
    for k in range(plane):
        for q in range(near_refs[k].shape[0]):
            d = jnp.bitwise_xor(place_ref[0], q) * plane + jnp.bitwise_xor(place_ref[1], k)
            out_ref[d] = near_refs[k][q]


def combine_kernel(parts, tiles, rhs_ref, got_ref, w_ref, update_ref, basis_ref):
    own = rhs_ref.shape[0]
    per = tiles * S + 1
    stats = got_ref[pl.ds(tiles * S, parts, stride=own * per), :]

    def stat(q):
        return jnp.broadcast_to(stats[:, q : q + 1], (parts, LANES))

    def add(x):
        return jnp.sum(x, axis=0, keepdims=True)

    rr, c1, uu, c2, c3, xx = (stat(q) for q in range(6))
    all_rr = add(rr)
    g1 = add(rr * c1) / all_rr
    g2 = add(rr * c2) / all_rr
    e1, e2 = c1 - g1, c2 - g2
    all_uu = add(uu + e1 * e1 * rr)
    g3 = add(c3 * uu + e1 * e2 * rr) / all_uu
    e3 = c3 - g3
    f = e2 - g3 * e1
    all_xx = add(xx + e3 * e3 * uu + f * f * rr)
    beta, nu, nx = jnp.sqrt(all_rr), jnp.sqrt(all_uu), jnp.sqrt(all_xx)
    h11 = 1.0 + g1
    h21 = nu / beta
    h12 = (g2 - g1 * g1) * beta / nu
    h22 = 1.0 + (g3 - g1)
    h32 = nx / nu
    m11 = h11 * h11 + h21 * h21
    m12 = h11 * h12 + h21 * h22
    m22 = h12 * h12 + h22 * h22 + h32 * h32
    b1, b2 = beta * h11, beta * h12
    determ = m11 * m22 - m12 * m12
    y1 = (m22 * b1 - m12 * b2) / determ
    y2 = (m11 * b2 - m12 * b1) / determ
    uw = y2 / nu
    ur = y1 / beta - uw * g1
    bz = 1.0 / nx
    bw = -g3 * bz
    br = (g3 * g1 - g2) * bz
    ur, uw, br, bw, bz = (jnp.broadcast_to(x, (S, LANES)) for x in (ur, uw, br, bw, bz))
    for d in range(parts):
        for m in range(own):
            for ct in range(tiles):
                at = slice((d * tiles + ct) * LANES, (d * tiles + ct + 1) * LANES)
                base = (d * own + m) * per + ct * S
                r = rhs_ref[m, :, at]
                w = w_ref[d, m, ct * S : (ct + 1) * S, :]
                update_ref[m, :, at] = ur * r + uw * w
                basis_ref[m, :, at] = br * r + bw * w + bz * got_ref[base : base + S, :]


def local(rhs, diffusivity, jac_coef, coef_index, row_mode, col_mode, multiplicity):
    parts = lax.axis_size("modes")
    own, _, total = rhs.shape
    n = own * parts
    cells = total // parts
    tiles = cells // LANES
    plane = GROUP // own
    sds = jax.ShapeDtypeStruct
    smem = pl.BlockSpec(memory_space=pltpu.SMEM)
    index = lax.axis_index("modes")
    place = jnp.stack([index // plane, index % plane]).astype(jnp.int32)

    early = (3 * tiles + 3) // 4
    block = (plane, own, early * S, LANES)

    def across(arrays):
        lead, rows = len(arrays), arrays[0].shape[2]
        come = [arrays[0]]
        for q in range(1, lead):
            come.append(lax.ppermute(arrays[q], "modes", [(i, i ^ (q * plane)) for i in range(parts)]))
        relayed = pl.pallas_call(
            functools.partial(relay_kernel, own),
            out_shape=[sds((lead, own, rows, LANES), F32)] * plane,
            in_specs=[smem] + [VMEM] * lead,
            out_specs=[VMEM] * plane,
            compiler_params=PARAMS,
            cost_estimate=pl.CostEstimate(flops=10**11, bytes_accessed=1 << 20, transcendentals=0),
            name="relay",
        )(place, *come)
        out = [relayed[0]]
        for k in range(1, plane):
            out.append(lax.ppermute(relayed[k], "modes", [(i, i ^ k) for i in range(parts)]))
        return out, relayed[0]

    late_send, *early_send = pl.pallas_call(
        functools.partial(arrange_kernel, parts, early),
        out_shape=[sds((n, tiles + 1 - early, S, LANES), F32)] + [sds(block, F32)] * (parts // plane),
        in_specs=[smem, VMEM],
        out_specs=[VMEM] * (1 + parts // plane),
        compiler_params=PARAMS,
        name="arrange",
    )(place, rhs)
    near, relayed = across(early_send)
    vector = lax.all_to_all(late_send, "modes", split_axis=0, concat_axis=0, tiled=True)

    edge = (NCOEF, S, S, LANES)
    head, tail = pl.pallas_call(
        pack_kernel,
        grid=(1,),
        out_shape=[sds((NCOEF, S // 4, S, LANES), F32)] * 2,
        in_specs=[
            pl.BlockSpec(edge, lambda g: (0, 0, 0, 0)),
            pl.BlockSpec(edge, lambda g: (0, 0, 0, tiles - 1)),
            pl.BlockSpec(memory_space=pl.ANY),
        ],
        compiler_params=PARAMS,
        name="pack",
    )(jac_coef, jac_coef, relayed)
    up = [(i, (i + 1) % parts) for i in range(parts)]
    down = [(j, i) for i, j in up]
    after = lax.ppermute(head, "modes", down)
    before = lax.ppermute(tail, "modes", up)
    coupling, stencil = pl.pallas_call(
        functools.partial(coupling_kernel, n),
        out_shape=[sds((NCOEF * n, 3 * n), BF16), sds((4 * LANES, LANES), BF16)],
        in_specs=[VMEM] * 4 + [pl.BlockSpec(memory_space=pl.ANY)],
        out_specs=[VMEM] * 2,
        compiler_params=PARAMS,
        name="coupling",
    )(*(x.reshape(1, -1) for x in (coef_index, row_mode, col_mode, multiplicity)), relayed)

    jac = jac_coef.reshape(NCOEF * S, S, cells)
    field = (tiles + 1, S, n, LANES)
    work = [
        pltpu.VMEM((2, 3 * n, S * LANES), BF16),
        pltpu.VMEM((2, S * n, 4 * LANES), BF16),
        pltpu.VMEM((2, NCOEF * n, S * LANES), F32),
        pltpu.VMEM((2, S * n, LANES), F32),
    ]
    late = tiles + 1 - early
    v_late, a_late = pl.pallas_call(
        functools.partial(late_kernel, n, early),
        out_shape=[sds((late, S, n, LANES), F32), sds((max(late - 1, 1), S, n, LANES), F32)],
        in_specs=[VMEM] * 3,
        out_specs=[VMEM] * 2,
        scratch_shapes=[work[0], work[2]],
        compiler_params=PARAMS,
        cost_estimate=pl.CostEstimate(flops=2 * 10**9, bytes_accessed=1 << 20, transcendentals=0),
        name="late",
    )(jac, coupling, vector.reshape(n * late * S, LANES))
    v, w, sums, *w_send = pl.pallas_call(
        functools.partial(first_kernel, n, tiles, plane),
        out_shape=[sds(field, F32), sds((tiles, S, n, LANES), F32), sds((16, LANES), F32)]
        + [sds((plane, own, tiles * S, LANES), F32)] * (n // GROUP),
        in_specs=[smem] * 2 + [VMEM] * (5 + plane),
        out_specs=[VMEM] * (3 + n // GROUP),
        scratch_shapes=[pltpu.VMEM((parts, own, early * S, LANES), F32)] + work,
        compiler_params=PARAMS,
        name="first",
    )(place, diffusivity, v_late, a_late, jac, coupling, stencil, *near)
    edges = pl.pallas_call(
        unpack_kernel,
        out_shape=sds((NCOEF * S, S, LANES), F32),
        in_specs=[VMEM] * 2 + [pl.BlockSpec(memory_space=pl.ANY)],
        out_specs=VMEM,
        compiler_params=PARAMS,
        name="unpack",
    )(after, before, sums)
    w_own, _ = across(w_send)

    z_send = pl.pallas_call(
        functools.partial(second_kernel, n, tiles),
        out_shape=sds((n * (tiles * S + 1), LANES), F32),
        in_specs=[smem] + [VMEM] * 7,
        out_specs=VMEM,
        scratch_shapes=[pltpu.VMEM((tiles, S, n, LANES), F32), pltpu.VMEM((S, n, LANES), F32)] + work,
        compiler_params=PARAMS,
        cost_estimate=pl.CostEstimate(flops=10**10, bytes_accessed=16 << 20, transcendentals=0),
        name="second",
    )(diffusivity, v, w, sums, jac, edges, coupling, stencil)
    line = (tiles * S + 1) * LANES
    got = lax.all_to_all(z_send.reshape(n, 1, line), "modes", split_axis=0, concat_axis=0, tiled=True)

    w_all = pl.pallas_call(
        gather_kernel,
        out_shape=sds((parts, own, tiles * S, LANES), F32),
        in_specs=[smem] + [VMEM] * plane,
        out_specs=VMEM,
        compiler_params=PARAMS,
        name="gather",
    )(place, *w_own)
    update, basis_next = pl.pallas_call(
        functools.partial(combine_kernel, parts, tiles),
        out_shape=[sds(rhs.shape, F32)] * 2,
        in_specs=[VMEM] * 3,
        out_specs=[VMEM] * 2,
        compiler_params=PARAMS,
        name="combine",
    )(rhs, got.reshape(n * (tiles * S + 1), LANES), w_all)
    return (update, basis_next)


def solution(mesh):
    return jax.shard_map(
        local,
        mesh=mesh,
        in_specs=(
            P(("groups", "modes"), None, None),
            P(),
            P(None, None, None, "modes"),
            P(),
            P(),
            P(),
            P(),
        ),
        out_specs=(P(("groups", "modes"), None, None), P(("groups", "modes"), None, None)),
        check_vma=False,
    )
```

```python
import functools

import jax
import jax.numpy as jnp
from jax import lax
from jax.experimental import pallas as pl
from jax.experimental.pallas import tpu as pltpu
from jax.sharding import PartitionSpec as P

NCOEF = 9
GY = 32
S = 8
LANES = 128
GROUP = 8
F32 = jnp.float32
BF16 = jnp.bfloat16
VMEM = pl.BlockSpec(memory_space=pltpu.VMEM)
PARAMS = pltpu.CompilerParams(vmem_limit_bytes=40 * 1024 * 1024)


def lane_iota():
    return lax.broadcasted_iota(jnp.int32, (S, LANES), 1)


def arrange_kernel(parts, early, place_ref, rhs_ref, out_ref, *refs):
    own, _, total = rhs_ref.shape
    cells = total // parts
    tiles = cells // LANES
    plane = GROUP // own
    low = lane_iota() < LANES // 2
    for q in range(parts // plane):
        base = jnp.bitwise_xor(place_ref[0], q) * plane
        for k in range(plane):
            for m in range(own):
                for ct in range(early):
                    at = pl.multiple_of((base + k) * cells + ct * LANES, LANES)
                    refs[q][k, m, ct * S : (ct + 1) * S, :] = rhs_ref[m, :, pl.ds(at, LANES)]
    for d in range(parts):
        after = ((d + 1) * cells) % total
        before = (d * cells - LANES) % total
        for m in range(own):
            for ct in range(early, tiles):
                at = d * cells + ct * LANES
                out_ref[d * own + m, ct - early] = rhs_ref[m, :, at : at + LANES]
            out_ref[d * own + m, tiles - early] = jnp.where(
                low, rhs_ref[m, :, after : after + LANES], rhs_ref[m, :, before : before + LANES]
            )


def pack_kernel(first_ref, last_ref, _, head_ref, tail_ref):
    piece = lane_iota() // GY
    for i in range(NCOEF):
        for q in range(S // 4):
            head = first_ref[i, q * 4]
            tail = pltpu.roll(last_ref[i, q * 4], GY, 1)
            for p in range(1, 4):
                head = jnp.where(piece == p, pltpu.roll(first_ref[i, q * 4 + p], GY * p, 1), head)
                moved = last_ref[i, q * 4 + p]
                if p < 3:
                    moved = pltpu.roll(moved, GY * (p + 1), 1)
                tail = jnp.where(piece == p, moved, tail)
            head_ref[i, q] = head
            tail_ref[i, q] = tail


def coupling_kernel(modes, coef_ref, row_ref, col_ref, mult_ref, _, out_ref, stencil_ref):
    rows, cols = out_ref.shape
    triples = coef_ref.shape[1]
    key = coef_ref[...] * modes + row_ref[...]
    weight = 0.25 * mult_ref[...].astype(F32)
    row = lax.broadcasted_iota(jnp.int32, (rows, triples), 0)
    left = jnp.where(row == key, weight, 0.0).astype(BF16)
    col = lax.rem(lax.broadcasted_iota(jnp.int32, (cols, triples), 0), modes)
    right = jnp.where(col == col_ref[...], 1.0, 0.0).astype(BF16)
    dense = lax.dot_general(left, right, (((1,), (1,)), ((), ())), preferred_element_type=F32)
    r = lax.broadcasted_iota(jnp.int32, (rows, cols), 0)
    c = lax.broadcasted_iota(jnp.int32, (rows, cols), 1)
    dense = dense + jnp.where(r == lax.rem(c, modes), 1.0, 0.0)
    high = dense.astype(BF16)
    low = (dense - high.astype(F32)).astype(BF16)
    out_ref[...] = jnp.where(c < 2 * modes, high.astype(F32), low.astype(F32)).astype(BF16)

    a = lax.broadcasted_iota(jnp.int32, (LANES, LANES), 0)
    b = lax.broadcasted_iota(jnp.int32, (LANES, LANES), 1)
    step = jnp.bitwise_and(a - b, GY - 1)
    same = (a // GY == b // GY) & ((step == 1) | (step == GY - 1))
    apart = jnp.abs(a - b)
    inner = jnp.where(apart == 0, 4.0, jnp.where(same | (apart == GY), -1.0, 0.0)).astype(BF16)
    outer = jnp.where(apart == LANES - GY, -1.0, 0.0).astype(BF16)
    stencil_ref[0:LANES] = inner
    stencil_ref[LANES : 2 * LANES] = inner
    stencil_ref[2 * LANES : 3 * LANES] = outer
    stencil_ref[3 * LANES :] = outer


def split(x):
    high = x.astype(BF16)
    return high, (x - high.astype(F32)).astype(BF16)


def ratio(a, b):
    return jnp.where(b > 0.0, a / jnp.where(b > 0.0, b, 1.0), 0.0)


def unpack_kernel(next_ref, prev_ref, _, out_ref):
    lane = lane_iota()
    for i in range(NCOEF):
        for q in range(S // 4):
            after, before = next_ref[i, q], prev_ref[i, q]
            for p in range(4):
                a = after if p == 0 else pltpu.roll(after, LANES - GY * p, 1)
                b = before if p == 3 else pltpu.roll(before, LANES - GY - GY * p, 1)
                out_ref[i * S + q * 4 + p] = jnp.where(lane < LANES // 2, a, b)


def mix(get, ct, slot, coup_ref, vs_ref, mx_ref):
    n = vs_ref.shape[1] // 3

    def step(first):
        for t in (first, first + 1):
            at = slice(t * LANES, (t + 1) * LANES)
            high, low = split(get(ct, t))
            vs_ref[slot, 0:n, at] = high
            vs_ref[slot, n : 2 * n, at] = low
            vs_ref[slot, 2 * n : 3 * n, at] = high
        at = slice(first * LANES, (first + 2) * LANES)
        mx_ref[slot, :, at] = jnp.dot(coup_ref[...], vs_ref[slot, :, at], preferred_element_type=F32)

    return [functools.partial(step, first) for first in range(0, S, 2)]


def spread(get, ct, slot, every, stencil_ref, xs_ref, bs_ref):
    n = bs_ref.shape[1] // S
    before, after = (ct - 1) % every, (ct + 1) % every

    def fill(first):
        wide = lax.broadcasted_iota(jnp.int32, (n, LANES), 1) < LANES // 2
        for t in (first, first + 1):
            to = slice(t * n, (t + 1) * n)
            high, low = split(get(ct, t))
            xs_ref[slot, to, 0:LANES] = high
            xs_ref[slot, to, LANES : 2 * LANES] = low
            high, low = split(jnp.where(wide, get(after, t), get(before, t)))
            xs_ref[slot, to, 2 * LANES : 3 * LANES] = high
            xs_ref[slot, to, 3 * LANES :] = low
        if first + 2 == S:
            bs_ref[slot] = jnp.dot(xs_ref[slot], stencil_ref[...], preferred_element_type=F32)

    return [functools.partial(fill, first) for first in range(0, S, 2)]


def run(steps):
    for step in steps:
        step()


def react(n, jac, slot, mx_ref, finish, steps=()):
    steps = list(steps)
    for kb in range(0, n, 32):
        acc = [None] * 32
        for i in range(NCOEF):
            if steps:
                steps.pop(0)()
            for t in range(S):
                m = [
                    mx_ref[slot, i * n + kb + kt * 8 : i * n + kb + kt * 8 + 8, t * LANES : (t + 1) * LANES]
                    for kt in range(4)
                ]
                for s in range(S):
                    j = jnp.broadcast_to(jac(i * S + s, t), (8, LANES))
                    for kt in range(4):
                        term = j * m[kt]
                        at = s * 4 + kt
                        acc[at] = term if acc[at] is None else acc[at] + term
        for s in range(S):
            for kt in range(4):
                finish(s, kb + kt * 8, acc[s * 4 + kt])
    run(steps)


def tile_of(jac_ref, ct):
    return lambda row, t: jac_ref[row, t : t + 1, ct * LANES : (ct + 1) * LANES]


def spread_sum(x):
    return jnp.broadcast_to(jnp.sum(x, axis=(0, 1), keepdims=True), (8, LANES))


class Sums:
    def __init__(self):
        self.parts = {}

    def add(self, name, at, term):
        mine = self.parts.setdefault(name, {})
        mine[at % 4] = mine[at % 4] + term if at % 4 in mine else term

    def partial(self, name):
        return functools.reduce(lambda a, b: a + b, self.parts[name].values())

    def total(self, name):
        return spread_sum(self.partial(name))


def late_kernel(n, early, jac_ref, coup_ref, r_ref, v_ref, a_ref, vs_ref, mx_ref):
    late = v_ref.shape[0]
    for ct in range(late):
        for s in range(S):
            v_ref[ct, s] = r_ref[pl.ds(ct * S + s, n, stride=late * S), :]

    def get(ct, t):
        return v_ref[ct, t]

    def finisher(ct):
        def finish(s, k, acc):
            a_ref[ct, s, k : k + 8] = acc

        return finish

    if late > 1:
        run(mix(get, 0, 0, coup_ref, vs_ref, mx_ref))
    for ct in range(late - 1):
        steps = mix(get, ct + 1, (ct + 1) % 2, coup_ref, vs_ref, mx_ref) if ct + 2 < late else []
        react(n, tile_of(jac_ref, early + ct), ct % 2, mx_ref, finisher(ct), steps)


def first_kernel(n, tiles, plane, place_ref, dif_ref, vl_ref, al_ref, jac_ref, coup_ref, stencil_ref, *refs):
    every = tiles + 1
    near_refs, (v_ref, w_ref, sum_ref), refs = refs[:plane], refs[plane : plane + 3], refs[plane + 3 :]
    send_refs, (gather_ref, vs_ref, xs_ref, mx_ref, bs_ref) = refs[: n // GROUP], refs[n // GROUP :]
    early = every - vl_ref.shape[0]
    gather_kernel(place_ref, *near_refs, gather_ref)
    flat = gather_ref.reshape(n * early * S, LANES)
    for ct in range(early):
        for s in range(S):
            v_ref[ct, s] = flat[pl.ds(ct * S + s, n, stride=early * S), :]
    for ct in range(early, every):
        v_ref[ct] = vl_ref[ct - early]
    sums = Sums()

    def get(ct, t):
        return v_ref[ct, t]

    def finisher(ct, slot):
        def finish(s, k, acc):
            w = dif_ref[s] * bs_ref[slot, s * n + k : s * n + k + 8] - acc
            w_ref[ct, s, k : k + 8] = w
            v = v_ref[ct, s, k : k + 8]
            sums.add("rr", k // 8, v * v)
            sums.add("rw", k // 8, v * w)

        return finish

    def prepare(ct):
        return mix(get, ct, ct % 2, coup_ref, vs_ref, mx_ref) + sides(ct, ct % 2)

    def sides(ct, slot):
        return spread(get, ct, slot, every, stencil_ref, xs_ref, bs_ref)

    def close(ct, slot):
        for s in range(S):
            for k in range(0, n, 8):
                finisher(ct, slot)(s, k, al_ref[ct - early, s, k : k + 8])

    def pack(ct):
        for q in range(n // GROUP):
            at = pl.multiple_of(jnp.bitwise_xor(place_ref[0], q) * GROUP, GROUP)
            flat = send_refs[q].reshape(GROUP * tiles * S, LANES)
            for s in range(S):
                flat[pl.ds(ct * S + s, GROUP, stride=tiles * S), :] = w_ref[ct, s, pl.ds(at, GROUP)]

    spare = early % 2
    rest = []
    for ct in range(early, tiles):
        rest += sides(ct, spare) + [functools.partial(close, ct, spare), functools.partial(pack, ct)]
    run(prepare(0))
    for ct in range(early):
        steps = prepare(ct + 1) if ct + 1 < early else rest
        react(n, tile_of(jac_ref, ct), ct % 2, mx_ref, finisher(ct, ct % 2), steps)
        pack(ct)
    sum_ref[0:8] = sums.partial("rr")
    sum_ref[8:16] = sums.partial("rw")


def second_kernel(
    n,
    tiles,
    dif_ref,
    v_ref,
    w_ref,
    sum_ref,
    jac_ref,
    edge_ref,
    coup_ref,
    stencil_ref,
    out_ref,
    z_ref,
    wh_ref,
    vs_ref,
    xs_ref,
    mx_ref,
    bs_ref,
):
    every = tiles + 1
    per = tiles * S + 1
    rr, rw = spread_sum(sum_ref[0:8]), spread_sum(sum_ref[8:16])
    c1 = ratio(rw, rr)
    sums = Sums()

    def get_v(ct, t):
        return v_ref[ct, t]

    def get_w(ct, t):
        return w_ref[ct, t] if ct < tiles else wh_ref[t]

    def finish_edge(s, k, acc):
        wh_ref[s, k : k + 8] = dif_ref[s] * bs_ref[0, s * n + k : s * n + k + 8] - acc

    def finisher(ct, slot):
        def finish(s, k, acc):
            z = dif_ref[s] * bs_ref[slot, s * n + k : s * n + k + 8] - acc
            v, w = v_ref[ct, s, k : k + 8], w_ref[ct, s, k : k + 8]
            z_ref[ct, s, k : k + 8] = z
            out_ref[pl.ds(k * per + ct * S + s, 8, stride=per), :] = z
            u = w - c1 * v
            sums.add("uu", k // 8, u * u)
            sums.add("ur", k // 8, u * v)
            sums.add("uz", k // 8, u * z)
            sums.add("rz", k // 8, v * z)

        return finish

    order = list(range(1, tiles)) + [0]

    def mixed(get, ct, slot):
        return mix(get, ct, slot, coup_ref, vs_ref, mx_ref)

    def sides(get, ct, slot):
        return spread(get, ct, slot, every, stencil_ref, xs_ref, bs_ref)

    run(mixed(get_v, tiles, 0) + sides(get_v, tiles, 0))
    inside = tiles > 2
    steps = mixed(get_w, order[0], 1) + (sides(get_w, order[0], 1) if inside else [])
    react(n, tile_of(edge_ref, 0), 0, mx_ref, finish_edge, steps)
    if not inside:
        run(sides(get_w, order[0], 1))
    for at, ct in enumerate(order):
        slot = (at + 1) % 2
        steps = []
        if at + 1 < tiles:
            steps = mixed(get_w, order[at + 1], 1 - slot) + sides(get_w, order[at + 1], 1 - slot)
        react(n, tile_of(jac_ref, ct), slot, mx_ref, finisher(ct, slot), steps)
    uu, ur, uz, rz = (sums.total(name) for name in ("uu", "ur", "uz", "rz"))
    c2 = ratio(rz, rr)
    c3 = ratio(uz - c2 * ur, uu)
    for ct in range(tiles):
        for s in range(S):
            for k in range(0, n, 8):
                v, w, z = (ref[ct, s, k : k + 8] for ref in (v_ref, w_ref, z_ref))
                x = (z - c2 * v) - c3 * (w - c1 * v)
                sums.add("xx", k // 8, x * x)
    xx = sums.total("xx")
    lane = lane_iota()
    tile = jnp.zeros((8, LANES), F32)
    for q, value in enumerate((rr, c1, uu, c2, c3, xx)):
        tile = jnp.where(lane == q, value, tile)
    for k in range(0, n, 8):
        out_ref[pl.ds(k * per + tiles * S, 8, stride=per), :] = tile


def flip(arrays):
    return list(arrays[:1]) + list(arrays[1:])[::-1]


def relay_kernel(own, place_ref, *refs):
    parts = GROUP // own
    count = len(refs) - parts
    refs = flip(refs[:count]) + list(refs[count:])
    for k in range(parts):
        at = jnp.bitwise_xor(place_ref[1], k)
        for q in range(count):
            refs[count + k][q] = refs[q][at]


def gather_kernel(place_ref, *refs):
    near_refs, out_ref = flip(refs[:-1]), refs[-1]
    plane = len(near_refs)
    for k in range(plane):
        for q in range(near_refs[k].shape[0]):
            d = jnp.bitwise_xor(place_ref[0], q) * plane + jnp.bitwise_xor(place_ref[1], k)
            out_ref[d] = near_refs[k][q]


def combine_kernel(parts, tiles, rhs_ref, got_ref, w_ref, update_ref, basis_ref):
    own = rhs_ref.shape[0]
    per = tiles * S + 1
    stats = got_ref[pl.ds(tiles * S, parts, stride=own * per), :]

    def stat(q):
        return jnp.broadcast_to(stats[:, q : q + 1], (parts, LANES))

    def add(x):
        return jnp.sum(x, axis=0, keepdims=True)

    rr, c1, uu, c2, c3, xx = (stat(q) for q in range(6))
    all_rr = add(rr)
    g1 = add(rr * c1) / all_rr
    g2 = add(rr * c2) / all_rr
    e1, e2 = c1 - g1, c2 - g2
    all_uu = add(uu + e1 * e1 * rr)
    g3 = add(c3 * uu + e1 * e2 * rr) / all_uu
    e3 = c3 - g3
    f = e2 - g3 * e1
    all_xx = add(xx + e3 * e3 * uu + f * f * rr)
    beta, nu, nx = jnp.sqrt(all_rr), jnp.sqrt(all_uu), jnp.sqrt(all_xx)
    h11 = 1.0 + g1
    h21 = nu / beta
    h12 = (g2 - g1 * g1) * beta / nu
    h22 = 1.0 + (g3 - g1)
    h32 = nx / nu
    m11 = h11 * h11 + h21 * h21
    m12 = h11 * h12 + h21 * h22
    m22 = h12 * h12 + h22 * h22 + h32 * h32
    b1, b2 = beta * h11, beta * h12
    determ = m11 * m22 - m12 * m12
    y1 = (m22 * b1 - m12 * b2) / determ
    y2 = (m11 * b2 - m12 * b1) / determ
    uw = y2 / nu
    ur = y1 / beta - uw * g1
    bz = 1.0 / nx
    bw = -g3 * bz
    br = (g3 * g1 - g2) * bz
    ur, uw, br, bw, bz = (jnp.broadcast_to(x, (S, LANES)) for x in (ur, uw, br, bw, bz))
    for d in range(parts):
        for m in range(own):
            for ct in range(tiles):
                at = slice((d * tiles + ct) * LANES, (d * tiles + ct + 1) * LANES)
                base = (d * own + m) * per + ct * S
                r = rhs_ref[m, :, at]
                w = w_ref[d, m, ct * S : (ct + 1) * S, :]
                update_ref[m, :, at] = ur * r + uw * w
                basis_ref[m, :, at] = br * r + bw * w + bz * got_ref[base : base + S, :]


def local(rhs, diffusivity, jac_coef, coef_index, row_mode, col_mode, multiplicity):
    parts = lax.axis_size("modes")
    own, _, total = rhs.shape
    n = own * parts
    cells = total // parts
    tiles = cells // LANES
    plane = GROUP // own
    sds = jax.ShapeDtypeStruct
    smem = pl.BlockSpec(memory_space=pltpu.SMEM)
    index = lax.axis_index("modes")
    place = jnp.stack([index // plane, index % plane]).astype(jnp.int32)

    early = (3 * tiles + 3) // 4
    block = (plane, own, early * S, LANES)

    def across(arrays):
        lead, rows = len(arrays), arrays[0].shape[2]
        come = [arrays[0]] * lead
        for q in reversed(range(1, lead)):
            come[q] = lax.ppermute(arrays[q], "modes", [(i, i ^ (q * plane)) for i in range(parts)])
        relayed = pl.pallas_call(
            functools.partial(relay_kernel, own),
            out_shape=[sds((lead, own, rows, LANES), F32)] * plane,
            in_specs=[smem] + [VMEM] * lead,
            out_specs=[VMEM] * plane,
            compiler_params=PARAMS,
            cost_estimate=pl.CostEstimate(flops=10**11, bytes_accessed=1 << 20, transcendentals=0),
            name="relay",
        )(place, *flip(come))
        out = [relayed[0]] * plane
        for k in reversed(range(1, plane)):
            out[k] = lax.ppermute(relayed[k], "modes", [(i, i ^ k) for i in range(parts)])
        return out, relayed[0]

    late_send, *early_send = pl.pallas_call(
        functools.partial(arrange_kernel, parts, early),
        out_shape=[sds((n, tiles + 1 - early, S, LANES), F32)] + [sds(block, F32)] * (parts // plane),
        in_specs=[smem, VMEM],
        out_specs=[VMEM] * (1 + parts // plane),
        compiler_params=PARAMS,
        name="arrange",
    )(place, rhs)
    near, relayed = across(early_send)
    vector = lax.all_to_all(late_send, "modes", split_axis=0, concat_axis=0, tiled=True)

    edge = (NCOEF, S, S, LANES)
    head, tail = pl.pallas_call(
        pack_kernel,
        grid=(1,),
        out_shape=[sds((NCOEF, S // 4, S, LANES), F32)] * 2,
        in_specs=[
            pl.BlockSpec(edge, lambda g: (0, 0, 0, 0)),
            pl.BlockSpec(edge, lambda g: (0, 0, 0, tiles - 1)),
            pl.BlockSpec(memory_space=pl.ANY),
        ],
        compiler_params=PARAMS,
        name="pack",
    )(jac_coef, jac_coef, relayed)
    up = [(i, (i + 1) % parts) for i in range(parts)]
    down = [(j, i) for i, j in up]
    after = lax.ppermute(head, "modes", down)
    before = lax.ppermute(tail, "modes", up)
    coupling, stencil = pl.pallas_call(
        functools.partial(coupling_kernel, n),
        out_shape=[sds((NCOEF * n, 3 * n), BF16), sds((4 * LANES, LANES), BF16)],
        in_specs=[VMEM] * 4 + [pl.BlockSpec(memory_space=pl.ANY)],
        out_specs=[VMEM] * 2,
        compiler_params=PARAMS,
        name="coupling",
    )(*(x.reshape(1, -1) for x in (coef_index, row_mode, col_mode, multiplicity)), relayed)

    jac = jac_coef.reshape(NCOEF * S, S, cells)
    field = (tiles + 1, S, n, LANES)
    work = [
        pltpu.VMEM((2, 3 * n, S * LANES), BF16),
        pltpu.VMEM((2, S * n, 4 * LANES), BF16),
        pltpu.VMEM((2, NCOEF * n, S * LANES), F32),
        pltpu.VMEM((2, S * n, LANES), F32),
    ]
    late = tiles + 1 - early
    v_late, a_late = pl.pallas_call(
        functools.partial(late_kernel, n, early),
        out_shape=[sds((late, S, n, LANES), F32), sds((max(late - 1, 1), S, n, LANES), F32)],
        in_specs=[VMEM] * 3,
        out_specs=[VMEM] * 2,
        scratch_shapes=[work[0], work[2]],
        compiler_params=PARAMS,
        cost_estimate=pl.CostEstimate(flops=2 * 10**9, bytes_accessed=1 << 20, transcendentals=0),
        name="late",
    )(jac, coupling, vector.reshape(n * late * S, LANES))
    v, w, sums, *w_send = pl.pallas_call(
        functools.partial(first_kernel, n, tiles, plane),
        out_shape=[sds(field, F32), sds((tiles, S, n, LANES), F32), sds((16, LANES), F32)]
        + [sds((plane, own, tiles * S, LANES), F32)] * (n // GROUP),
        in_specs=[smem] * 2 + [VMEM] * (5 + plane),
        out_specs=[VMEM] * (3 + n // GROUP),
        scratch_shapes=[pltpu.VMEM((parts, own, early * S, LANES), F32)] + work,
        compiler_params=PARAMS,
        name="first",
    )(place, diffusivity, v_late, a_late, jac, coupling, stencil, *flip(near))
    edges = pl.pallas_call(
        unpack_kernel,
        out_shape=sds((NCOEF * S, S, LANES), F32),
        in_specs=[VMEM] * 2 + [pl.BlockSpec(memory_space=pl.ANY)],
        out_specs=VMEM,
        compiler_params=PARAMS,
        name="unpack",
    )(after, before, sums)
    w_own, _ = across(w_send)

    z_send = pl.pallas_call(
        functools.partial(second_kernel, n, tiles),
        out_shape=sds((n * (tiles * S + 1), LANES), F32),
        in_specs=[smem] + [VMEM] * 7,
        out_specs=VMEM,
        scratch_shapes=[pltpu.VMEM((tiles, S, n, LANES), F32), pltpu.VMEM((S, n, LANES), F32)] + work,
        compiler_params=PARAMS,
        cost_estimate=pl.CostEstimate(flops=10**10, bytes_accessed=16 << 20, transcendentals=0),
        name="second",
    )(diffusivity, v, w, sums, jac, edges, coupling, stencil)
    line = (tiles * S + 1) * LANES
    got = lax.all_to_all(z_send.reshape(n, 1, line), "modes", split_axis=0, concat_axis=0, tiled=True)

    w_all = pl.pallas_call(
        gather_kernel,
        out_shape=sds((parts, own, tiles * S, LANES), F32),
        in_specs=[smem] + [VMEM] * plane,
        out_specs=VMEM,
        compiler_params=PARAMS,
        name="gather",
    )(place, *flip(w_own))
    update, basis_next = pl.pallas_call(
        functools.partial(combine_kernel, parts, tiles),
        out_shape=[sds(rhs.shape, F32)] * 2,
        in_specs=[VMEM] * 3,
        out_specs=[VMEM] * 2,
        compiler_params=PARAMS,
        name="combine",
    )(rhs, got.reshape(n * (tiles * S + 1), LANES), w_all)
    return (update, basis_next)


def solution(mesh):
    return jax.shard_map(
        local,
        mesh=mesh,
        in_specs=(
            P(("groups", "modes"), None, None),
            P(),
            P(None, None, None, "modes"),
            P(),
            P(),
            P(),
            P(),
        ),
        out_specs=(P(("groups", "modes"), None, None), P(("groups", "modes"), None, None)),
        check_vma=False,
    )
```

```python
import functools

import jax
import jax.numpy as jnp
from jax import lax
from jax.experimental import pallas as pl
from jax.experimental.pallas import tpu as pltpu
from jax.sharding import PartitionSpec as P

NCOEF = 9
GY = 32
S = 8
LANES = 128
GROUP = 8
F32 = jnp.float32
BF16 = jnp.bfloat16
VMEM = pl.BlockSpec(memory_space=pltpu.VMEM)
PARAMS = pltpu.CompilerParams(vmem_limit_bytes=40 * 1024 * 1024)


def lane_iota():
    return lax.broadcasted_iota(jnp.int32, (S, LANES), 1)


def arrange_kernel(parts, early, place_ref, rhs_ref, out_ref, *refs):
    own, _, total = rhs_ref.shape
    cells = total // parts
    tiles = cells // LANES
    plane = GROUP // own
    low = lane_iota() < LANES // 2
    for q in range(parts // plane):
        base = jnp.bitwise_xor(place_ref[0], q) * plane
        for k in range(plane):
            for m in range(own):
                for ct in range(early):
                    at = pl.multiple_of((base + k) * cells + ct * LANES, LANES)
                    refs[q][k, m, ct * S : (ct + 1) * S, :] = rhs_ref[m, :, pl.ds(at, LANES)]
    for d in range(parts):
        after = ((d + 1) * cells) % total
        before = (d * cells - LANES) % total
        for m in range(own):
            for ct in range(early, tiles):
                at = d * cells + ct * LANES
                out_ref[d * own + m, ct - early] = rhs_ref[m, :, at : at + LANES]
            out_ref[d * own + m, tiles - early] = jnp.where(
                low, rhs_ref[m, :, after : after + LANES], rhs_ref[m, :, before : before + LANES]
            )


def pack_kernel(first_ref, last_ref, _, head_ref, tail_ref):
    piece = lane_iota() // GY
    for i in range(NCOEF):
        for q in range(S // 4):
            head = first_ref[i, q * 4]
            tail = pltpu.roll(last_ref[i, q * 4], GY, 1)
            for p in range(1, 4):
                head = jnp.where(piece == p, pltpu.roll(first_ref[i, q * 4 + p], GY * p, 1), head)
                moved = last_ref[i, q * 4 + p]
                if p < 3:
                    moved = pltpu.roll(moved, GY * (p + 1), 1)
                tail = jnp.where(piece == p, moved, tail)
            head_ref[i, q] = head
            tail_ref[i, q] = tail


def coupling_kernel(modes, coef_ref, row_ref, col_ref, mult_ref, _, out_ref, stencil_ref):
    rows, cols = out_ref.shape
    triples = coef_ref.shape[1]
    key = coef_ref[...] * modes + row_ref[...]
    weight = 0.25 * mult_ref[...].astype(F32)
    row = lax.broadcasted_iota(jnp.int32, (rows, triples), 0)
    left = jnp.where(row == key, weight, 0.0).astype(BF16)
    col = lax.rem(lax.broadcasted_iota(jnp.int32, (cols, triples), 0), modes)
    right = jnp.where(col == col_ref[...], 1.0, 0.0).astype(BF16)
    dense = lax.dot_general(left, right, (((1,), (1,)), ((), ())), preferred_element_type=F32)
    r = lax.broadcasted_iota(jnp.int32, (rows, cols), 0)
    c = lax.broadcasted_iota(jnp.int32, (rows, cols), 1)
    dense = dense + jnp.where(r == lax.rem(c, modes), 1.0, 0.0)
    high = dense.astype(BF16)
    low = (dense - high.astype(F32)).astype(BF16)
    out_ref[...] = jnp.where(c < 2 * modes, high.astype(F32), low.astype(F32)).astype(BF16)

    a = lax.broadcasted_iota(jnp.int32, (LANES, LANES), 0)
    b = lax.broadcasted_iota(jnp.int32, (LANES, LANES), 1)
    step = jnp.bitwise_and(a - b, GY - 1)
    same = (a // GY == b // GY) & ((step == 1) | (step == GY - 1))
    apart = jnp.abs(a - b)
    inner = jnp.where(apart == 0, 4.0, jnp.where(same | (apart == GY), -1.0, 0.0)).astype(BF16)
    outer = jnp.where(apart == LANES - GY, -1.0, 0.0).astype(BF16)
    stencil_ref[0:LANES] = inner
    stencil_ref[LANES : 2 * LANES] = inner
    stencil_ref[2 * LANES : 3 * LANES] = outer
    stencil_ref[3 * LANES :] = outer


def split(x):
    high = x.astype(BF16)
    return high, (x - high.astype(F32)).astype(BF16)


def ratio(a, b):
    return jnp.where(b > 0.0, a / jnp.where(b > 0.0, b, 1.0), 0.0)


def unpack_kernel(next_ref, prev_ref, _, out_ref):
    lane = lane_iota()
    for i in range(NCOEF):
        for q in range(S // 4):
            after, before = next_ref[i, q], prev_ref[i, q]
            for p in range(4):
                a = after if p == 0 else pltpu.roll(after, LANES - GY * p, 1)
                b = before if p == 3 else pltpu.roll(before, LANES - GY - GY * p, 1)
                out_ref[i * S + q * 4 + p] = jnp.where(lane < LANES // 2, a, b)


def mix(get, ct, slot, coup_ref, vs_ref, mx_ref):
    n = vs_ref.shape[1] // 3

    def step(first):
        for t in (first, first + 1):
            at = slice(t * LANES, (t + 1) * LANES)
            high, low = split(get(ct, t))
            vs_ref[slot, 0:n, at] = high
            vs_ref[slot, n : 2 * n, at] = low
            vs_ref[slot, 2 * n : 3 * n, at] = high
        at = slice(first * LANES, (first + 2) * LANES)
        mx_ref[slot, :, at] = jnp.dot(coup_ref[...], vs_ref[slot, :, at], preferred_element_type=F32)

    return [functools.partial(step, first) for first in range(0, S, 2)]


def spread(get, ct, slot, every, stencil_ref, xs_ref, bs_ref):
    n = bs_ref.shape[1] // S
    before, after = (ct - 1) % every, (ct + 1) % every

    def fill(first):
        wide = lax.broadcasted_iota(jnp.int32, (n, LANES), 1) < LANES // 2
        for t in (first, first + 1):
            to = slice(t * n, (t + 1) * n)
            high, low = split(get(ct, t))
            xs_ref[slot, to, 0:LANES] = high
            xs_ref[slot, to, LANES : 2 * LANES] = low
            high, low = split(jnp.where(wide, get(after, t), get(before, t)))
            xs_ref[slot, to, 2 * LANES : 3 * LANES] = high
            xs_ref[slot, to, 3 * LANES :] = low
        if first + 2 == S:
            bs_ref[slot] = jnp.dot(xs_ref[slot], stencil_ref[...], preferred_element_type=F32)

    return [functools.partial(fill, first) for first in range(0, S, 2)]


def prepare(get, ct, slot, every, coup_ref, stencil_ref, vs_ref, xs_ref, mx_ref, bs_ref):
    n = bs_ref.shape[1] // S
    before, after = (ct - 1) % every, (ct + 1) % every

    def step(first):
        wide = lax.broadcasted_iota(jnp.int32, (n, LANES), 1) < LANES // 2
        for t in (first, first + 1):
            at = slice(t * LANES, (t + 1) * LANES)
            to = slice(t * n, (t + 1) * n)
            high, low = split(get(ct, t))
            vs_ref[slot, 0:n, at] = high
            vs_ref[slot, n : 2 * n, at] = low
            vs_ref[slot, 2 * n : 3 * n, at] = high
            xs_ref[slot, to, 0:LANES] = high
            xs_ref[slot, to, LANES : 2 * LANES] = low
            high, low = split(jnp.where(wide, get(after, t), get(before, t)))
            xs_ref[slot, to, 2 * LANES : 3 * LANES] = high
            xs_ref[slot, to, 3 * LANES :] = low
        at = slice(first * LANES, (first + 2) * LANES)
        mx_ref[slot, :, at] = jnp.dot(coup_ref[...], vs_ref[slot, :, at], preferred_element_type=F32)
        if first + 2 == S:
            bs_ref[slot] = jnp.dot(xs_ref[slot], stencil_ref[...], preferred_element_type=F32)

    return [functools.partial(step, first) for first in range(0, S, 2)]


def run(steps):
    for step in steps:
        step()


def react(n, jac, slot, mx_ref, finish, steps=()):
    steps = list(steps)
    for kb in range(0, n, 32):
        acc = [None] * 32
        for i in range(NCOEF):
            if steps:
                steps.pop(0)()
            for t in range(S):
                m = [
                    mx_ref[slot, i * n + kb + kt * 8 : i * n + kb + kt * 8 + 8, t * LANES : (t + 1) * LANES]
                    for kt in range(4)
                ]
                for s in range(S):
                    j = jnp.broadcast_to(jac(i * S + s, t), (8, LANES))
                    for kt in range(4):
                        term = j * m[kt]
                        at = s * 4 + kt
                        acc[at] = term if acc[at] is None else acc[at] + term
        for s in range(S):
            for kt in range(4):
                finish(s, kb + kt * 8, acc[s * 4 + kt])
    run(steps)


def tile_of(jac_ref, ct):
    return lambda row, t: jac_ref[row, t : t + 1, ct * LANES : (ct + 1) * LANES]


def spread_sum(x):
    return jnp.broadcast_to(jnp.sum(x, axis=(0, 1), keepdims=True), (8, LANES))


class Sums:
    def __init__(self):
        self.parts = {}

    def add(self, name, at, term):
        mine = self.parts.setdefault(name, {})
        mine[at % 4] = mine[at % 4] + term if at % 4 in mine else term

    def partial(self, name):
        return functools.reduce(lambda a, b: a + b, self.parts[name].values())

    def total(self, name):
        return spread_sum(self.partial(name))


def late_kernel(n, early, jac_ref, coup_ref, r_ref, v_ref, a_ref, vs_ref, mx_ref):
    late = v_ref.shape[0]
    for ct in range(late):
        for s in range(S):
            v_ref[ct, s] = r_ref[pl.ds(ct * S + s, n, stride=late * S), :]

    def get(ct, t):
        return v_ref[ct, t]

    def finisher(ct):
        def finish(s, k, acc):
            a_ref[ct, s, k : k + 8] = acc

        return finish

    if late > 1:
        run(mix(get, 0, 0, coup_ref, vs_ref, mx_ref))
    for ct in range(late - 1):
        steps = mix(get, ct + 1, (ct + 1) % 2, coup_ref, vs_ref, mx_ref) if ct + 2 < late else []
        react(n, tile_of(jac_ref, early + ct), ct % 2, mx_ref, finisher(ct), steps)


def first_kernel(n, tiles, plane, place_ref, dif_ref, vl_ref, al_ref, jac_ref, coup_ref, stencil_ref, *refs):
    every = tiles + 1
    near_refs, (v_ref, w_ref, sum_ref), refs = refs[:plane], refs[plane : plane + 3], refs[plane + 3 :]
    send_refs, (gather_ref, vs_ref, xs_ref, mx_ref, bs_ref) = refs[: n // GROUP], refs[n // GROUP :]
    early = every - vl_ref.shape[0]
    gather_kernel(place_ref, *near_refs, gather_ref)
    flat = gather_ref.reshape(n * early * S, LANES)
    for ct in range(early):
        for s in range(S):
            v_ref[ct, s] = flat[pl.ds(ct * S + s, n, stride=early * S), :]
    for ct in range(early, every):
        v_ref[ct] = vl_ref[ct - early]
    sums = Sums()

    def get(ct, t):
        return v_ref[ct, t]

    def finisher(ct, slot):
        def finish(s, k, acc):
            w = dif_ref[s] * bs_ref[slot, s * n + k : s * n + k + 8] - acc
            w_ref[ct, s, k : k + 8] = w
            v = v_ref[ct, s, k : k + 8]
            sums.add("rr", k // 8, v * v)
            sums.add("rw", k // 8, v * w)

        return finish

    def ready(ct):
        return prepare(get, ct, ct % 2, every, coup_ref, stencil_ref, vs_ref, xs_ref, mx_ref, bs_ref)

    def sides(ct, slot):
        return spread(get, ct, slot, every, stencil_ref, xs_ref, bs_ref)

    def close(ct, slot):
        for s in range(S):
            for k in range(0, n, 8):
                finisher(ct, slot)(s, k, al_ref[ct - early, s, k : k + 8])

    def pack(ct):
        for q in range(n // GROUP):
            at = pl.multiple_of(jnp.bitwise_xor(place_ref[0], q) * GROUP, GROUP)
            flat = send_refs[q].reshape(GROUP * tiles * S, LANES)
            for s in range(S):
                flat[pl.ds(ct * S + s, GROUP, stride=tiles * S), :] = w_ref[ct, s, pl.ds(at, GROUP)]

    spare = early % 2
    rest = []
    for ct in range(early, tiles):
        rest += sides(ct, spare) + [functools.partial(close, ct, spare), functools.partial(pack, ct)]
    run(ready(0))
    for ct in range(early):
        steps = ready(ct + 1) if ct + 1 < early else rest
        react(n, tile_of(jac_ref, ct), ct % 2, mx_ref, finisher(ct, ct % 2), steps)
        pack(ct)
    sum_ref[0:8] = sums.partial("rr")
    sum_ref[8:16] = sums.partial("rw")


def second_kernel(
    n,
    tiles,
    dif_ref,
    v_ref,
    w_ref,
    sum_ref,
    jac_ref,
    edge_ref,
    coup_ref,
    stencil_ref,
    out_ref,
    z_ref,
    wh_ref,
    vs_ref,
    xs_ref,
    mx_ref,
    bs_ref,
):
    every = tiles + 1
    per = tiles * S + 1
    rr, rw = spread_sum(sum_ref[0:8]), spread_sum(sum_ref[8:16])
    c1 = ratio(rw, rr)
    sums = Sums()

    def get_v(ct, t):
        return v_ref[ct, t]

    def get_w(ct, t):
        return w_ref[ct, t] if ct < tiles else wh_ref[t]

    def finish_edge(s, k, acc):
        wh_ref[s, k : k + 8] = dif_ref[s] * bs_ref[0, s * n + k : s * n + k + 8] - acc

    def finisher(ct, slot):
        def finish(s, k, acc):
            z = dif_ref[s] * bs_ref[slot, s * n + k : s * n + k + 8] - acc
            v, w = v_ref[ct, s, k : k + 8], w_ref[ct, s, k : k + 8]
            z_ref[ct, s, k : k + 8] = z
            out_ref[pl.ds(k * per + ct * S + s, 8, stride=per), :] = z
            u = w - c1 * v
            sums.add("uu", k // 8, u * u)
            sums.add("ur", k // 8, u * v)
            sums.add("uz", k // 8, u * z)
            sums.add("rz", k // 8, v * z)

        return finish

    order = list(range(1, tiles)) + [0]

    def ready(get, ct, slot):
        return prepare(get, ct, slot, every, coup_ref, stencil_ref, vs_ref, xs_ref, mx_ref, bs_ref)

    run(ready(get_v, tiles, 0))
    inside = tiles > 2
    steps = ready(get_w, order[0], 1) if inside else []
    react(n, tile_of(edge_ref, 0), 0, mx_ref, finish_edge, steps)
    if not inside:
        run(ready(get_w, order[0], 1))
    for at, ct in enumerate(order):
        slot = (at + 1) % 2
        steps = ready(get_w, order[at + 1], 1 - slot) if at + 1 < tiles else []
        react(n, tile_of(jac_ref, ct), slot, mx_ref, finisher(ct, slot), steps)
    uu, ur, uz, rz = (sums.total(name) for name in ("uu", "ur", "uz", "rz"))
    c2 = ratio(rz, rr)
    c3 = ratio(uz - c2 * ur, uu)
    for ct in range(tiles):
        for s in range(S):
            for k in range(0, n, 8):
                v, w, z = (ref[ct, s, k : k + 8] for ref in (v_ref, w_ref, z_ref))
                x = (z - c2 * v) - c3 * (w - c1 * v)
                sums.add("xx", k // 8, x * x)
    xx = sums.total("xx")
    lane = lane_iota()
    tile = jnp.zeros((8, LANES), F32)
    for q, value in enumerate((rr, c1, uu, c2, c3, xx)):
        tile = jnp.where(lane == q, value, tile)
    for k in range(0, n, 8):
        out_ref[pl.ds(k * per + tiles * S, 8, stride=per), :] = tile


def flip(arrays):
    return list(arrays[:1]) + list(arrays[1:])[::-1]


def relay_kernel(own, place_ref, *refs):
    parts = GROUP // own
    count = len(refs) - parts
    refs = flip(refs[:count]) + list(refs[count:])
    for k in range(parts):
        at = jnp.bitwise_xor(place_ref[1], k)
        for q in range(count):
            refs[count + k][q] = refs[q][at]


def gather_kernel(place_ref, *refs):
    near_refs, out_ref = flip(refs[:-1]), refs[-1]
    plane = len(near_refs)
    for k in range(plane):
        for q in range(near_refs[k].shape[0]):
            d = jnp.bitwise_xor(place_ref[0], q) * plane + jnp.bitwise_xor(place_ref[1], k)
            out_ref[d] = near_refs[k][q]


def combine_kernel(parts, tiles, rhs_ref, got_ref, w_ref, update_ref, basis_ref):
    own = rhs_ref.shape[0]
    per = tiles * S + 1
    stats = got_ref[pl.ds(tiles * S, parts, stride=own * per), :]

    def stat(q):
        return jnp.broadcast_to(stats[:, q : q + 1], (parts, LANES))

    def add(x):
        return jnp.sum(x, axis=0, keepdims=True)

    rr, c1, uu, c2, c3, xx = (stat(q) for q in range(6))
    all_rr = add(rr)
    g1 = add(rr * c1) / all_rr
    g2 = add(rr * c2) / all_rr
    e1, e2 = c1 - g1, c2 - g2
    all_uu = add(uu + e1 * e1 * rr)
    g3 = add(c3 * uu + e1 * e2 * rr) / all_uu
    e3 = c3 - g3
    f = e2 - g3 * e1
    all_xx = add(xx + e3 * e3 * uu + f * f * rr)
    beta, nu, nx = jnp.sqrt(all_rr), jnp.sqrt(all_uu), jnp.sqrt(all_xx)
    h11 = 1.0 + g1
    h21 = nu / beta
    h12 = (g2 - g1 * g1) * beta / nu
    h22 = 1.0 + (g3 - g1)
    h32 = nx / nu
    m11 = h11 * h11 + h21 * h21
    m12 = h11 * h12 + h21 * h22
    m22 = h12 * h12 + h22 * h22 + h32 * h32
    b1, b2 = beta * h11, beta * h12
    determ = m11 * m22 - m12 * m12
    y1 = (m22 * b1 - m12 * b2) / determ
    y2 = (m11 * b2 - m12 * b1) / determ
    uw = y2 / nu
    ur = y1 / beta - uw * g1
    bz = 1.0 / nx
    bw = -g3 * bz
    br = (g3 * g1 - g2) * bz
    ur, uw, br, bw, bz = (jnp.broadcast_to(x, (S, LANES)) for x in (ur, uw, br, bw, bz))
    for d in range(parts):
        for m in range(own):
            for ct in range(tiles):
                at = slice((d * tiles + ct) * LANES, (d * tiles + ct + 1) * LANES)
                base = (d * own + m) * per + ct * S
                r = rhs_ref[m, :, at]
                w = w_ref[d, m, ct * S : (ct + 1) * S, :]
                update_ref[m, :, at] = ur * r + uw * w
                basis_ref[m, :, at] = br * r + bw * w + bz * got_ref[base : base + S, :]


def local(rhs, diffusivity, jac_coef, coef_index, row_mode, col_mode, multiplicity):
    parts = lax.axis_size("modes")
    own, _, total = rhs.shape
    n = own * parts
    cells = total // parts
    tiles = cells // LANES
    plane = GROUP // own
    sds = jax.ShapeDtypeStruct
    smem = pl.BlockSpec(memory_space=pltpu.SMEM)
    index = lax.axis_index("modes")
    place = jnp.stack([index // plane, index % plane]).astype(jnp.int32)

    early = (3 * tiles + 3) // 4
    block = (plane, own, early * S, LANES)

    def across(arrays):
        lead, rows = len(arrays), arrays[0].shape[2]
        come = [arrays[0]] * lead
        for q in reversed(range(1, lead)):
            come[q] = lax.ppermute(arrays[q], "modes", [(i, i ^ (q * plane)) for i in range(parts)])
        relayed = pl.pallas_call(
            functools.partial(relay_kernel, own),
            out_shape=[sds((lead, own, rows, LANES), F32)] * plane,
            in_specs=[smem] + [VMEM] * lead,
            out_specs=[VMEM] * plane,
            compiler_params=PARAMS,
            cost_estimate=pl.CostEstimate(flops=10**11, bytes_accessed=1 << 20, transcendentals=0),
            name="relay",
        )(place, *flip(come))
        out = [relayed[0]] * plane
        for k in reversed(range(1, plane)):
            out[k] = lax.ppermute(relayed[k], "modes", [(i, i ^ k) for i in range(parts)])
        return out, relayed[0]

    late_send, *early_send = pl.pallas_call(
        functools.partial(arrange_kernel, parts, early),
        out_shape=[sds((n, tiles + 1 - early, S, LANES), F32)] + [sds(block, F32)] * (parts // plane),
        in_specs=[smem, VMEM],
        out_specs=[VMEM] * (1 + parts // plane),
        compiler_params=PARAMS,
        name="arrange",
    )(place, rhs)
    near, relayed = across(early_send)
    vector = lax.all_to_all(late_send, "modes", split_axis=0, concat_axis=0, tiled=True)

    edge = (NCOEF, S, S, LANES)
    head, tail = pl.pallas_call(
        pack_kernel,
        grid=(1,),
        out_shape=[sds((NCOEF, S // 4, S, LANES), F32)] * 2,
        in_specs=[
            pl.BlockSpec(edge, lambda g: (0, 0, 0, 0)),
            pl.BlockSpec(edge, lambda g: (0, 0, 0, tiles - 1)),
            pl.BlockSpec(memory_space=pl.ANY),
        ],
        compiler_params=PARAMS,
        name="pack",
    )(jac_coef, jac_coef, relayed)
    up = [(i, (i + 1) % parts) for i in range(parts)]
    down = [(j, i) for i, j in up]
    after = lax.ppermute(head, "modes", down)
    before = lax.ppermute(tail, "modes", up)
    coupling, stencil = pl.pallas_call(
        functools.partial(coupling_kernel, n),
        out_shape=[sds((NCOEF * n, 3 * n), BF16), sds((4 * LANES, LANES), BF16)],
        in_specs=[VMEM] * 4 + [pl.BlockSpec(memory_space=pl.ANY)],
        out_specs=[VMEM] * 2,
        compiler_params=PARAMS,
        name="coupling",
    )(*(x.reshape(1, -1) for x in (coef_index, row_mode, col_mode, multiplicity)), relayed)

    jac = jac_coef.reshape(NCOEF * S, S, cells)
    field = (tiles + 1, S, n, LANES)
    work = [
        pltpu.VMEM((2, 3 * n, S * LANES), BF16),
        pltpu.VMEM((2, S * n, 4 * LANES), BF16),
        pltpu.VMEM((2, NCOEF * n, S * LANES), F32),
        pltpu.VMEM((2, S * n, LANES), F32),
    ]
    late = tiles + 1 - early
    v_late, a_late = pl.pallas_call(
        functools.partial(late_kernel, n, early),
        out_shape=[sds((late, S, n, LANES), F32), sds((max(late - 1, 1), S, n, LANES), F32)],
        in_specs=[VMEM] * 3,
        out_specs=[VMEM] * 2,
        scratch_shapes=[work[0], work[2]],
        compiler_params=PARAMS,
        cost_estimate=pl.CostEstimate(flops=2 * 10**9, bytes_accessed=1 << 20, transcendentals=0),
        name="late",
    )(jac, coupling, vector.reshape(n * late * S, LANES))
    v, w, sums, *w_send = pl.pallas_call(
        functools.partial(first_kernel, n, tiles, plane),
        out_shape=[sds(field, F32), sds((tiles, S, n, LANES), F32), sds((16, LANES), F32)]
        + [sds((plane, own, tiles * S, LANES), F32)] * (n // GROUP),
        in_specs=[smem] * 2 + [VMEM] * (5 + plane),
        out_specs=[VMEM] * (3 + n // GROUP),
        scratch_shapes=[pltpu.VMEM((parts, own, early * S, LANES), F32)] + work,
        compiler_params=PARAMS,
        name="first",
    )(place, diffusivity, v_late, a_late, jac, coupling, stencil, *flip(near))
    edges = pl.pallas_call(
        unpack_kernel,
        out_shape=sds((NCOEF * S, S, LANES), F32),
        in_specs=[VMEM] * 2 + [pl.BlockSpec(memory_space=pl.ANY)],
        out_specs=VMEM,
        compiler_params=PARAMS,
        name="unpack",
    )(after, before, sums)
    w_own, _ = across(w_send)

    z_send = pl.pallas_call(
        functools.partial(second_kernel, n, tiles),
        out_shape=sds((n * (tiles * S + 1), LANES), F32),
        in_specs=[smem] + [VMEM] * 7,
        out_specs=VMEM,
        scratch_shapes=[pltpu.VMEM((tiles, S, n, LANES), F32), pltpu.VMEM((S, n, LANES), F32)] + work,
        compiler_params=PARAMS,
        cost_estimate=pl.CostEstimate(flops=10**10, bytes_accessed=16 << 20, transcendentals=0),
        name="second",
    )(diffusivity, v, w, sums, jac, edges, coupling, stencil)
    line = (tiles * S + 1) * LANES
    got = lax.all_to_all(z_send.reshape(n, 1, line), "modes", split_axis=0, concat_axis=0, tiled=True)

    w_all = pl.pallas_call(
        gather_kernel,
        out_shape=sds((parts, own, tiles * S, LANES), F32),
        in_specs=[smem] + [VMEM] * plane,
        out_specs=VMEM,
        compiler_params=PARAMS,
        name="gather",
    )(place, *flip(w_own))
    update, basis_next = pl.pallas_call(
        functools.partial(combine_kernel, parts, tiles),
        out_shape=[sds(rhs.shape, F32)] * 2,
        in_specs=[VMEM] * 3,
        out_specs=[VMEM] * 2,
        compiler_params=PARAMS,
        name="combine",
    )(rhs, got.reshape(n * (tiles * S + 1), LANES), w_all)
    return (update, basis_next)


def solution(mesh):
    return jax.shard_map(
        local,
        mesh=mesh,
        in_specs=(
            P(("groups", "modes"), None, None),
            P(),
            P(None, None, None, "modes"),
            P(),
            P(),
            P(),
            P(),
        ),
        out_specs=(P(("groups", "modes"), None, None), P(("groups", "modes"), None, None)),
        check_vma=False,
    )
```
